256 devices in a mesh: lat: 32 (over x, y, core), ch: 8 (over z).
Axes of the slice: x: 4, y: 4, z: 8, core: 2. Of those that a mesh axis runs over, the one named last changes fastest.
Arguments:
- field_in: bfloat16 [480, 256, 1024], P('lat', 'ch'), may hold values from -6 to 6
- mix_weight: bfloat16 [2, 256, 256, 480], P(None, None, 'ch', 'lat'), may hold values from -0.375 to 0.375
- order_slots: int32 [480], replicated, may hold values from 0 to 479, each once
Outputs:
- field_out: bfloat16 [480, 256, 1024], P('lat', 'ch')
- spectrum: bfloat16 [480, 2, 256, 480], P('lat', None, 'ch')
The draws below stay inside these ranges and needn't reach their ends.
Inputs may be any that keep to these rules, and one draw needn't show every extreme that they name: `order_slots`: every order of 0 to 479 stands in exactly one slot.
All inputs are finite; a program needn't handle non-finite values.
Results may differ from the reference program's by a relative error of at most 0.009.
Values may be sent and summed in bfloat16 or wider, within the bound.
No kernel may reach another device: no remote copies, remote signals or barrier semaphores. Data moves between devices by JAX's collectives and lax.ppermute only.
A program may use at most 128 MiB of HBM per device.

```python
import math
import jax
import jax.numpy as jnp
from jax import lax

NLAT = 480
NLON = 1024
MODES = 480
C = 256


def shard_levels(own_key, extent, cuts, low, top_value):
    level = 1.0
    for dim, shards_of in cuts:
        steps = jax.random.uniform(jax.random.fold_in(jax.random.fold_in(own_key, 6), dim), (shards_of,), jnp.float32, low / len(cuts), top_value / len(cuts))
        level = level * jnp.repeat(jnp.exp(steps), extent[dim] // shards_of).reshape((-1,) + (1,) * (len(extent) - 1 - dim))
    return level


def gaussian(key, shape, scale, bound, pieces=(), kind=jnp.bfloat16):
    result = jax.random.normal(key, shape, jnp.float32) * scale
    if len(pieces) > 0:
        result = shard_levels(key, shape, pieces, -0.22, 0.18) * result
    return jnp.clip(result, min=-bound, max=bound).astype(kind)


def setup_inputs(seed: int = 0) -> dict:
    seeds = jax.random.split(jax.random.key(seed), 4)
    field_in = gaussian(seeds[0], (NLAT, C, NLON), 1.0, 6.0, ((0, 32), (1, 8)))
    mix_weight = gaussian(seeds[1], (2, C, C, MODES), C ** -0.5, 0.375, ((2, 8), (3, 32)))
    order_slots = jax.random.permutation(seeds[2], MODES).astype(jnp.int32)
    return dict(field_in=field_in, mix_weight=mix_weight, order_slots=order_slots)


rescale_bits = 60
degree_block = 16

def fourier_tables(orders, lon_total):
    longitude = jnp.arange(lon_total, dtype=jnp.int32)
    phases = orders[None, :] * longitude[:, None] % lon_total
    angles = phases.astype(jnp.float32) * (2.0 * math.pi / lon_total)
    return (jnp.cos(angles), jnp.sin(angles))

def legendre_tables(orders, lat_total, mode_total):
    colatitude = (jnp.arange(lat_total, dtype=jnp.float32) + 0.5) * (math.pi / lat_total)
    cosine_lat = jnp.cos(colatitude)
    sine_lat = jnp.sin(colatitude)
    factor_idx = jnp.arange(1, mode_total, dtype=jnp.float32)
    log_prod = jnp.concatenate([jnp.zeros((1,), jnp.float32), jnp.cumsum(0.5 * jnp.log((2.0 * factor_idx - 1.0) / (2.0 * factor_idx)))])
    order_vals = orders.astype(jnp.float32)
    matches = orders[:, None] == jnp.arange(mode_total, dtype=jnp.int32)[None, :]
    picked = lax.optimization_barrier(jnp.sum(jnp.where(matches, log_prod[None, :], jnp.float32(0.0)), axis=1))
    log_start = 0.5 * jnp.log(order_vals + 0.5)[:, None] + picked[:, None] + order_vals[:, None] * jnp.log(sine_lat)[None, :]
    quadrature = math.pi / lat_total * sine_lat
    ord_sq = order_vals * order_vals
    shrink = jnp.float32(2.0 ** (-rescale_bits))
    limit = jnp.float32(2.0 ** rescale_bits)
    log_step = jnp.float32(rescale_bits * math.log(2.0))

    def advance(state_now, block_start):
        before, current, rescales = state_now
        forward_rows = []
        inverse_rows = []
        for offset in range(degree_block):
            degree = (block_start + offset).astype(jnp.float32)
            deg_sq = degree * degree
            deg_prev = degree - 1.0
            alpha_coef = jnp.sqrt(jnp.maximum(4.0 * deg_sq - 1.0, 1.0) / jnp.maximum(deg_sq - ord_sq, 1.0))
            beta_coef = jnp.sqrt(jnp.maximum(deg_prev * deg_prev - ord_sq, 0.0) / jnp.maximum(4.0 * deg_prev * deg_prev - 1.0, 1.0))
            next_value = alpha_coef[:, None] * (cosine_lat[None, :] * current - beta_coef[:, None] * before)
            is_start = (degree == order_vals)[:, None]
            is_below = (degree < order_vals)[:, None]
            next_value = jnp.where(is_start, jnp.float32(1.0), jnp.where(is_below, jnp.float32(0.0), next_value))
            before = jnp.where(is_start | is_below, jnp.float32(0.0), current)
            too_large = jnp.abs(next_value) > limit
            next_value = jnp.where(too_large, next_value * shrink, next_value)
            before = jnp.where(too_large, before * shrink, before)
            rescales = rescales + jnp.where(too_large, jnp.float32(1.0), jnp.float32(0.0))
            current = next_value
            p_value = current * jnp.exp(log_start + rescales * log_step)
            forward_rows.append((p_value * quadrature[None, :]).astype(jnp.bfloat16))
            inverse_rows.append(p_value.astype(jnp.bfloat16))
        return ((before, current, rescales), (jnp.stack(forward_rows), jnp.stack(inverse_rows)))
    zeros = jnp.zeros((orders.shape[0], lat_total), jnp.float32)
    starts = jnp.arange(0, mode_total, degree_block, dtype=jnp.int32)
    _, (forward_all, inverse_all) = lax.scan(advance, (zeros, zeros, zeros), starts)
    shape = (mode_total, orders.shape[0], lat_total)
    return (forward_all.reshape(shape), inverse_all.reshape(shape))

def mix_channels(coeffs, weight):
    products = jnp.einsum('wiol,mxil->mwxol', weight, coeffs, preferred_element_type=jnp.float32)
    real_part = products[:, 0, 0] - products[:, 1, 1]
    imag_part = products[:, 0, 1] + products[:, 1, 0]
    return jnp.stack([real_part, imag_part], axis=1)

def reference(field_in, mix_weight, order_slots):
    lat_total, channels, lon_total = field_in.shape
    mode_total = order_slots.shape[0]
    orders = jnp.arange(mode_total, dtype=jnp.int32)
    cosines, sines = fourier_tables(orders, lon_total)
    forward_table = jnp.stack([cosines, -sines], axis=1).astype(jnp.bfloat16)
    spectral_rows = jnp.einsum('acn,nxm->xacm', field_in.astype(jnp.float32), forward_table.astype(jnp.float32)).astype(jnp.bfloat16)
    weight_f32 = mix_weight.astype(jnp.float32)

    def per_block(block_start):
        block_orders = block_start + jnp.arange(degree_block, dtype=jnp.int32)
        analysis, synthesis = legendre_tables(block_orders, lat_total, mode_total)
        block_part = lax.dynamic_slice_in_dim(spectral_rows, block_start, degree_block, 3)
        coeffs = jnp.einsum('lmj,xjcm->mxcl', analysis.astype(jnp.float32), block_part.astype(jnp.float32)).astype(jnp.bfloat16)
        mixed = mix_channels(coeffs.astype(jnp.float32), weight_f32).astype(jnp.bfloat16)
        synth_rows = jnp.einsum('lmj,mxcl->xjcm', synthesis.astype(jnp.float32), mixed.astype(jnp.float32)).astype(jnp.bfloat16)
        return (mixed, synth_rows)
    block_starts = jnp.arange(0, mode_total, degree_block, dtype=jnp.int32)
    mixed_all, synth_all = lax.map(per_block, block_starts)
    mixed_all = mixed_all.reshape(mode_total, 2, channels, mode_total)
    synth_all = jnp.transpose(synth_all, (1, 2, 3, 0, 4)).reshape(2, lat_total, channels, mode_total)
    order_weight = jnp.where(orders == 0, jnp.float32(1.0), jnp.float32(2.0)) / lon_total
    inverse_table = jnp.stack([cosines.T * order_weight[:, None], -sines.T * order_weight[:, None]], axis=0).astype(jnp.bfloat16)
    wave_out = jnp.einsum('xacm,xmn->acn', synth_all.astype(jnp.float32), inverse_table.astype(jnp.float32))
    field_out = (field_in.astype(jnp.float32) + jax.nn.gelu(wave_out)).astype(jnp.bfloat16)
    spectrum = jnp.take(mixed_all, order_slots, axis=0)
    return (field_out, spectrum)
```

```python
import functools
import math

import jax
import jax.numpy as jnp
import numpy as np
from jax import lax
from jax.experimental import pallas as pl
from jax.experimental.pallas import tpu as pltpu
from jax.sharding import PartitionSpec as P

PAD = 16
PAIRS = 8
LANES = 128
NO_ORDER = 1000
RESCALE_BITS = 60
f32 = jnp.float32
bf16 = jnp.bfloat16


def cos_turns(turns):
    part = turns - jnp.floor(turns + 0.5)
    y = part * math.pi
    z = y * y
    s = 1.0 / 362880 - z * (1.0 / 39916800)
    s = -1.0 / 5040 + z * s
    s = 1.0 / 120 + z * s
    s = -1.0 / 6 + z * s
    s = y * (1.0 + z * s)
    return 1.0 - 2.0 * s * s


def minus_sin_turns(turns):
    return cos_turns(turns + 0.25)


def chunk_transpose(rows):
    lane = lax.broadcasted_iota(jnp.int32, rows[0].shape, 1)
    low = lane < 64
    even = (lane // 32) % 2 == 0
    mid = [None] * 4
    for i in range(2):
        a, b = rows[i], rows[i + 2]
        mid[i] = jnp.where(low, a, pltpu.roll(b, 64, 1))
        mid[i + 2] = jnp.where(low, pltpu.roll(a, 64, 1), b)
    out = []
    for i in (0, 2):
        a, b = mid[i], mid[i + 1]
        out.append(jnp.where(even, a, pltpu.roll(b, 32, 1)))
        out.append(jnp.where(even, pltpu.roll(a, 96, 1), b))
    return out


def forward_kernel(lat_dev, index_ref, quad_ref, field_ref, order_ref, out_ref, table, rows, turned):
    lon = table.shape[0]
    half = table.shape[1] // 4
    order = order_ref[...]
    step_cos = cos_turns(order * (LANES / lon))
    step_sin = -minus_sin_turns(order * (LANES / lon))

    @pl.loop(0, LANES // PAD)
    def _(r):
        n = (lax.broadcasted_iota(jnp.int32, (PAD, order.shape[1]), 0) + r * PAD).astype(f32)
        turns = order * n * (1.0 / lon)
        re, im = cos_turns(turns), minus_sin_turns(turns)
        for k in range(lon // LANES):
            at = pl.ds(pl.multiple_of(k * LANES + r * PAD, PAD), PAD)
            for m2 in range(2):
                cut = slice(m2 * half, (m2 + 1) * half)
                table[at, 2 * m2 * half : (2 * m2 + 1) * half] = re[:, cut].astype(bf16)
                table[at, (2 * m2 + 1) * half : (2 * m2 + 2) * half] = im[:, cut].astype(bf16)
            re, im = re * step_cos + im * step_sin, im * step_cos - re * step_sin

    ch_dev = field_ref.shape[1]
    field = field_ref[...].reshape(lat_dev * ch_dev, lon)
    for q in range(4):
        part = jnp.dot(field, table[:, q * half : (q + 1) * half], preferred_element_type=f32)
        rows[:, q] = part.reshape(lat_dev, ch_dev, half)
    first = index_ref[0] * lat_dev
    for j in range(lat_dev):
        block = rows[j].reshape(4 * ch_dev, half) * quad_ref[first + j]
        turned[pl.ds(j, half, stride=PAD), :] = block.T
    turned[pl.ds(lat_dev, half, stride=PAD), :] = jnp.zeros((half, LANES), f32)
    out_ref[...] = turned[...].astype(bf16).reshape(out_ref.shape)


def inverse_table_kernel(order_ref, out_ref):
    lon = out_ref.shape[1]
    half = out_ref.shape[0] // 4
    steps = half // PAD

    @pl.loop(0, 2 * steps)
    def _(r):
        order = order_ref[pl.ds(pl.multiple_of(r * PAD, PAD), PAD), :]
        step_cos = cos_turns(order * (LANES / lon))
        step_sin = -minus_sin_turns(order * (LANES / lon))
        n = lax.broadcasted_iota(jnp.int32, (PAD, LANES), 1).astype(f32)
        turns = order * n * (1.0 / lon)
        re, im = cos_turns(turns), minus_sin_turns(turns)
        top = (r // steps) * (2 * half) + (r % steps) * PAD
        for k in range(lon // LANES):
            cut = slice(k * LANES, (k + 1) * LANES)
            out_ref[pl.ds(pl.multiple_of(top, PAD), PAD), cut] = re.astype(bf16)
            out_ref[pl.ds(pl.multiple_of(top + half, PAD), PAD), cut] = im.astype(bf16)
            re, im = re * step_cos + im * step_sin, im * step_cos - re * step_sin


def legendre_kernel(
    deg_dev, blocks, scale_ref, order_ref, geo_ref, prod_ref, out_ref, cur, bef, resc, start, expo, root, buf
):
    groups = cur.shape[0]
    log_step = RESCALE_BITS * math.log(2.0)
    shrink = 2.0 ** (-RESCALE_BITS)
    limit = 2.0**RESCALE_BITS
    order = order_ref[...]
    order_sq = order * order

    @pl.when(pl.program_id(0) == 0)
    def _():
        cur[...] = jnp.zeros_like(cur)
        bef[...] = jnp.zeros_like(bef)
        resc[...] = jnp.zeros_like(resc)
        root[...] = jnp.zeros_like(root)
        picked = jnp.zeros((PAD, 1), f32)
        for g in range(groups):
            lane = lax.broadcasted_iota(jnp.int32, (PAD, LANES), 1) + g * LANES
            hit = order == lane.astype(f32)
            term = jnp.where(hit, prod_ref[:, g * LANES : (g + 1) * LANES], 0.0)
            picked = picked + jnp.sum(term, axis=1, keepdims=True)
        head = 0.5 * jnp.log(order + 0.5) + picked
        for g in range(groups):
            log_start = head + order * geo_ref[1:2, g * LANES : (g + 1) * LANES]
            start[g] = log_start
            expo[g] = jnp.exp(log_start)
            buf[g, pl.ds(deg_dev, PAD, stride=PAD), :] = jnp.zeros((PAD, LANES), f32)

    @pl.loop(0, blocks)
    def _(block):
        first = (pl.program_id(0) * blocks + block) * deg_dev
        now = [cur[g] for g in range(groups)]
        old = [bef[g] for g in range(groups)]
        factor = [expo[g] for g in range(groups)]
        cosine = [geo_ref[0:1, g * LANES : (g + 1) * LANES] for g in range(groups)]
        root_prev = root[...]
        for i in range(deg_dev):
            degree = first + i
            deg = degree.astype(f32)
            gap = deg * deg - order_sq
            gap_one = jnp.maximum(gap, 1.0)
            inv = lax.rsqrt(gap_one)
            inv = inv * (1.5 - 0.5 * gap_one * inv * inv)
            alpha = inv * scale_ref[0, degree]
            beta = root_prev * scale_ref[1, degree]
            root_prev = jnp.maximum(gap, 0.0) * inv
            begin = jnp.where(order == deg, 1.0, 0.0)
            for g in range(groups):
                new = alpha * (cosine[g] * now[g] - beta * old[g]) + begin
                old[g], now[g] = now[g], new
                buf[g, pl.ds(i, PAD, stride=PAD), :] = new * factor[g]
            if i in (deg_dev // 2, deg_dev - 1):
                for g in range(groups):
                    large = jnp.abs(now[g]) > limit
                    ratio = jnp.where(large, shrink, 1.0)
                    now[g] = now[g] * ratio
                    old[g] = old[g] * ratio
                    count = resc[g] + jnp.where(large, 1.0, 0.0)
                    resc[g] = count
                    factor[g] = jnp.exp(start[g] + count * log_step)
        root[...] = root_prev
        for g in range(groups):
            cur[g] = now[g]
            bef[g] = old[g]
            expo[g] = factor[g]
            tile = buf[g].reshape(PAD, PAD, LANES).astype(bf16)
            out_ref[:, block, :, g * LANES : (g + 1) * LANES] = tile


def analysis_kernel(rows_ref, table_ref, out_ref):
    rows = rows_ref[...].reshape(-1, LANES)
    even = jnp.dot(table_ref[0], rows, preferred_element_type=f32)
    odd = jnp.dot(table_ref[1], rows, preferred_element_type=f32)
    lane = lax.broadcasted_iota(jnp.int32, even.shape, 1)
    out_ref[...] = jnp.where(lane < LANES // 2, even, odd).astype(bf16).reshape(out_ref.shape)


def mix_kernel(blocks, ch_count, coef_ref, weight_ref, out_ref, wide, mixed):
    degree = pl.program_id(0)
    jump = ch_count * PAD
    ch_dev = LANES // 4

    @pl.when(degree == 0)
    def _():
        wide[...] = coef_ref[...].reshape(wide.shape).astype(f32)
        count = blocks * ch_count
        mixed[pl.ds(PAD - 1, count, stride=PAD), :] = jnp.zeros((count, LANES), f32)

    groups = []
    for h in range(ch_count // 4):
        quads = [wide[pl.ds((4 * h + e) * PAD + degree, blocks, stride=jump), :] for e in range(4)]
        groups.append(chunk_transpose(quads))
    left = jnp.concatenate(
        [jnp.concatenate([g[q] for g in groups], axis=1) for q in range(4)], axis=0
    ).astype(bf16)
    channels = ch_count * ch_dev
    contract = (((1,), (1,)), ((), ()))
    prod = [
        lax.dot_general(
            left, weight_ref[:, w, 0].reshape(channels, channels), contract, preferred_element_type=f32
        )
        for w in range(2)
    ]

    def take(w, q):
        return prod[w][q * blocks : (q + 1) * blocks]

    results = []
    for m2 in range(2):
        results.append(take(0, 2 * m2) - take(1, 2 * m2 + 1))
        results.append(take(1, 2 * m2) + take(0, 2 * m2 + 1))
    for h in range(ch_count // 4):
        quads = chunk_transpose([r[:, h * LANES : (h + 1) * LANES] for r in results])
        for e in range(4):
            mixed[pl.ds((4 * h + e) * PAD + degree, blocks, stride=jump), :] = quads[e]

    @pl.when(degree == pl.num_programs(0) - 1)
    def _():
        out_ref[...] = mixed[...].astype(bf16).reshape(out_ref.shape)


def synthesis_kernel(ord_dev, lon, order_ref, mixed_ref, table_ref, pick_ref, out_ref, spec_ref):
    pair = pl.program_id(0)
    side = mixed_ref[...].reshape(-1, LANES).astype(f32).T.astype(bf16)
    half = LANES // 2
    spec = jnp.dot(side, pick_ref[...], preferred_element_type=f32).astype(bf16)
    shape = spec_ref.shape[1:]
    spec_ref[2 * pair] = spec[:half].reshape(shape)

    @pl.when(2 * pair + 1 < ord_dev)
    def _():
        spec_ref[2 * pair + 1] = spec[half:].reshape(shape)

    parts = []
    for m2 in range(2):
        weight = jnp.where(order_ref[2 * pair + m2] == 0, 1.0 / lon, 2.0 / lon)
        part = jnp.dot(
            side[m2 * half : (m2 + 1) * half], table_ref[m2], preferred_element_type=f32
        )
        parts.append(part * weight)
    out_ref[...] = jnp.concatenate(parts, axis=0).T.astype(bf16).reshape(out_ref.shape)


def backward_kernel(lat_dev, rows_ref, table_ref, field_ref, out_ref, wide, left):
    half = rows_ref.shape[0] * rows_ref.shape[1]
    ch_dev = LANES // 4
    wide[...] = rows_ref[...].reshape(wide.shape).astype(f32)
    for j in range(lat_dev):
        block = wide[pl.ds(j, half, stride=PAD), :].T.astype(bf16)
        for q in range(4):
            left[j * ch_dev : (j + 1) * ch_dev, q * half : (q + 1) * half] = block[
                q * ch_dev : (q + 1) * ch_dev
            ]
    lon = out_ref.shape[2]
    for b in range(4):
        cut = slice(b * lon // 4, (b + 1) * lon // 4)
        wave = jnp.dot(left[...], table_ref[:, cut], preferred_element_type=f32)
        cubic = wave * wave * wave
        grown = 0.5 * wave * (1.0 + jnp.tanh(math.sqrt(2.0 / math.pi) * (wave + 0.044715 * cubic)))
        field = field_ref[:, :, cut].astype(f32)
        out_ref[:, :, cut] = (field + grown.reshape(field.shape)).astype(bf16)


def params(mib, grid=False):
    more = dict(dimension_semantics=("arbitrary",)) if grid else {}
    return pltpu.CompilerParams(vmem_limit_bytes=mib << 20, **more)


def cost(flops, moved):
    return pl.CostEstimate(flops=int(flops), bytes_accessed=int(moved), transcendentals=0)


def on_device(field_in, mix_weight, order_slots):
    lat_dev, ch_dev, lon = field_in.shape
    lat_count = lax.axis_size("lat")
    ch_count = lax.axis_size("ch")
    lat_total = lat_dev * lat_count
    modes = order_slots.shape[0]
    ord_dev = modes // lat_count
    full = lat_count * PAD
    half = lat_count * PAIRS
    index = lax.axis_index("lat")
    vmem = pl.BlockSpec(memory_space=pltpu.VMEM)
    smem = pl.BlockSpec(memory_space=pltpu.SMEM)
    buffer = jax.ShapeDtypeStruct((lat_count, PAIRS, PAD, LANES), bf16)

    angle = math.pi * (np.arange(lat_total) + 0.5) / lat_total
    quad = (math.pi / lat_total * np.sin(angle)).astype(np.float32)
    geo = np.zeros((2, lat_count, PAD), np.float32)
    geo[0, :, :lat_dev] = np.cos(angle).reshape(lat_count, lat_dev)
    geo[1, :, :lat_dev] = np.log(np.sin(angle)).reshape(lat_count, lat_dev)
    geo = geo.reshape(2, full)
    k = np.arange(1, modes)
    prod = np.zeros((1, full), np.float32)
    prod[0, 1:modes] = np.cumsum(0.5 * np.log((2.0 * k - 1.0) / (2.0 * k)))
    deg = np.arange(modes, dtype=np.float64)
    scale = np.sqrt(np.maximum(4.0 * deg * deg - 1.0, 1.0))
    scales = np.ones((2, modes), np.float32)
    scales[0] = scale
    scales[1, 1:] = 1.0 / scale[:-1]
    pick = np.zeros((lat_count, PAD, modes), np.float32)
    pick[:, :ord_dev] = np.eye(modes, dtype=np.float32).reshape(lat_count, ord_dev, modes)
    pick = jnp.asarray(pick.reshape(full, modes), bf16)

    padded = jnp.pad(
        order_slots.reshape(lat_count, ord_dev), ((0, 0), (0, PAD - ord_dev)), constant_values=NO_ORDER
    )
    mine = lax.dynamic_slice_in_dim(padded, index, 1, 0).reshape(PAD)
    by_pair = padded.reshape(lat_count, PAIRS, 2).transpose(2, 0, 1).astype(f32)

    weights = lax.all_gather(jnp.transpose(mix_weight, (0, 3, 2, 1)), "ch", axis=0)

    rows = pl.pallas_call(
        functools.partial(forward_kernel, lat_dev),
        out_shape=buffer,
        in_specs=[smem, smem, vmem, vmem],
        out_specs=vmem,
        scratch_shapes=[
            pltpu.VMEM((lon, 4 * half), bf16),
            pltpu.VMEM((lat_dev, 4, ch_dev, half), f32),
            pltpu.VMEM((half * PAD, LANES), f32),
        ],
        compiler_params=params(32),
        name="forward",
    )(index.reshape(1), jnp.asarray(quad), field_in, by_pair.reshape(1, 2 * half))
    rows = lax.all_to_all(rows, "lat", 0, 0, tiled=True)

    blocks = 4
    groups = full // LANES
    state = pltpu.VMEM((groups, PAD, LANES), f32)
    legendre = pl.pallas_call(
        functools.partial(legendre_kernel, ord_dev, blocks),
        grid=(lat_count // blocks,),
        out_shape=jax.ShapeDtypeStruct((PAD, lat_count, PAD, full), bf16),
        in_specs=[smem, vmem, vmem, vmem],
        out_specs=pl.BlockSpec((PAD, blocks, PAD, full), lambda i: (0, i, 0, 0)),
        scratch_shapes=[state] * 5
        + [pltpu.VMEM((PAD, LANES), f32), pltpu.VMEM((groups, PAD * PAD, LANES), f32)],
        compiler_params=params(32, True),
        cost_estimate=cost(8e9, 2e7),
        name="legendre",
    )(
        jnp.asarray(scales),
        jnp.broadcast_to(mine.astype(f32)[:, None], (PAD, LANES)),
        jnp.asarray(geo),
        jnp.asarray(prod),
    )
    legendre = legendre.reshape(PAD, full, full)
    inverse_table = pl.pallas_call(
        inverse_table_kernel,
        out_shape=jax.ShapeDtypeStruct((4 * half, lon), bf16),
        in_specs=[vmem],
        out_specs=vmem,
        compiler_params=params(32),
        cost_estimate=cost(2e9, 4e6),
        name="inverse_table",
    )(jnp.broadcast_to(by_pair.reshape(2 * half, 1), (2 * half, LANES)))

    pair_block = pl.BlockSpec((lat_count, 1, PAD, LANES), lambda p: (0, p, 0, 0))
    table_block = pl.BlockSpec((2, full, full), lambda p: (p, 0, 0))
    coeffs = pl.pallas_call(
        analysis_kernel,
        grid=(PAIRS,),
        out_shape=buffer,
        in_specs=[pair_block, table_block],
        out_specs=pair_block,
        compiler_params=params(32, True),
        name="analysis",
    )(rows, legendre)
    everywhere = lat_count * ch_count
    coeffs = lax.all_to_all(
        coeffs.reshape(everywhere, PAD, LANES), ("lat", "ch"), 0, 0, tiled=True
    )

    mixed = pl.pallas_call(
        functools.partial(mix_kernel, lat_count, ch_count),
        grid=(ord_dev,),
        out_shape=jax.ShapeDtypeStruct((everywhere, PAD, LANES), bf16),
        in_specs=[
            pl.BlockSpec((everywhere, PAD, LANES), lambda i: (0, 0, 0)),
            pl.BlockSpec((ch_count, 2, 1, ch_dev, ch_count * ch_dev), lambda i: (0, 0, i, 0, 0)),
        ],
        out_specs=pl.BlockSpec((everywhere, PAD, LANES), lambda i: (0, 0, 0)),
        scratch_shapes=[pltpu.VMEM((everywhere * PAD, LANES), f32)] * 2,
        compiler_params=params(32, True),
        name="mix",
    )(coeffs, weights)
    mixed = lax.all_to_all(mixed, ("lat", "ch"), 0, 0, tiled=True)

    synth, spectrum = pl.pallas_call(
        functools.partial(synthesis_kernel, ord_dev, lon),
        grid=(PAIRS,),
        out_shape=(buffer, jax.ShapeDtypeStruct((ord_dev, 2, ch_dev, modes), bf16)),
        in_specs=[smem, pair_block, table_block, pl.BlockSpec((full, modes), lambda p: (0, 0))],
        out_specs=(pair_block, pl.BlockSpec((ord_dev, 2, ch_dev, modes), lambda p: (0, 0, 0, 0))),
        compiler_params=params(32, True),
        name="synthesis",
    )(mine, mixed.reshape(buffer.shape), legendre, pick)
    synth = lax.all_to_all(synth, "lat", 0, 0, tiled=True)

    field_out = pl.pallas_call(
        functools.partial(backward_kernel, lat_dev),
        out_shape=jax.ShapeDtypeStruct(field_in.shape, bf16),
        in_specs=[vmem, vmem, vmem],
        out_specs=vmem,
        scratch_shapes=[
            pltpu.VMEM((half * PAD, LANES), f32),
            pltpu.VMEM((lat_dev * ch_dev, 4 * half), bf16),
        ],
        compiler_params=params(32),
        name="backward",
    )(synth, inverse_table, field_in)
    return (field_out, spectrum)


def solution(mesh):
    placed = (P("lat", "ch", None), P(None, None, "ch", "lat"), P())
    return jax.shard_map(
        on_device,
        mesh=mesh,
        in_specs=placed,
        out_specs=(P("lat", "ch", None), P("lat", None, "ch", None)),
        check_vma=False,
    )
```

```python
import functools
import math

import jax
import jax.numpy as jnp
import numpy as np
from jax import lax
from jax.experimental import pallas as pl
from jax.experimental.pallas import tpu as pltpu
from jax.sharding import PartitionSpec as P

PAD = 16
PAIRS = 8
LANES = 128
NO_ORDER = 1000
PITCH = 17
RESCALE_BITS = 60
f32 = jnp.float32
bf16 = jnp.bfloat16


VMEM_MIB = 57
TABLE_MIB = 63


def cos_turns(turns):
    part = turns - jnp.floor(turns + 0.5)
    y = part * math.pi
    z = y * y
    s = 1.0 / 362880 - z * (1.0 / 39916800)
    s = -1.0 / 5040 + z * s
    s = 1.0 / 120 + z * s
    s = -1.0 / 6 + z * s
    s = y * (1.0 + z * s)
    return 1.0 - 2.0 * s * s


def minus_sin_turns(turns):
    return cos_turns(turns + 0.25)


def chunk_transpose(rows):
    lane = lax.broadcasted_iota(jnp.int32, rows[0].shape, 1)
    low = lane < 64
    even = (lane // 32) % 2 == 0
    mid = [None] * 4
    for i in range(2):
        a, b = rows[i], rows[i + 2]
        mid[i] = jnp.where(low, a, pltpu.roll(b, 64, 1))
        mid[i + 2] = jnp.where(low, pltpu.roll(a, 64, 1), b)
    out = []
    for i in (0, 2):
        a, b = mid[i], mid[i + 1]
        out.append(jnp.where(even, a, pltpu.roll(b, 32, 1)))
        out.append(jnp.where(even, pltpu.roll(a, 96, 1), b))
    return out


def slot_of(j, lat_dev, index, lat_count):
    return jnp.where(index < lat_count // 2, j, lat_dev - 1 - j)


def forward_kernel(lat_dev, lat_count, index_ref, order_ref, field_hbm, out_ref, table, field_ref, rows, turned, sem):
    fetch = pltpu.make_async_copy(field_hbm, field_ref, sem)
    fetch.start()
    lon = table.shape[0]
    half = table.shape[1] // 4
    order = order_ref[...]
    step_cos = cos_turns(order * (LANES / lon))
    step_sin = -minus_sin_turns(order * (LANES / lon))

    @pl.loop(0, LANES // PAD)
    def _(r):
        n = (lax.broadcasted_iota(jnp.int32, (PAD, order.shape[1]), 0) + r * PAD).astype(f32)
        turns = order * n * (1.0 / lon)
        re, im = cos_turns(turns), minus_sin_turns(turns)
        for k in range(lon // LANES):
            at = pl.ds(pl.multiple_of(k * LANES + r * PAD, PAD), PAD)
            for m2 in range(2):
                cut = slice(m2 * half, (m2 + 1) * half)
                table[at, 2 * m2 * half : (2 * m2 + 1) * half] = re[:, cut].astype(bf16)
                table[at, (2 * m2 + 1) * half : (2 * m2 + 2) * half] = im[:, cut].astype(bf16)
            re, im = re * step_cos + im * step_sin, im * step_cos - re * step_sin

    fetch.wait()
    ch_dev = field_ref.shape[1]
    field = field_ref[...].reshape(lat_dev * ch_dev, lon)
    for q in range(4):
        part = jnp.dot(field, table[:, q * half : (q + 1) * half], preferred_element_type=f32)
        rows[:, q] = part.reshape(lat_dev, ch_dev, half)
    index = index_ref[0]
    lat_total = lat_dev * lat_count
    for j in range(lat_dev):
        place = jnp.full((1, half), index * lat_dev + j, jnp.int32).astype(f32)
        quad = cos_turns((place + 0.5) * (0.5 / lat_total) - 0.25) * (math.pi / lat_total)
        block = rows[j].reshape(4 * ch_dev, half) * quad
        turned[pl.ds(slot_of(j, lat_dev, index, lat_count), half, stride=PITCH), :] = block.T
    turned[pl.ds(lat_dev, half, stride=PITCH), :] = jnp.zeros((half, LANES), f32)
    for i in range(half):
        tile = turned[i * PITCH : i * PITCH + PAD, :]
        out_ref[i // PAIRS, i % PAIRS] = tile.astype(bf16)


def inverse_table_kernel(order_ref, out_hbm, out_ref, sem):
    lon = out_ref.shape[1]
    half = out_ref.shape[0] // 4
    steps = half // PAD

    @pl.loop(0, 2 * steps)
    def _(r):
        order = order_ref[pl.ds(pl.multiple_of(r * PAD, PAD), PAD), :]
        step_cos = cos_turns(order * (LANES / lon))
        step_sin = -minus_sin_turns(order * (LANES / lon))
        n = lax.broadcasted_iota(jnp.int32, (PAD, LANES), 1).astype(f32)
        turns = order * n * (1.0 / lon)
        re, im = cos_turns(turns), minus_sin_turns(turns)
        top = (r // steps) * (2 * half) + (r % steps) * PAD
        for k in range(lon // LANES):
            cut = slice(k * LANES, (k + 1) * LANES)
            out_ref[pl.ds(pl.multiple_of(top, PAD), PAD), cut] = re.astype(bf16)
            out_ref[pl.ds(pl.multiple_of(top + half, PAD), PAD), cut] = im.astype(bf16)
            re, im = re * step_cos + im * step_sin, im * step_cos - re * step_sin

    copy = pltpu.make_async_copy(out_ref, out_hbm, sem)
    copy.start()
    copy.wait()


def legendre_kernel(
    deg_dev, scale_ref, order_ref, geo_ref, prod_ref, out_hbm, cur, bef, resc, start, expo, root, buf, table, sems
):
    groups = cur.shape[0]
    log_step = RESCALE_BITS * math.log(2.0)
    shrink = 2.0 ** (-RESCALE_BITS)
    limit = 2.0**RESCALE_BITS
    order = order_ref[...]
    order_sq = order * order
    for state in (cur, bef, resc, root):
        state[...] = jnp.zeros_like(state)
    picked = jnp.zeros((PAD, 1), f32)
    for g in range(prod_ref.shape[1] // LANES):
        lane = lax.broadcasted_iota(jnp.int32, (PAD, LANES), 1) + g * LANES
        hit = order == lane.astype(f32)
        term = jnp.where(hit, prod_ref[:, g * LANES : (g + 1) * LANES], 0.0)
        picked = picked + jnp.sum(term, axis=1, keepdims=True)
    head = 0.5 * jnp.log(order + 0.5) + picked
    for g in range(groups):
        log_start = head + order * geo_ref[1:2, g * LANES : (g + 1) * LANES]
        start[g] = log_start
        expo[g] = jnp.exp(log_start)
        buf[g, pl.ds(deg_dev, PAD, stride=PITCH), :] = jnp.zeros((PAD, LANES), f32)

    def block(index):
        first = index * deg_dev
        now = [cur[g] for g in range(groups)]
        old = [bef[g] for g in range(groups)]
        factor = [expo[g] for g in range(groups)]
        cosine = [geo_ref[0:1, g * LANES : (g + 1) * LANES] for g in range(groups)]
        root_prev = root[...]
        for i in range(deg_dev):
            degree = first + i
            deg = degree.astype(f32)
            gap = deg * deg - order_sq
            gap_one = jnp.maximum(gap, 1.0)
            inv = lax.rsqrt(gap_one)
            inv = inv * (1.5 - 0.5 * gap_one * inv * inv)
            alpha = inv * scale_ref[0, degree]
            beta = root_prev * scale_ref[1, degree]
            root_prev = jnp.maximum(gap, 0.0) * inv
            begin = jnp.where(order == deg, 1.0, 0.0)
            for g in range(groups):
                new = alpha * (cosine[g] * now[g] - beta * old[g]) + begin
                old[g], now[g] = now[g], new
                buf[g, pl.ds(i, PAD, stride=PITCH), :] = new * factor[g]
            if i in (deg_dev // 2, deg_dev - 1):
                for g in range(groups):
                    large = jnp.abs(now[g]) > limit
                    ratio = jnp.where(large, shrink, 1.0)
                    now[g] = now[g] * ratio
                    old[g] = old[g] * ratio
                    count = resc[g] + jnp.where(large, 1.0, 0.0)
                    resc[g] = count
                    factor[g] = jnp.exp(start[g] + count * log_step)
        root[...] = root_prev
        for g in range(groups):
            cur[g] = now[g]
            bef[g] = old[g]
            expo[g] = factor[g]
            for m in range(PAD):
                tile = buf[g, m * PITCH : m * PITCH + PAD, :].astype(bf16)
                table[m, index, :, g * LANES : (g + 1) * LANES] = tile

    parts = sems.shape[0]
    count = table.shape[1] // parts
    copies = []
    for part in range(parts):
        pl.loop(part * count, (part + 1) * count)(block)
        cut = slice(part * count, (part + 1) * count)
        copies.append(pltpu.make_async_copy(table.at[:, cut], out_hbm.at[:, cut], sems.at[part]))
        copies[-1].start()
    for copy in copies:
        copy.wait()


def degree_parity(shape, dim, ord_dev):
    i = lax.broadcasted_iota(jnp.int32, shape, dim)
    return ((i // PAD) * ord_dev + i % PAD) & 1


def fetch_pairs(table_hbm, table, sems):
    def copy(p):
        cut = pl.ds(2 * p, 2)
        return pltpu.make_async_copy(table_hbm.at[cut], table.at[cut], sems.at[p])

    for p in range(PAIRS):
        copy(p).start()
    return copy


def analysis_kernel(ord_dev, order_ref, rows_ref, table_hbm, out_ref, table, sems):
    copy = fetch_pairs(table_hbm, table, sems)
    count = rows_ref.shape[0]
    parity = degree_parity((table.shape[1], LANES), 0, ord_dev)

    @pl.loop(0, PAIRS)
    def _(p):
        north = jnp.concatenate([rows_ref[s, p] for s in range(count // 2)], axis=0)
        south = jnp.concatenate([rows_ref[count - 1 - s, p] for s in range(count // 2)], axis=0)
        both = jnp.concatenate([north, south], axis=1)
        copy(p).wait()
        parts = []
        for m2 in range(2):
            order = order_ref[2 * p + m2]
            prod = jnp.dot(table[2 * p + m2], both, preferred_element_type=f32)
            mirror = prod[:, LANES:]
            parts.append(prod[:, :LANES] + jnp.where(parity == (order & 1), mirror, -mirror))
        lane = lax.broadcasted_iota(jnp.int32, parts[0].shape, 1)
        out = jnp.where(lane < LANES // 2, parts[0], parts[1]).astype(bf16)
        for d in range(count):
            out_ref[d, p] = out[d * PAD : (d + 1) * PAD]


def mix_kernel(blocks, ch_count, deg_dev, coef_ref, weight_hbm, out_ref, wide, mixed, weight, sems):
    jump = ch_count * PAD + 1
    ch_dev = LANES // 4
    channels = ch_count * ch_dev
    contract = (((1,), (1,)), ((), ()))

    def copy(degree):
        return pltpu.make_async_copy(weight_hbm.at[:, :, degree], weight.at[degree], sems.at[degree])

    for degree in range(deg_dev):
        copy(degree).start()
    for d in range(blocks):
        part = coef_ref[d * ch_count : (d + 1) * ch_count].reshape(jump - 1, LANES)
        wide[d * jump : (d + 1) * jump - 1, :] = part.astype(f32)
    for e in range(ch_count):
        mixed[pl.ds((e + 1) * PAD - 1, blocks, stride=jump), :] = jnp.zeros((blocks, LANES), f32)

    def one_degree(degree):
        groups = []
        for h in range(ch_count // 4):
            quads = [wide[pl.ds((4 * h + e) * PAD + degree, blocks, stride=jump), :] for e in range(4)]
            groups.append(chunk_transpose(quads))
        left = jnp.concatenate(
            [jnp.concatenate([g[q] for g in groups], axis=1) for q in range(4)], axis=0
        ).astype(bf16)
        prod = [
            lax.dot_general(
                left,
                weight[degree, :, w].reshape(channels, channels),
                contract,
                preferred_element_type=f32,
            )
            for w in range(2)
        ]

        def take(w, q):
            return prod[w][q * blocks : (q + 1) * blocks]

        results = []
        for m2 in range(2):
            results.append(take(0, 2 * m2) - take(1, 2 * m2 + 1))
            results.append(take(1, 2 * m2) + take(0, 2 * m2 + 1))
        for h in range(ch_count // 4):
            quads = chunk_transpose([r[:, h * LANES : (h + 1) * LANES] for r in results])
            for e in range(4):
                mixed[pl.ds((4 * h + e) * PAD + degree, blocks, stride=jump), :] = quads[e]

    group = MIX_GROUP

    @pl.loop(0, deg_dev // group)
    def _(step):
        for i in range(group):
            copy(step * group + i).wait()
        for i in range(group):
            one_degree(step * group + i)

    for d in range(blocks):
        part = mixed[d * jump : (d + 1) * jump - 1, :].astype(bf16)
        out_ref[d * ch_count : (d + 1) * ch_count] = part.reshape(ch_count, PAD, LANES)


def synthesis_kernel(
    ord_dev, lon, order_ref, mixed_ref, pick_ref, table_hbm, out_ref, spec_ref, table, sems
):
    copy = fetch_pairs(table_hbm, table, sems)
    count = out_ref.shape[0]
    half = LANES // 2
    shape = spec_ref.shape[1:]
    parity = degree_parity((half, table.shape[1]), 1, ord_dev)

    @pl.loop(0, PAIRS)
    def _(p):
        side = jnp.concatenate([mixed_ref[d, p] for d in range(count)], axis=0).astype(f32).T
        spec = jnp.dot(side.astype(bf16), pick_ref[...], preferred_element_type=f32).astype(bf16)
        spec_ref[2 * p] = spec[:half].reshape(shape)

        @pl.when(2 * p + 1 < ord_dev)
        def _():
            spec_ref[2 * p + 1] = spec[half:].reshape(shape)

        copy(p).wait()
        north, south = [], []
        for m2 in range(2):
            order = order_ref[2 * p + m2]
            weight = jnp.where(order == 0, 1.0 / lon, 2.0 / lon)
            part = side[m2 * half : (m2 + 1) * half]
            same = parity == (order & 1)
            split = jnp.concatenate([jnp.where(same, part, 0.0), jnp.where(same, 0.0, part)], axis=0)
            prod = jnp.dot(split.astype(bf16), table[2 * p + m2], preferred_element_type=f32)
            north.append((prod[:half] + prod[half:]) * weight)
            south.append((prod[:half] - prod[half:]) * weight)
        up = jnp.concatenate(north, axis=0).T.astype(bf16)
        down = jnp.concatenate(south, axis=0).T.astype(bf16)
        for s in range(count // 2):
            out_ref[s, p] = up[s * PAD : (s + 1) * PAD]
            out_ref[count - 1 - s, p] = down[s * PAD : (s + 1) * PAD]


def backward_kernel(
    lat_dev, lat_count, index_ref, rows_ref, table_hbm, field_hbm, out_ref, wide, left, table_ref, field_ref, sems
):
    copies = [
        pltpu.make_async_copy(table_hbm, table_ref, sems.at[0]),
        pltpu.make_async_copy(field_hbm, field_ref, sems.at[1]),
    ]
    for copy in copies:
        copy.start()
    half = rows_ref.shape[0] * rows_ref.shape[1]
    ch_dev = LANES // 4
    for i in range(half):
        wide[i * PITCH : i * PITCH + PAD, :] = rows_ref[i // PAIRS, i % PAIRS].astype(f32)
    for j in range(lat_dev):
        slot = slot_of(j, lat_dev, index_ref[0], lat_count)
        block = wide[pl.ds(slot, half, stride=PITCH), :].T.astype(bf16)
        for q in range(4):
            left[j * ch_dev : (j + 1) * ch_dev, q * half : (q + 1) * half] = block[
                q * ch_dev : (q + 1) * ch_dev
            ]
    lon = out_ref.shape[2]
    for copy in copies:
        copy.wait()
    for b in range(4):
        cut = slice(b * lon // 4, (b + 1) * lon // 4)
        wave = jnp.dot(left[...], table_ref[:, cut], preferred_element_type=f32)
        cubic = wave * wave * wave
        grown = 0.5 * wave * (1.0 + jnp.tanh(math.sqrt(2.0 / math.pi) * (wave + 0.044715 * cubic)))
        field = field_ref[:, :, cut].astype(f32)
        out_ref[:, :, cut] = (field + grown.reshape(field.shape)).astype(bf16)


def params(mib=VMEM_MIB):
    return pltpu.CompilerParams(vmem_limit_bytes=int(mib * 2**20))


def cost(flops, moved):
    return pl.CostEstimate(flops=int(flops), bytes_accessed=int(moved), transcendentals=0)


MIX_GROUP = 3
vmem = pl.BlockSpec(memory_space=pltpu.VMEM)
smem = pl.BlockSpec(memory_space=pltpu.SMEM)
hbm = pl.BlockSpec(memory_space=pltpu.HBM)


def buffer_of(lat_count):
    return jax.ShapeDtypeStruct((lat_count, PAIRS, PAD, LANES), bf16)


def call_forward(lat_count, index, order_lanes, field_in):
    lat_dev, ch_dev, lon = field_in.shape
    half = lat_count * PAIRS
    return pl.pallas_call(
        functools.partial(forward_kernel, lat_dev, lat_count),
        out_shape=buffer_of(lat_count),
        in_specs=[smem, vmem, hbm],
        out_specs=vmem,
        scratch_shapes=[
            pltpu.VMEM((lon, 4 * half), bf16),
            pltpu.VMEM(field_in.shape, bf16),
            pltpu.VMEM((lat_dev, 4, ch_dev, half), f32),
            pltpu.VMEM((half * PITCH, LANES), f32),
            pltpu.SemaphoreType.DMA,
        ],
        compiler_params=params(),
        name="forward",
    )(index, order_lanes, field_in)


def call_legendre(lat_count, lat_dev, modes, order_rows):
    lat_total = lat_count * lat_dev
    ord_dev = modes // lat_count
    full = lat_count * PAD
    near = full // 2
    angle = math.pi * (np.arange(lat_total) + 0.5) / lat_total
    geo = np.zeros((2, lat_count, PAD), np.float32)
    geo[0, :, :lat_dev] = np.cos(angle).reshape(lat_count, lat_dev)
    geo[1, :, :lat_dev] = np.log(np.sin(angle)).reshape(lat_count, lat_dev)
    geo = geo.reshape(2, full)[:, :near]
    k = np.arange(1, modes)
    prod = np.zeros((1, full), np.float32)
    prod[0, 1:modes] = np.cumsum(0.5 * np.log((2.0 * k - 1.0) / (2.0 * k)))
    deg = np.arange(modes, dtype=np.float64)
    scale = np.sqrt(np.maximum(4.0 * deg * deg - 1.0, 1.0))
    scales = np.ones((2, modes), np.float32)
    scales[0] = scale
    scales[1, 1:] = 1.0 / scale[:-1]
    groups = near // LANES
    parts = 4
    state = pltpu.VMEM((groups, PAD, LANES), f32)
    table = pl.pallas_call(
        functools.partial(legendre_kernel, ord_dev),
        out_shape=jax.ShapeDtypeStruct((PAD, lat_count, PAD, near), bf16),
        in_specs=[smem, vmem, vmem, vmem],
        out_specs=hbm,
        scratch_shapes=[state] * 5
        + [
            pltpu.VMEM((PAD, LANES), f32),
            pltpu.VMEM((groups, PAD * PITCH, LANES), f32),
            pltpu.VMEM((PAD, lat_count, PAD, near), bf16),
            pltpu.SemaphoreType.DMA((parts,)),
        ],
        compiler_params=params(TABLE_MIB),
        cost_estimate=cost(8e9, 2e7),
        name="legendre",
    )(jnp.asarray(scales), order_rows, jnp.asarray(geo), jnp.asarray(prod))
    return table.reshape(PAD, full, near)


def call_inverse_table(lon, order_rows):
    return pl.pallas_call(
        inverse_table_kernel,
        out_shape=jax.ShapeDtypeStruct((2 * order_rows.shape[0], lon), bf16),
        in_specs=[vmem],
        out_specs=hbm,
        scratch_shapes=[
            pltpu.VMEM((2 * order_rows.shape[0], lon), bf16),
            pltpu.SemaphoreType.DMA,
        ],
        compiler_params=params(TABLE_MIB),
        cost_estimate=cost(2e9, 4e6),
        name="inverse_table",
    )(order_rows)


def call_analysis(ord_dev, orders, rows, table):
    return pl.pallas_call(
        functools.partial(analysis_kernel, ord_dev),
        out_shape=jax.ShapeDtypeStruct(rows.shape, bf16),
        in_specs=[smem, vmem, hbm],
        out_specs=vmem,
        scratch_shapes=[pltpu.VMEM(table.shape, bf16), pltpu.SemaphoreType.DMA((PAIRS,))],
        compiler_params=params(),
        name="analysis",
    )(orders, rows, table)


def call_mix(lat_count, coeffs, weights):
    ch_count, _, ord_dev, ch_dev, channels = weights.shape
    return pl.pallas_call(
        functools.partial(mix_kernel, lat_count, ch_count, ord_dev),
        out_shape=jax.ShapeDtypeStruct(coeffs.shape, bf16),
        in_specs=[vmem, hbm],
        out_specs=vmem,
        scratch_shapes=[pltpu.VMEM((lat_count * (ch_count * PAD + 1), LANES), f32)] * 2
        + [
            pltpu.VMEM((ord_dev, ch_count, 2, ch_dev, channels), bf16),
            pltpu.SemaphoreType.DMA((ord_dev,)),
        ],
        compiler_params=params(),
        name="mix",
    )(coeffs, weights)


def call_synthesis(ord_dev, lon, orders, mixed, table):
    lat_count = mixed.shape[0]
    modes = ord_dev * lat_count
    full = lat_count * PAD
    ch_dev = LANES // 4
    pick = np.zeros((lat_count, PAD, modes), np.float32)
    pick[:, :ord_dev] = np.eye(modes, dtype=np.float32).reshape(lat_count, ord_dev, modes)
    pick = jnp.asarray(pick.reshape(full, modes), bf16)
    return pl.pallas_call(
        functools.partial(synthesis_kernel, ord_dev, lon),
        out_shape=(
            buffer_of(lat_count),
            jax.ShapeDtypeStruct((ord_dev, 2, ch_dev, modes), bf16),
        ),
        in_specs=[smem, vmem, vmem, hbm],
        out_specs=(vmem, vmem),
        scratch_shapes=[pltpu.VMEM(table.shape, bf16), pltpu.SemaphoreType.DMA((PAIRS,))],
        compiler_params=params(),
        name="synthesis",
    )(orders, mixed, pick, table)


def call_backward(index, rows, table, field_in):
    lat_dev, ch_dev, _ = field_in.shape
    lat_count = rows.shape[0]
    half = lat_count * PAIRS
    return pl.pallas_call(
        functools.partial(backward_kernel, lat_dev, lat_count),
        out_shape=jax.ShapeDtypeStruct(field_in.shape, bf16),
        in_specs=[smem, vmem, hbm, hbm],
        out_specs=vmem,
        scratch_shapes=[
            pltpu.VMEM((half * PITCH, LANES), f32),
            pltpu.VMEM((lat_dev * ch_dev, 4 * half), bf16),
            pltpu.VMEM(table.shape, bf16),
            pltpu.VMEM(field_in.shape, bf16),
            pltpu.SemaphoreType.DMA((2,)),
        ],
        compiler_params=params(),
        name="backward",
    )(index, rows, table, field_in)


def on_device(field_in, mix_weight, order_slots):
    lat_dev, _, lon = field_in.shape
    lat_count = lax.axis_size("lat")
    modes = order_slots.shape[0]
    ord_dev = modes // lat_count
    half = lat_count * PAIRS
    index = lax.axis_index("lat")
    padded = jnp.pad(
        order_slots.reshape(lat_count, ord_dev), ((0, 0), (0, PAD - ord_dev)), constant_values=NO_ORDER
    )
    mine = lax.dynamic_slice_in_dim(padded, index, 1, 0).reshape(PAD)
    by_pair = padded.reshape(lat_count, PAIRS, 2).transpose(2, 0, 1).astype(f32)
    index = index.reshape(1)

    weights = lax.all_gather(jnp.transpose(mix_weight, (0, 3, 2, 1)), "ch", axis=0)
    rows = call_forward(lat_count, index, by_pair.reshape(1, 2 * half), field_in)
    rows = lax.all_to_all(rows, "lat", 0, 0, tiled=True)
    order_rows = jnp.broadcast_to(mine.astype(f32)[:, None], (PAD, LANES))
    legendre = call_legendre(lat_count, lat_dev, modes, order_rows)
    order_rows = jnp.broadcast_to(by_pair.reshape(2 * half, 1), (2 * half, LANES))
    inverse_table = call_inverse_table(lon, order_rows)
    coeffs = call_analysis(ord_dev, mine, rows, legendre)
    coeffs = lax.all_to_all(coeffs.reshape(-1, PAD, LANES), ("lat", "ch"), 0, 0, tiled=True)
    mixed = call_mix(lat_count, coeffs, weights)
    mixed = lax.all_to_all(mixed, ("lat", "ch"), 0, 0, tiled=True)
    synth, spectrum = call_synthesis(ord_dev, lon, mine, mixed.reshape(rows.shape), legendre)
    synth = lax.all_to_all(synth, "lat", 0, 0, tiled=True)
    field_out = call_backward(index, synth, inverse_table, field_in)
    return (field_out, spectrum)


def solution(mesh):
    placed = (P("lat", "ch", None), P(None, None, "ch", "lat"), P())
    return jax.shard_map(
        on_device,
        mesh=mesh,
        in_specs=placed,
        out_specs=(P("lat", "ch", None), P("lat", None, "ch", None)),
        check_vma=False,
    )
```

```python
import functools
import math

import jax
import jax.numpy as jnp
import numpy as np
from jax import lax
from jax.experimental import pallas as pl
from jax.experimental.pallas import tpu as pltpu
from jax.sharding import PartitionSpec as P

PAD = 16
PAIRS = 8
LANES = 128
NO_ORDER = 1000
PITCH = 17
RESCALE_BITS = 60
f32 = jnp.float32
bf16 = jnp.bfloat16


VMEM_MIB = 50
TABLE_MIB = 57


def cos_turns(turns):
    part = turns - jnp.floor(turns + 0.5)
    y = part * math.pi
    z = y * y
    s = 1.0 / 362880 - z * (1.0 / 39916800)
    s = -1.0 / 5040 + z * s
    s = 1.0 / 120 + z * s
    s = -1.0 / 6 + z * s
    s = y * (1.0 + z * s)
    return 1.0 - 2.0 * s * s


def minus_sin_turns(turns):
    return cos_turns(turns + 0.25)


def chunk_transpose(rows):
    lane = lax.broadcasted_iota(jnp.int32, rows[0].shape, 1)
    low = lane < 64
    even = (lane // 32) % 2 == 0
    mid = [None] * 4
    for i in range(2):
        a, b = rows[i], rows[i + 2]
        mid[i] = jnp.where(low, a, pltpu.roll(b, 64, 1))
        mid[i + 2] = jnp.where(low, pltpu.roll(a, 64, 1), b)
    out = []
    for i in (0, 2):
        a, b = mid[i], mid[i + 1]
        out.append(jnp.where(even, a, pltpu.roll(b, 32, 1)))
        out.append(jnp.where(even, pltpu.roll(a, 96, 1), b))
    return out


def digits_of(slots_ref):
    slots = slots_ref[...].astype(f32)
    high = jnp.floor(slots * (1.0 / PAD))
    return high.astype(bf16), (slots - PAD * high).astype(bf16)


def one_hot(hit):
    return jnp.where(hit, 1.0, 0.0).astype(bf16)


def slot_wanted(place, ord_dev, half):
    within = 2 * (place % PAIRS) + place // half
    return jnp.where(within < ord_dev, (place % half) // PAIRS * ord_dev + within, -1)


def order_lanes(slots_ref, ord_dev, lat_count):
    modes = slots_ref.shape[1]
    half = lat_count * PAIRS
    wanted = slot_wanted(lax.broadcasted_iota(jnp.int32, (1, 2 * half), 1), ord_dev, half)
    pick = one_hot(lax.broadcasted_iota(jnp.int32, (modes, 2 * half), 0) == wanted)
    digits = [jnp.broadcast_to(d.astype(f32), (8, modes)).astype(bf16) for d in digits_of(slots_ref)]
    high, low = [jnp.dot(d, pick, preferred_element_type=f32) for d in digits]
    return high[0:1] * PAD + low[0:1]


def order_rows(slots_ref, ord_dev, lat_count):
    modes = slots_ref.shape[1]
    half = lat_count * PAIRS
    wanted = slot_wanted(lax.broadcasted_iota(jnp.int32, (2 * half, 1), 0), ord_dev, half)
    pick = one_hot(lax.broadcasted_iota(jnp.int32, (2 * half, modes), 1) == wanted)
    contract = (((1,), (1,)), ((), ()))
    high, low = [
        lax.dot_general(
            pick,
            jnp.broadcast_to(d.astype(f32), (LANES, modes)).astype(bf16),
            contract,
            preferred_element_type=f32,
        )
        for d in digits_of(slots_ref)
    ]
    return high * PAD + low


def order_column(slots, wanted):
    place = lax.broadcasted_iota(jnp.int32, (wanted.shape[0], slots.shape[1]), 1)
    return jnp.sum(jnp.where(place == wanted, slots, 0.0), axis=1, keepdims=True)


def slot_of(j, lat_dev, index, lat_count):
    return jnp.where(index < lat_count // 2, j, lat_dev - 1 - j)


def forward_kernel(
    lat_dev, lat_count, ord_dev, index_ref, slots_ref, field_hbm, out_hbm, table, field_ref, rows, turned, out_ref, sem, sems
):
    fetch = pltpu.make_async_copy(field_hbm, field_ref, sem)
    fetch.start()
    lon = table.shape[0]
    half = table.shape[1] // 4
    order = order_lanes(slots_ref, ord_dev, lat_count)
    step_cos = cos_turns(order * (LANES / lon))
    step_sin = -minus_sin_turns(order * (LANES / lon))

    @pl.loop(0, LANES // PAD)
    def _(r):
        n = (lax.broadcasted_iota(jnp.int32, (PAD, order.shape[1]), 0) + r * PAD).astype(f32)
        turns = order * n * (1.0 / lon)
        re, im = cos_turns(turns), minus_sin_turns(turns)
        for k in range(lon // LANES):
            at = pl.ds(pl.multiple_of(k * LANES + r * PAD, PAD), PAD)
            for m2 in range(2):
                cut = slice(m2 * half, (m2 + 1) * half)
                table[at, 2 * m2 * half : (2 * m2 + 1) * half] = re[:, cut].astype(bf16)
                table[at, (2 * m2 + 1) * half : (2 * m2 + 2) * half] = im[:, cut].astype(bf16)
            re, im = re * step_cos + im * step_sin, im * step_cos - re * step_sin

    fetch.wait()
    ch_dev = field_ref.shape[1]
    field = field_ref[...].reshape(lat_dev * ch_dev, lon)
    for q in range(4):
        part = jnp.dot(field, table[:, q * half : (q + 1) * half], preferred_element_type=f32)
        rows[:, q] = part.reshape(lat_dev, ch_dev, half)
    index = index_ref[0]
    lat_total = lat_dev * lat_count
    for j in range(lat_dev):
        place = jnp.full((1, half), index * lat_dev + j, jnp.int32).astype(f32)
        quad = cos_turns((place + 0.5) * (0.5 / lat_total) - 0.25) * (math.pi / lat_total)
        block = rows[j].reshape(4 * ch_dev, half) * quad
        turned[pl.ds(slot_of(j, lat_dev, index, lat_count), half, stride=PITCH), :] = block.T
    turned[pl.ds(lat_dev, half, stride=PITCH), :] = jnp.zeros((half, LANES), f32)
    copies = []
    part = lat_count // sems.shape[0]
    for d in range(lat_count):
        for p in range(PAIRS):
            i = d * PAIRS + p
            out_ref[d, p] = turned[i * PITCH : i * PITCH + PAD, :].astype(bf16)
        if d % part == part - 1:
            cut = slice(d + 1 - part, d + 1)
            copies.append(pltpu.make_async_copy(out_ref.at[cut], out_hbm.at[cut], sems.at[d // part]))
            copies[-1].start()
    for copy in copies:
        copy.wait()


def inverse_table_kernel(ord_dev, lat_count, slots_ref, out_hbm, out_ref, orders, sem):
    lon = out_ref.shape[1]
    half = out_ref.shape[0] // 4
    steps = half // PAD
    orders[...] = order_rows(slots_ref, ord_dev, lat_count)

    @pl.loop(0, 2 * steps)
    def _(r):
        order = orders[pl.ds(pl.multiple_of(r * PAD, PAD), PAD), :]
        step_cos = cos_turns(order * (LANES / lon))
        step_sin = -minus_sin_turns(order * (LANES / lon))
        n = lax.broadcasted_iota(jnp.int32, (PAD, LANES), 1).astype(f32)
        turns = order * n * (1.0 / lon)
        re, im = cos_turns(turns), minus_sin_turns(turns)
        top = (r // steps) * (2 * half) + (r % steps) * PAD
        for k in range(lon // LANES):
            cut = slice(k * LANES, (k + 1) * LANES)
            out_ref[pl.ds(pl.multiple_of(top, PAD), PAD), cut] = re.astype(bf16)
            out_ref[pl.ds(pl.multiple_of(top + half, PAD), PAD), cut] = im.astype(bf16)
            re, im = re * step_cos + im * step_sin, im * step_cos - re * step_sin

    copy = pltpu.make_async_copy(out_ref, out_hbm, sem)
    copy.start()
    copy.wait()


def legendre_kernel(
    deg_dev, index_ref, scale_ref, slots_ref, geo_ref, prod_ref, out_hbm, cur, bef, resc, start, expo, root, buf, table, sems
):
    groups = cur.shape[0]
    log_step = RESCALE_BITS * math.log(2.0)
    shrink = 2.0 ** (-RESCALE_BITS)
    limit = 2.0**RESCALE_BITS
    row = lax.broadcasted_iota(jnp.int32, (PAD, 1), 0)
    order = order_column(slots_ref[...].astype(f32), jnp.where(row < deg_dev, index_ref[0] * deg_dev + row, -1))
    order = jnp.broadcast_to(jnp.where(row < deg_dev, order, 1.0 * NO_ORDER), (PAD, LANES))
    order_sq = order * order
    for state in (cur, bef, resc, root):
        state[...] = jnp.zeros_like(state)
    picked = jnp.zeros((PAD, 1), f32)
    for g in range(prod_ref.shape[1] // LANES):
        lane = lax.broadcasted_iota(jnp.int32, (PAD, LANES), 1) + g * LANES
        hit = order == lane.astype(f32)
        term = jnp.where(hit, prod_ref[:, g * LANES : (g + 1) * LANES], 0.0)
        picked = picked + jnp.sum(term, axis=1, keepdims=True)
    head = 0.5 * jnp.log(order + 0.5) + picked
    for g in range(groups):
        log_start = head + order * geo_ref[1:2, g * LANES : (g + 1) * LANES]
        start[g] = log_start
        expo[g] = jnp.exp(log_start)
        buf[g, pl.ds(deg_dev, PAD, stride=PITCH), :] = jnp.zeros((PAD, LANES), f32)

    def block(index):
        first = index * deg_dev
        now = [cur[g] for g in range(groups)]
        old = [bef[g] for g in range(groups)]
        factor = [expo[g] for g in range(groups)]
        cosine = [geo_ref[0:1, g * LANES : (g + 1) * LANES] for g in range(groups)]
        root_prev = root[...]
        for i in range(deg_dev):
            degree = first + i
            deg = degree.astype(f32)
            gap = deg * deg - order_sq
            gap_one = jnp.maximum(gap, 1.0)
            inv = lax.rsqrt(gap_one)
            inv = inv * (1.5 - 0.5 * gap_one * inv * inv)
            alpha = inv * scale_ref[0, degree]
            beta = root_prev * scale_ref[1, degree]
            root_prev = jnp.maximum(gap, 0.0) * inv
            begin = jnp.where(order == deg, 1.0, 0.0)
            for g in range(groups):
                new = alpha * (cosine[g] * now[g] - beta * old[g]) + begin
                old[g], now[g] = now[g], new
                buf[g, pl.ds(i, PAD, stride=PITCH), :] = new * factor[g]
            if i in (deg_dev // 2, deg_dev - 1):
                for g in range(groups):
                    large = jnp.abs(now[g]) > limit
                    ratio = jnp.where(large, shrink, 1.0)
                    now[g] = now[g] * ratio
                    old[g] = old[g] * ratio
                    count = resc[g] + jnp.where(large, 1.0, 0.0)
                    resc[g] = count
                    factor[g] = jnp.exp(start[g] + count * log_step)
        root[...] = root_prev
        for g in range(groups):
            cur[g] = now[g]
            bef[g] = old[g]
            expo[g] = factor[g]
            for m in range(PAD):
                tile = buf[g, m * PITCH : m * PITCH + PAD, :].astype(bf16)
                table[m, index, :, g * LANES : (g + 1) * LANES] = tile

    parts = sems.shape[0]
    count = table.shape[1] // parts
    copies = []
    for part in range(parts):
        pl.loop(part * count, (part + 1) * count)(block)
        cut = slice(part * count, (part + 1) * count)
        copies.append(pltpu.make_async_copy(table.at[:, cut], out_hbm.at[:, cut], sems.at[part]))
        copies[-1].start()
    for copy in copies:
        copy.wait()


def degree_parity(shape, dim, ord_dev):
    i = lax.broadcasted_iota(jnp.int32, shape, dim)
    return ((i // PAD) * ord_dev + i % PAD) & 1


def order_of(slots_ref, index_ref, ord_dev, m):
    return slots_ref[index_ref[0] * ord_dev + jnp.minimum(m, ord_dev - 1)]


def fetch_pairs(table_hbm, table, sems):
    def copy(p):
        cut = pl.ds(2 * p, 2)
        return pltpu.make_async_copy(table_hbm.at[cut], table.at[cut], sems.at[p])

    for p in range(PAIRS):
        copy(p).start()
    return copy


def analysis_kernel(ord_dev, index_ref, slots_ref, rows_ref, table_hbm, out_ref, table, sems):
    copy = fetch_pairs(table_hbm, table, sems)
    count = rows_ref.shape[0]
    parity = degree_parity((table.shape[1], LANES), 0, ord_dev)

    @pl.loop(0, PAIRS)
    def _(p):
        north = jnp.concatenate([rows_ref[s, p] for s in range(count // 2)], axis=0)
        south = jnp.concatenate([rows_ref[count - 1 - s, p] for s in range(count // 2)], axis=0)
        both = jnp.concatenate([north, south], axis=1)
        copy(p).wait()
        parts = []
        for m2 in range(2):
            order = order_of(slots_ref, index_ref, ord_dev, 2 * p + m2)
            prod = jnp.dot(table[2 * p + m2], both, preferred_element_type=f32)
            mirror = prod[:, LANES:]
            parts.append(prod[:, :LANES] + jnp.where(parity == (order & 1), mirror, -mirror))
        lane = lax.broadcasted_iota(jnp.int32, parts[0].shape, 1)
        out = jnp.where(lane < LANES // 2, parts[0], parts[1]).astype(bf16)
        for d in range(count):
            out_ref[d, p] = out[d * PAD : (d + 1) * PAD]


def mix_kernel(blocks, ch_count, deg_dev, coef_ref, weight_hbm, out_ref, wide, mixed, weight, sems):
    jump = ch_count * PAD + 1
    ch_dev = LANES // 4
    channels = ch_count * ch_dev
    contract = (((1,), (1,)), ((), ()))

    def copy(degree):
        return pltpu.make_async_copy(weight_hbm.at[:, :, degree], weight.at[degree], sems.at[degree])

    for degree in range(deg_dev):
        copy(degree).start()
    for d in range(blocks):
        part = coef_ref[d * ch_count : (d + 1) * ch_count].reshape(jump - 1, LANES)
        wide[d * jump : (d + 1) * jump - 1, :] = part.astype(f32)
    for e in range(ch_count):
        mixed[pl.ds((e + 1) * PAD - 1, blocks, stride=jump), :] = jnp.zeros((blocks, LANES), f32)

    def one_degree(degree):
        groups = []
        for h in range(ch_count // 4):
            quads = [wide[pl.ds((4 * h + e) * PAD + degree, blocks, stride=jump), :] for e in range(4)]
            groups.append(chunk_transpose(quads))
        left = jnp.concatenate(
            [jnp.concatenate([g[q] for g in groups], axis=1) for q in range(4)], axis=0
        ).astype(bf16)
        prod = [
            lax.dot_general(
                left,
                weight[degree, :, w].reshape(channels, channels),
                contract,
                preferred_element_type=f32,
            )
            for w in range(2)
        ]

        def take(w, q):
            return prod[w][q * blocks : (q + 1) * blocks]

        results = []
        for m2 in range(2):
            results.append(take(0, 2 * m2) - take(1, 2 * m2 + 1))
            results.append(take(1, 2 * m2) + take(0, 2 * m2 + 1))
        for h in range(ch_count // 4):
            quads = chunk_transpose([r[:, h * LANES : (h + 1) * LANES] for r in results])
            for e in range(4):
                mixed[pl.ds((4 * h + e) * PAD + degree, blocks, stride=jump), :] = quads[e]

    group = MIX_GROUP

    @pl.loop(0, deg_dev // group)
    def _(step):
        for i in range(group):
            copy(step * group + i).wait()
        for i in range(group):
            one_degree(step * group + i)

    for d in range(blocks):
        part = mixed[d * jump : (d + 1) * jump - 1, :].astype(bf16)
        out_ref[d * ch_count : (d + 1) * ch_count] = part.reshape(ch_count, PAD, LANES)


def synthesis_kernel(ord_dev, lon, index_ref, slots_ref, mixed_ref, table_hbm, out_ref, table, sems):
    copy = fetch_pairs(table_hbm, table, sems)
    count = out_ref.shape[0]
    half = LANES // 2
    parity = degree_parity((half, table.shape[1]), 1, ord_dev)

    @pl.loop(0, PAIRS)
    def _(p):
        side = jnp.concatenate([mixed_ref[d, p] for d in range(count)], axis=0).astype(f32).T
        copy(p).wait()
        north, south = [], []
        for m2 in range(2):
            order = order_of(slots_ref, index_ref, ord_dev, 2 * p + m2)
            weight = jnp.where(order == 0, 1.0 / lon, 2.0 / lon)
            part = side[m2 * half : (m2 + 1) * half]
            same = parity == (order & 1)
            split = jnp.concatenate([jnp.where(same, part, 0.0), jnp.where(same, 0.0, part)], axis=0)
            prod = jnp.dot(split.astype(bf16), table[2 * p + m2], preferred_element_type=f32)
            north.append((prod[:half] + prod[half:]) * weight)
            south.append((prod[:half] - prod[half:]) * weight)
        up = jnp.concatenate(north, axis=0).T.astype(bf16)
        down = jnp.concatenate(south, axis=0).T.astype(bf16)
        for s in range(count // 2):
            out_ref[s, p] = up[s * PAD : (s + 1) * PAD]
            out_ref[count - 1 - s, p] = down[s * PAD : (s + 1) * PAD]


def spectrum_kernel(ord_dev, mixed_ref, pick_ref, out_ref):
    count = mixed_ref.shape[0]
    half = LANES // 2
    shape = out_ref.shape[1:]

    @pl.loop(0, PAIRS)
    def _(p):
        rows = jnp.concatenate([mixed_ref[d, p] for d in range(count)], axis=0)
        side = rows.astype(f32).T.astype(bf16)
        spec = jnp.dot(side, pick_ref[...], preferred_element_type=f32).astype(bf16)
        out_ref[2 * p] = spec[:half].reshape(shape)

        @pl.when(2 * p + 1 < ord_dev)
        def _():
            out_ref[2 * p + 1] = spec[half:].reshape(shape)


def backward_kernel(
    lat_dev, lat_count, index_ref, rows_ref, table_hbm, field_hbm, out_ref, wide, left, table_ref, field_ref, sems
):
    copies = [
        pltpu.make_async_copy(table_hbm, table_ref, sems.at[0]),
        pltpu.make_async_copy(field_hbm, field_ref, sems.at[1]),
    ]
    for copy in copies:
        copy.start()
    half = rows_ref.shape[0] * rows_ref.shape[1]
    ch_dev = LANES // 4
    for i in range(half):
        wide[i * PITCH : i * PITCH + PAD, :] = rows_ref[i // PAIRS, i % PAIRS].astype(f32)
    for j in range(lat_dev):
        slot = slot_of(j, lat_dev, index_ref[0], lat_count)
        block = wide[pl.ds(slot, half, stride=PITCH), :].T.astype(bf16)
        for q in range(4):
            left[j * ch_dev : (j + 1) * ch_dev, q * half : (q + 1) * half] = block[
                q * ch_dev : (q + 1) * ch_dev
            ]
    lon = out_ref.shape[2]
    for copy in copies:
        copy.wait()
    for b in range(4):
        cut = slice(b * lon // 4, (b + 1) * lon // 4)
        wave = jnp.dot(left[...], table_ref[:, cut], preferred_element_type=f32)
        cubic = wave * wave * wave
        grown = 0.5 * wave * (1.0 + jnp.tanh(math.sqrt(2.0 / math.pi) * (wave + 0.044715 * cubic)))
        field = field_ref[:, :, cut].astype(f32)
        out_ref[:, :, cut] = (field + grown.reshape(field.shape)).astype(bf16)


def params(mib=VMEM_MIB):
    return pltpu.CompilerParams(vmem_limit_bytes=int(mib * 2**20))


def cost(flops, moved):
    return pl.CostEstimate(flops=int(flops), bytes_accessed=int(moved), transcendentals=0)


MIX_GROUP = 3
vmem = pl.BlockSpec(memory_space=pltpu.VMEM)
smem = pl.BlockSpec(memory_space=pltpu.SMEM)
hbm = pl.BlockSpec(memory_space=pltpu.HBM)


def buffer_of(lat_count):
    return jax.ShapeDtypeStruct((lat_count, PAIRS, PAD, LANES), bf16)


def call_forward(lat_count, index, slots, field_in):
    lat_dev, ch_dev, lon = field_in.shape
    half = lat_count * PAIRS
    return pl.pallas_call(
        functools.partial(forward_kernel, lat_dev, lat_count, slots.shape[1] // lat_count),
        out_shape=buffer_of(lat_count),
        in_specs=[smem, vmem, hbm],
        out_specs=hbm,
        scratch_shapes=[
            pltpu.VMEM((lon, 4 * half), bf16),
            pltpu.VMEM(field_in.shape, bf16),
            pltpu.VMEM((lat_dev, 4, ch_dev, half), f32),
            pltpu.VMEM((half * PITCH, LANES), f32),
            pltpu.VMEM((lat_count, PAIRS, PAD, LANES), bf16),
            pltpu.SemaphoreType.DMA,
            pltpu.SemaphoreType.DMA((4,)),
        ],
        compiler_params=params(TABLE_MIB),
        name="forward",
    )(index, slots, field_in)


def call_legendre(lat_count, lat_dev, index, slots):
    lat_total = lat_count * lat_dev
    modes = slots.shape[1]
    ord_dev = modes // lat_count
    full = lat_count * PAD
    near = full // 2
    angle = math.pi * (np.arange(lat_total) + 0.5) / lat_total
    geo = np.zeros((2, lat_count, PAD), np.float32)
    geo[0, :, :lat_dev] = np.cos(angle).reshape(lat_count, lat_dev)
    geo[1, :, :lat_dev] = np.log(np.sin(angle)).reshape(lat_count, lat_dev)
    geo = geo.reshape(2, full)[:, :near]
    k = np.arange(1, modes)
    prod = np.zeros((1, full), np.float32)
    prod[0, 1:modes] = np.cumsum(0.5 * np.log((2.0 * k - 1.0) / (2.0 * k)))
    deg = np.arange(modes, dtype=np.float64)
    scale = np.sqrt(np.maximum(4.0 * deg * deg - 1.0, 1.0))
    scales = np.ones((2, modes), np.float32)
    scales[0] = scale
    scales[1, 1:] = 1.0 / scale[:-1]
    groups = near // LANES
    parts = 4
    state = pltpu.VMEM((groups, PAD, LANES), f32)
    table = pl.pallas_call(
        functools.partial(legendre_kernel, ord_dev),
        out_shape=jax.ShapeDtypeStruct((PAD, lat_count, PAD, near), bf16),
        in_specs=[smem, smem, vmem, vmem, vmem],
        out_specs=hbm,
        scratch_shapes=[state] * 5
        + [
            pltpu.VMEM((PAD, LANES), f32),
            pltpu.VMEM((groups, PAD * PITCH, LANES), f32),
            pltpu.VMEM((PAD, lat_count, PAD, near), bf16),
            pltpu.SemaphoreType.DMA((parts,)),
        ],
        compiler_params=params(TABLE_MIB),
        cost_estimate=cost(8e9, 2e7),
        name="legendre",
    )(index, jnp.asarray(scales), slots, jnp.asarray(geo), jnp.asarray(prod))
    return table.reshape(PAD, full, near)


def call_inverse_table(lat_count, lon, slots):
    half = lat_count * PAIRS
    return pl.pallas_call(
        functools.partial(inverse_table_kernel, slots.shape[1] // lat_count, lat_count),
        out_shape=jax.ShapeDtypeStruct((4 * half, lon), bf16),
        in_specs=[vmem],
        out_specs=hbm,
        scratch_shapes=[
            pltpu.VMEM((4 * half, lon), bf16),
            pltpu.VMEM((2 * half, LANES), f32),
            pltpu.SemaphoreType.DMA,
        ],
        compiler_params=params(TABLE_MIB),
        cost_estimate=cost(2e9, 4e6),
        name="inverse_table",
    )(slots)


def call_analysis(ord_dev, index, orders, rows, table):
    return pl.pallas_call(
        functools.partial(analysis_kernel, ord_dev),
        out_shape=jax.ShapeDtypeStruct(rows.shape, bf16),
        in_specs=[smem, smem, vmem, hbm],
        out_specs=vmem,
        scratch_shapes=[pltpu.VMEM(table.shape, bf16), pltpu.SemaphoreType.DMA((PAIRS,))],
        compiler_params=params(),
        name="analysis",
    )(index, orders, rows, table)


def call_mix(lat_count, coeffs, weights):
    ch_count, _, ord_dev, ch_dev, channels = weights.shape
    return pl.pallas_call(
        functools.partial(mix_kernel, lat_count, ch_count, ord_dev),
        out_shape=jax.ShapeDtypeStruct(coeffs.shape, bf16),
        in_specs=[vmem, hbm],
        out_specs=vmem,
        scratch_shapes=[pltpu.VMEM((lat_count * (ch_count * PAD + 1), LANES), f32)] * 2
        + [
            pltpu.VMEM((ord_dev, ch_count, 2, ch_dev, channels), bf16),
            pltpu.SemaphoreType.DMA((ord_dev,)),
        ],
        compiler_params=params(),
        name="mix",
    )(coeffs, weights)


def call_synthesis(ord_dev, lon, index, orders, mixed, table):
    return pl.pallas_call(
        functools.partial(synthesis_kernel, ord_dev, lon),
        out_shape=buffer_of(mixed.shape[0]),
        in_specs=[smem, smem, vmem, hbm],
        out_specs=vmem,
        scratch_shapes=[pltpu.VMEM(table.shape, bf16), pltpu.SemaphoreType.DMA((PAIRS,))],
        compiler_params=params(),
        name="synthesis",
    )(index, orders, mixed, table)


def call_spectrum(ord_dev, mixed):
    lat_count = mixed.shape[0]
    modes = ord_dev * lat_count
    pick = np.zeros((lat_count, PAD, modes), np.float32)
    pick[:, :ord_dev] = np.eye(modes, dtype=np.float32).reshape(lat_count, ord_dev, modes)
    pick = jnp.asarray(pick.reshape(lat_count * PAD, modes), bf16)
    return pl.pallas_call(
        functools.partial(spectrum_kernel, ord_dev),
        out_shape=jax.ShapeDtypeStruct((ord_dev, 2, LANES // 4, modes), bf16),
        in_specs=[vmem, vmem],
        out_specs=vmem,
        compiler_params=params(),
        cost_estimate=cost(3e9, 4e6),
        name="spectrum",
    )(mixed, pick)


def call_backward(index, rows, table, field_in):
    lat_dev, ch_dev, _ = field_in.shape
    lat_count = rows.shape[0]
    half = lat_count * PAIRS
    return pl.pallas_call(
        functools.partial(backward_kernel, lat_dev, lat_count),
        out_shape=jax.ShapeDtypeStruct(field_in.shape, bf16),
        in_specs=[smem, vmem, hbm, hbm],
        out_specs=vmem,
        scratch_shapes=[
            pltpu.VMEM((half * PITCH, LANES), f32),
            pltpu.VMEM((lat_dev * ch_dev, 4 * half), bf16),
            pltpu.VMEM(table.shape, bf16),
            pltpu.VMEM(field_in.shape, bf16),
            pltpu.SemaphoreType.DMA((2,)),
        ],
        compiler_params=params(),
        name="backward",
    )(index, rows, table, field_in)


def on_device(field_in, mix_weight, order_slots):
    lat_dev, _, lon = field_in.shape
    lat_count = lax.axis_size("lat")
    modes = order_slots.shape[0]
    ord_dev = modes // lat_count
    index = lax.axis_index("lat")
    index = index.reshape(1)
    slots = order_slots.reshape(1, modes)

    weights = lax.all_gather(jnp.transpose(mix_weight, (0, 3, 2, 1)), "ch", axis=0)
    rows = call_forward(lat_count, index, slots, field_in)
    rows = lax.all_to_all(rows, "lat", 0, 0, tiled=True)
    legendre = call_legendre(lat_count, lat_dev, index, slots)
    coeffs = call_analysis(ord_dev, index, order_slots, rows, legendre)
    coeffs = lax.all_to_all(coeffs.reshape(-1, PAD, LANES), ("lat", "ch"), 0, 0, tiled=True)
    mixed = call_mix(lat_count, coeffs, weights)
    mixed = lax.all_to_all(mixed, ("lat", "ch"), 0, 0, tiled=True).reshape(rows.shape)
    synth = call_synthesis(ord_dev, lon, index, order_slots, mixed, legendre)
    synth = lax.all_to_all(synth, "lat", 0, 0, tiled=True)
    spectrum = call_spectrum(ord_dev, mixed)
    inverse_table = call_inverse_table(lat_count, lon, slots)
    field_out = call_backward(index, synth, inverse_table, field_in)
    return (field_out, spectrum)


def solution(mesh):
    placed = (P("lat", "ch", None), P(None, None, "ch", "lat"), P())
    return jax.shard_map(
        on_device,
        mesh=mesh,
        in_specs=placed,
        out_specs=(P("lat", "ch", None), P("lat", None, "ch", None)),
        check_vma=False,
    )
```

```python
import functools
import math

import jax
import jax.numpy as jnp
import numpy as np
from jax import lax
from jax.experimental import pallas as pl
from jax.experimental.pallas import tpu as pltpu
from jax.sharding import PartitionSpec as P

PAD = 16
PAIRS = 8
LANES = 128
NO_ORDER = 1000
PITCH = 17
RESCALE_BITS = 60
f32 = jnp.float32
bf16 = jnp.bfloat16


VMEM_MIB = 50
TABLE_MIB = 57


def cos_turns(turns):
    part = turns - jnp.floor(turns + 0.5)
    y = part * math.pi
    z = y * y
    s = 1.0 / 362880 - z * (1.0 / 39916800)
    s = -1.0 / 5040 + z * s
    s = 1.0 / 120 + z * s
    s = -1.0 / 6 + z * s
    s = y * (1.0 + z * s)
    return 1.0 - 2.0 * s * s


def minus_sin_turns(turns):
    return cos_turns(turns + 0.25)


def chunk_transpose(rows):
    lane = lax.broadcasted_iota(jnp.int32, rows[0].shape, 1)
    low = lane < 64
    even = (lane // 32) % 2 == 0
    mid = [None] * 4
    for i in range(2):
        a, b = rows[i], rows[i + 2]
        mid[i] = jnp.where(low, a, pltpu.roll(b, 64, 1))
        mid[i + 2] = jnp.where(low, pltpu.roll(a, 64, 1), b)
    out = []
    for i in (0, 2):
        a, b = mid[i], mid[i + 1]
        out.append(jnp.where(even, a, pltpu.roll(b, 32, 1)))
        out.append(jnp.where(even, pltpu.roll(a, 96, 1), b))
    return out


def digits_of(slots_ref):
    slots = slots_ref[...].astype(f32)
    high = jnp.floor(slots * (1.0 / PAD))
    return high.astype(bf16), (slots - PAD * high).astype(bf16)


def one_hot(hit):
    return jnp.where(hit, 1.0, 0.0).astype(bf16)


def slot_wanted(place, ord_dev, half):
    within = 2 * (place % PAIRS) + place // half
    return jnp.where(within < ord_dev, (place % half) // PAIRS * ord_dev + within, -1)


def order_lanes(slots_ref, ord_dev, lat_count):
    modes = slots_ref.shape[1]
    half = lat_count * PAIRS
    wanted = slot_wanted(lax.broadcasted_iota(jnp.int32, (1, 2 * half), 1), ord_dev, half)
    pick = one_hot(lax.broadcasted_iota(jnp.int32, (modes, 2 * half), 0) == wanted)
    digits = [jnp.broadcast_to(d.astype(f32), (8, modes)).astype(bf16) for d in digits_of(slots_ref)]
    high, low = [jnp.dot(d, pick, preferred_element_type=f32) for d in digits]
    return high[0:1] * PAD + low[0:1]


def order_rows(slots_ref, ord_dev, lat_count):
    modes = slots_ref.shape[1]
    half = lat_count * PAIRS
    wanted = slot_wanted(lax.broadcasted_iota(jnp.int32, (2 * half, 1), 0), ord_dev, half)
    pick = one_hot(lax.broadcasted_iota(jnp.int32, (2 * half, modes), 1) == wanted)
    contract = (((1,), (1,)), ((), ()))
    high, low = [
        lax.dot_general(
            pick,
            jnp.broadcast_to(d.astype(f32), (LANES, modes)).astype(bf16),
            contract,
            preferred_element_type=f32,
        )
        for d in digits_of(slots_ref)
    ]
    return high * PAD + low


def order_column(slots, wanted):
    place = lax.broadcasted_iota(jnp.int32, (wanted.shape[0], slots.shape[1]), 1)
    return jnp.sum(jnp.where(place == wanted, slots, 0.0), axis=1, keepdims=True)


def slot_of(j, lat_dev, index, lat_count):
    return jnp.where(index < lat_count // 2, j, lat_dev - 1 - j)


def forward_kernel(
    lat_dev, lat_count, ord_dev, index_ref, slots_ref, field_hbm, out_hbm, table, field_ref, rows, turned, out_ref, sem, sems
):
    fetch = pltpu.make_async_copy(field_hbm, field_ref, sem)
    fetch.start()
    lon = table.shape[0]
    half = table.shape[1] // 4
    order = order_lanes(slots_ref, ord_dev, lat_count)
    step_cos = cos_turns(order * (LANES / lon))
    step_sin = -minus_sin_turns(order * (LANES / lon))

    @pl.loop(0, LANES // PAD)
    def _(r):
        n = (lax.broadcasted_iota(jnp.int32, (PAD, order.shape[1]), 0) + r * PAD).astype(f32)
        turns = order * n * (1.0 / lon)
        re, im = cos_turns(turns), minus_sin_turns(turns)
        for k in range(lon // LANES):
            at = pl.ds(pl.multiple_of(k * LANES + r * PAD, PAD), PAD)
            for m2 in range(2):
                cut = slice(m2 * half, (m2 + 1) * half)
                table[at, 2 * m2 * half : (2 * m2 + 1) * half] = re[:, cut].astype(bf16)
                table[at, (2 * m2 + 1) * half : (2 * m2 + 2) * half] = im[:, cut].astype(bf16)
            re, im = re * step_cos + im * step_sin, im * step_cos - re * step_sin

    fetch.wait()
    ch_dev = field_ref.shape[1]
    field = field_ref[...].reshape(lat_dev * ch_dev, lon)
    for q in range(4):
        part = jnp.dot(field, table[:, q * half : (q + 1) * half], preferred_element_type=f32)
        rows[:, q] = part.reshape(lat_dev, ch_dev, half)
    index = index_ref[0]
    lat_total = lat_dev * lat_count
    for j in range(lat_dev):
        place = jnp.full((1, half), index * lat_dev + j, jnp.int32).astype(f32)
        quad = cos_turns((place + 0.5) * (0.5 / lat_total) - 0.25) * (math.pi / lat_total)
        block = rows[j].reshape(4 * ch_dev, half) * quad
        turned[pl.ds(slot_of(j, lat_dev, index, lat_count), half, stride=PITCH), :] = block.T
    turned[pl.ds(lat_dev, half, stride=PITCH), :] = jnp.zeros((half, LANES), f32)
    copies = []
    part = lat_count // sems.shape[0]
    for d in range(lat_count):
        for p in range(PAIRS):
            i = d * PAIRS + p
            out_ref[d, p] = turned[i * PITCH : i * PITCH + PAD, :].astype(bf16)
        if d % part == part - 1:
            cut = slice(d + 1 - part, d + 1)
            copies.append(pltpu.make_async_copy(out_ref.at[cut], out_hbm.at[cut], sems.at[d // part]))
            copies[-1].start()
    for copy in copies:
        copy.wait()


def inverse_table_kernel(ord_dev, lat_count, slots_ref, out_hbm, out_ref, orders, sem):
    lon = out_ref.shape[1]
    half = out_ref.shape[0] // 4
    steps = half // PAD
    orders[...] = order_rows(slots_ref, ord_dev, lat_count)

    @pl.loop(0, 2 * steps)
    def _(r):
        order = orders[pl.ds(pl.multiple_of(r * PAD, PAD), PAD), :]
        step_cos = cos_turns(order * (LANES / lon))
        step_sin = -minus_sin_turns(order * (LANES / lon))
        n = lax.broadcasted_iota(jnp.int32, (PAD, LANES), 1).astype(f32)
        turns = order * n * (1.0 / lon)
        re, im = cos_turns(turns), minus_sin_turns(turns)
        top = (r // steps) * (2 * half) + (r % steps) * PAD
        for k in range(lon // LANES):
            cut = slice(k * LANES, (k + 1) * LANES)
            out_ref[pl.ds(pl.multiple_of(top, PAD), PAD), cut] = re.astype(bf16)
            out_ref[pl.ds(pl.multiple_of(top + half, PAD), PAD), cut] = im.astype(bf16)
            re, im = re * step_cos + im * step_sin, im * step_cos - re * step_sin

    copy = pltpu.make_async_copy(out_ref, out_hbm, sem)
    copy.start()
    copy.wait()


def legendre_kernel(
    deg_dev, index_ref, scale_ref, slots_ref, geo_ref, prod_ref, out_hbm, cur, bef, resc, start, expo, root, buf, table, sems
):
    groups = cur.shape[0]
    pitch = 2 * PAD + 1
    log_step = RESCALE_BITS * math.log(2.0)
    shrink = 2.0 ** (-RESCALE_BITS)
    limit = 2.0**RESCALE_BITS
    row = lax.broadcasted_iota(jnp.int32, (PAD, 1), 0)
    order = order_column(slots_ref[...].astype(f32), jnp.where(row < deg_dev, index_ref[0] * deg_dev + row, -1))
    order = jnp.broadcast_to(jnp.where(row < deg_dev, order, 1.0 * NO_ORDER), (PAD, LANES))
    order_sq = order * order
    for state in (cur, bef, resc, root):
        state[...] = jnp.zeros_like(state)
    picked = jnp.zeros((PAD, 1), f32)
    for g in range(prod_ref.shape[1] // LANES):
        lane = lax.broadcasted_iota(jnp.int32, (PAD, LANES), 1) + g * LANES
        hit = order == lane.astype(f32)
        term = jnp.where(hit, prod_ref[:, g * LANES : (g + 1) * LANES], 0.0)
        picked = picked + jnp.sum(term, axis=1, keepdims=True)
    head = 0.5 * jnp.log(order + 0.5) + picked
    for g in range(groups):
        log_start = head + order * geo_ref[1:2, g * LANES : (g + 1) * LANES]
        start[g] = log_start
        expo[g] = jnp.exp(log_start)
        for twin in range(2):
            buf[g, pl.ds(PAD + twin * PAIRS + PAIRS - 1, PAD, stride=pitch), :] = jnp.zeros((PAD, LANES), f32)

    def block(index):
        now = [cur[g] for g in range(groups)]
        old = [bef[g] for g in range(groups)]
        factor = [expo[g] for g in range(groups)]
        cosine = [geo_ref[0:1, g * LANES : (g + 1) * LANES] for g in range(groups)]
        root_prev = root[...]
        for twin, i in [(t, k) for t in range(2) for k in range(deg_dev)]:
            degree = (2 * index + twin) * deg_dev + i
            deg = degree.astype(f32)
            gap = deg * deg - order_sq
            gap_one = jnp.maximum(gap, 1.0)
            inv = lax.rsqrt(gap_one)
            inv = inv * (1.5 - 0.5 * gap_one * inv * inv)
            alpha = inv * scale_ref[0, degree]
            beta = root_prev * scale_ref[1, degree]
            root_prev = jnp.maximum(gap, 0.0) * inv
            begin = jnp.where(order == deg, 1.0, 0.0)
            for g in range(groups):
                new = alpha * (cosine[g] * now[g] - beta * old[g]) + begin
                old[g], now[g] = now[g], new
                row = i % 2 * PAD + twin * PAIRS + i // 2
                buf[g, pl.ds(row, PAD, stride=pitch), :] = new * factor[g]
            if i in (deg_dev // 2, deg_dev - 1):
                for g in range(groups):
                    large = jnp.abs(now[g]) > limit
                    ratio = jnp.where(large, shrink, 1.0)
                    now[g] = now[g] * ratio
                    old[g] = old[g] * ratio
                    count = resc[g] + jnp.where(large, 1.0, 0.0)
                    resc[g] = count
                    factor[g] = jnp.exp(start[g] + count * log_step)
        root[...] = root_prev
        for g in range(groups):
            cur[g] = now[g]
            bef[g] = old[g]
            expo[g] = factor[g]
            for m in range(PAD):
                for side in range(2):
                    row = m * pitch + side * PAD
                    tile = buf[g, row : row + PAD, :].astype(bf16)
                    table[m, side, index, :, g * LANES : (g + 1) * LANES] = tile

    parts = sems.shape[0]
    count = table.shape[2] // parts
    copies = []
    for part in range(parts):
        pl.loop(part * count, (part + 1) * count)(block)
        cut = slice(part * count, (part + 1) * count)
        copies.append(pltpu.make_async_copy(table.at[:, :, cut], out_hbm.at[:, :, cut], sems.at[part]))
        copies[-1].start()
    for copy in copies:
        copy.wait()


def degree_parity(shape, dim, deg_dev):
    half = shape[dim] // 2
    i = lax.broadcasted_iota(jnp.int32, shape, dim)
    return ((i % half) // PAIRS * deg_dev + i // half) & 1


def order_of(slots_ref, index_ref, ord_dev, m):
    return slots_ref[index_ref[0] * ord_dev + jnp.minimum(m, ord_dev - 1)]


def fetch_pairs(table_hbm, table, sems):
    def copy(p):
        cut = pl.ds(2 * p, 2)
        return pltpu.make_async_copy(table_hbm.at[cut], table.at[cut], sems.at[p])

    for p in range(PAIRS):
        copy(p).start()
    return copy


def analysis_kernel(ord_dev, index_ref, slots_ref, rows_ref, table_hbm, out_ref, table, wide, sems):
    copy = fetch_pairs(table_hbm, table, sems)
    count = rows_ref.shape[0]
    half = count * PAIRS
    parity = degree_parity((table.shape[1], LANES), 0, ord_dev)

    @pl.loop(0, PAIRS)
    def _(p):
        north = jnp.concatenate([rows_ref[s, p] for s in range(count // 2)], axis=0)
        south = jnp.concatenate([rows_ref[count - 1 - s, p] for s in range(count // 2)], axis=0)
        both = jnp.concatenate([north, south], axis=1)
        copy(p).wait()
        for m2 in range(2):
            order = order_of(slots_ref, index_ref, ord_dev, 2 * p + m2)
            prod = jnp.dot(table[2 * p + m2], both, preferred_element_type=f32)
            mirror = prod[:, LANES:]
            coefs = prod[:, :LANES] + jnp.where(parity == (order & 1), mirror, -mirror)
            low, high = coefs[:half], coefs[half:]
            if m2 == 0:
                high = pltpu.roll(high, LANES // 2, 1)
            else:
                low = pltpu.roll(low, LANES // 2, 1)
            lane = lax.broadcasted_iota(jnp.int32, low.shape, 1)
            wide[pl.ds(2 * p + m2, half, stride=PITCH), :] = jnp.where(lane < LANES // 2, low, high)

    for i in range(half):
        out_ref[i // PAIRS, i % PAIRS] = wide[i * PITCH : i * PITCH + PAD, :].astype(bf16)


def mix_kernel(coef_ref, weight_hbm, out_ref, weight, sem):
    copy = pltpu.make_async_copy(weight_hbm, weight, sem)
    copy.start()
    copy.wait()
    bands, ch_count = coef_ref.shape[:2]
    ch_dev = LANES // 4
    channels = ch_count * ch_dev
    contract = (((1,), (1,)), ((), ()))
    step = MIX_BANDS
    count = step * PAD

    @pl.loop(0, bands // step)
    def _(chunk):
        here = pl.ds(chunk * step, step)
        groups = []
        for h in range(ch_count // 4):
            quads = [coef_ref[here, 4 * h + e].reshape(count, LANES).astype(f32) for e in range(4)]
            groups.append(chunk_transpose(quads))
        results = []
        for l2 in range(2):
            left = jnp.concatenate(
                [jnp.concatenate([g[2 * l2 + x] for g in groups], axis=1) for x in range(2)], axis=0
            ).astype(bf16)
            prod = [
                lax.dot_general(
                    left,
                    weight[:, w, l2].reshape(channels, channels),
                    contract,
                    preferred_element_type=f32,
                )
                for w in range(2)
            ]
            results.append(prod[0][:count] - prod[1][count:])
            results.append(prod[1][:count] + prod[0][count:])
        for h in range(ch_count // 4):
            quads = chunk_transpose([r[:, h * LANES : (h + 1) * LANES] for r in results])
            for e in range(4):
                out_ref[here, 4 * h + e] = quads[e].astype(bf16).reshape(step, PAD, LANES)


def widen(mixed_ref, wide):
    for i in range(mixed_ref.shape[0] * PAIRS):
        wide[i * PITCH : i * PITCH + PAD, :] = mixed_ref[i // PAIRS, i % PAIRS].astype(f32)


def side_of(wide, count, m):
    turned = wide[pl.ds(m, count * PAIRS, stride=PITCH), :].T
    return jnp.concatenate([turned[: LANES // 2], turned[LANES // 2 :]], axis=1)


def synthesis_kernel(ord_dev, lon, index_ref, slots_ref, mixed_ref, table_hbm, out_ref, table, wide, sems):
    copy = fetch_pairs(table_hbm, table, sems)
    widen(mixed_ref, wide)
    count = out_ref.shape[0]
    half = LANES // 2
    parity = degree_parity((half, table.shape[1]), 1, ord_dev)

    @pl.loop(0, PAIRS)
    def _(p):
        copy(p).wait()
        north, south = [], []
        for m2 in range(2):
            order = order_of(slots_ref, index_ref, ord_dev, 2 * p + m2)
            weight = jnp.where(order == 0, 1.0 / lon, 2.0 / lon)
            part = side_of(wide, count, 2 * p + m2)
            same = parity == (order & 1)
            split = jnp.concatenate([jnp.where(same, part, 0.0), jnp.where(same, 0.0, part)], axis=0)
            prod = jnp.dot(split.astype(bf16), table[2 * p + m2], preferred_element_type=f32)
            north.append((prod[:half] + prod[half:]) * weight)
            south.append((prod[:half] - prod[half:]) * weight)
        up = jnp.concatenate(north, axis=0).T.astype(bf16)
        down = jnp.concatenate(south, axis=0).T.astype(bf16)
        for s in range(count // 2):
            out_ref[s, p] = up[s * PAD : (s + 1) * PAD]
            out_ref[count - 1 - s, p] = down[s * PAD : (s + 1) * PAD]


def spectrum_kernel(ord_dev, mixed_ref, pick_ref, out_ref, wide):
    count = mixed_ref.shape[0]
    widen(mixed_ref, wide)

    @pl.loop(0, ord_dev)
    def _(m):
        side = side_of(wide, count, m).astype(bf16)
        spec = jnp.dot(side, pick_ref[...], preferred_element_type=f32).astype(bf16)
        out_ref[m] = spec.reshape(out_ref.shape[1:])


def backward_kernel(
    lat_dev, lat_count, index_ref, rows_ref, table_hbm, field_hbm, out_ref, wide, left, table_ref, field_ref, sems
):
    copies = [
        pltpu.make_async_copy(table_hbm, table_ref, sems.at[0]),
        pltpu.make_async_copy(field_hbm, field_ref, sems.at[1]),
    ]
    for copy in copies:
        copy.start()
    half = rows_ref.shape[0] * rows_ref.shape[1]
    ch_dev = LANES // 4
    for i in range(half):
        wide[i * PITCH : i * PITCH + PAD, :] = rows_ref[i // PAIRS, i % PAIRS].astype(f32)
    for j in range(lat_dev):
        slot = slot_of(j, lat_dev, index_ref[0], lat_count)
        block = wide[pl.ds(slot, half, stride=PITCH), :].T.astype(bf16)
        for q in range(4):
            left[j * ch_dev : (j + 1) * ch_dev, q * half : (q + 1) * half] = block[
                q * ch_dev : (q + 1) * ch_dev
            ]
    lon = out_ref.shape[2]
    for copy in copies:
        copy.wait()
    for b in range(4):
        cut = slice(b * lon // 4, (b + 1) * lon // 4)
        wave = jnp.dot(left[...], table_ref[:, cut], preferred_element_type=f32)
        cubic = wave * wave * wave
        grown = 0.5 * wave * (1.0 + jnp.tanh(math.sqrt(2.0 / math.pi) * (wave + 0.044715 * cubic)))
        field = field_ref[:, :, cut].astype(f32)
        out_ref[:, :, cut] = (field + grown.reshape(field.shape)).astype(bf16)


def params(mib=VMEM_MIB):
    return pltpu.CompilerParams(vmem_limit_bytes=int(mib * 2**20))


def cost(flops, moved):
    return pl.CostEstimate(flops=int(flops), bytes_accessed=int(moved), transcendentals=0)


MIX_BANDS = 8
vmem = pl.BlockSpec(memory_space=pltpu.VMEM)
smem = pl.BlockSpec(memory_space=pltpu.SMEM)
hbm = pl.BlockSpec(memory_space=pltpu.HBM)


def buffer_of(lat_count):
    return jax.ShapeDtypeStruct((lat_count, PAIRS, PAD, LANES), bf16)


def call_forward(lat_count, index, slots, field_in):
    lat_dev, ch_dev, lon = field_in.shape
    half = lat_count * PAIRS
    return pl.pallas_call(
        functools.partial(forward_kernel, lat_dev, lat_count, slots.shape[1] // lat_count),
        out_shape=buffer_of(lat_count),
        in_specs=[smem, vmem, hbm],
        out_specs=hbm,
        scratch_shapes=[
            pltpu.VMEM((lon, 4 * half), bf16),
            pltpu.VMEM(field_in.shape, bf16),
            pltpu.VMEM((lat_dev, 4, ch_dev, half), f32),
            pltpu.VMEM((half * PITCH, LANES), f32),
            pltpu.VMEM((lat_count, PAIRS, PAD, LANES), bf16),
            pltpu.SemaphoreType.DMA,
            pltpu.SemaphoreType.DMA((4,)),
        ],
        compiler_params=params(TABLE_MIB),
        name="forward",
    )(index, slots, field_in)


def call_legendre(lat_count, lat_dev, index, slots):
    lat_total = lat_count * lat_dev
    modes = slots.shape[1]
    ord_dev = modes // lat_count
    full = lat_count * PAD
    near = full // 2
    angle = math.pi * (np.arange(lat_total) + 0.5) / lat_total
    geo = np.zeros((2, lat_count, PAD), np.float32)
    geo[0, :, :lat_dev] = np.cos(angle).reshape(lat_count, lat_dev)
    geo[1, :, :lat_dev] = np.log(np.sin(angle)).reshape(lat_count, lat_dev)
    geo = geo.reshape(2, full)[:, :near]
    k = np.arange(1, modes)
    prod = np.zeros((1, full), np.float32)
    prod[0, 1:modes] = np.cumsum(0.5 * np.log((2.0 * k - 1.0) / (2.0 * k)))
    deg = np.arange(modes, dtype=np.float64)
    scale = np.sqrt(np.maximum(4.0 * deg * deg - 1.0, 1.0))
    scales = np.ones((2, modes), np.float32)
    scales[0] = scale
    scales[1, 1:] = 1.0 / scale[:-1]
    groups = near // LANES
    parts = 4
    state = pltpu.VMEM((groups, PAD, LANES), f32)
    table = pl.pallas_call(
        functools.partial(legendre_kernel, ord_dev),
        out_shape=jax.ShapeDtypeStruct((PAD, 2, lat_count // 2, PAD, near), bf16),
        in_specs=[smem, smem, vmem, vmem, vmem],
        out_specs=hbm,
        scratch_shapes=[state] * 5
        + [
            pltpu.VMEM((PAD, LANES), f32),
            pltpu.VMEM((groups, PAD * (2 * PAD + 1), LANES), f32),
            pltpu.VMEM((PAD, 2, lat_count // 2, PAD, near), bf16),
            pltpu.SemaphoreType.DMA((parts,)),
        ],
        compiler_params=params(TABLE_MIB),
        cost_estimate=cost(8e9, 2e7),
        name="legendre",
    )(index, jnp.asarray(scales), slots, jnp.asarray(geo), jnp.asarray(prod))
    return table.reshape(PAD, full, near)


def call_inverse_table(lat_count, lon, slots):
    half = lat_count * PAIRS
    return pl.pallas_call(
        functools.partial(inverse_table_kernel, slots.shape[1] // lat_count, lat_count),
        out_shape=jax.ShapeDtypeStruct((4 * half, lon), bf16),
        in_specs=[vmem],
        out_specs=hbm,
        scratch_shapes=[
            pltpu.VMEM((4 * half, lon), bf16),
            pltpu.VMEM((2 * half, LANES), f32),
            pltpu.SemaphoreType.DMA,
        ],
        compiler_params=params(TABLE_MIB),
        cost_estimate=cost(2e9, 4e6),
        name="inverse_table",
    )(slots)


def call_analysis(ord_dev, index, orders, rows, table):
    lat_count = rows.shape[0]
    return pl.pallas_call(
        functools.partial(analysis_kernel, ord_dev),
        out_shape=jax.ShapeDtypeStruct(rows.shape, bf16),
        in_specs=[smem, smem, vmem, hbm],
        out_specs=vmem,
        scratch_shapes=[
            pltpu.VMEM(table.shape, bf16),
            pltpu.VMEM((lat_count * PAIRS * PITCH, LANES), f32),
            pltpu.SemaphoreType.DMA((PAIRS,)),
        ],
        compiler_params=params(),
        name="analysis",
    )(index, orders, rows, table)


def call_mix(coeffs, weights):
    return pl.pallas_call(
        mix_kernel,
        out_shape=jax.ShapeDtypeStruct(coeffs.shape, bf16),
        in_specs=[vmem, hbm],
        out_specs=vmem,
        scratch_shapes=[pltpu.VMEM(weights.shape, bf16), pltpu.SemaphoreType.DMA],
        compiler_params=params(),
        name="mix",
    )(coeffs, weights)


def call_synthesis(ord_dev, lon, index, orders, mixed, table):
    lat_count = mixed.shape[0]
    return pl.pallas_call(
        functools.partial(synthesis_kernel, ord_dev, lon),
        out_shape=buffer_of(mixed.shape[0]),
        in_specs=[smem, smem, vmem, hbm],
        out_specs=vmem,
        scratch_shapes=[
            pltpu.VMEM(table.shape, bf16),
            pltpu.VMEM((lat_count * PAIRS * PITCH, LANES), f32),
            pltpu.SemaphoreType.DMA((PAIRS,)),
        ],
        compiler_params=params(),
        name="synthesis",
    )(index, orders, mixed, table)


def call_spectrum(ord_dev, mixed):
    lat_count = mixed.shape[0]
    modes = ord_dev * lat_count
    pick = np.zeros((lat_count, PAD, modes), np.float32)
    pick[:, :ord_dev] = np.eye(modes, dtype=np.float32).reshape(lat_count, ord_dev, modes)
    pick = pick.reshape(lat_count * PAIRS, 2, modes).transpose(1, 0, 2)
    pick = jnp.asarray(pick.reshape(lat_count * PAD, modes), bf16)
    return pl.pallas_call(
        functools.partial(spectrum_kernel, ord_dev),
        out_shape=jax.ShapeDtypeStruct((ord_dev, 2, LANES // 4, modes), bf16),
        in_specs=[vmem, vmem],
        out_specs=vmem,
        scratch_shapes=[pltpu.VMEM((lat_count * PAIRS * PITCH, LANES), f32)],
        compiler_params=params(),
        cost_estimate=cost(3e9, 4e6),
        name="spectrum",
    )(mixed, pick)


def call_backward(index, rows, table, field_in):
    lat_dev, ch_dev, _ = field_in.shape
    lat_count = rows.shape[0]
    half = lat_count * PAIRS
    return pl.pallas_call(
        functools.partial(backward_kernel, lat_dev, lat_count),
        out_shape=jax.ShapeDtypeStruct(field_in.shape, bf16),
        in_specs=[smem, vmem, hbm, hbm],
        out_specs=vmem,
        scratch_shapes=[
            pltpu.VMEM((half * PITCH, LANES), f32),
            pltpu.VMEM((lat_dev * ch_dev, 4 * half), bf16),
            pltpu.VMEM(table.shape, bf16),
            pltpu.VMEM(field_in.shape, bf16),
            pltpu.SemaphoreType.DMA((2,)),
        ],
        compiler_params=params(),
        name="backward",
    )(index, rows, table, field_in)


def on_device(field_in, mix_weight, order_slots):
    lat_dev, _, lon = field_in.shape
    lat_count = lax.axis_size("lat")
    modes = order_slots.shape[0]
    ord_dev = modes // lat_count
    index = lax.axis_index("lat")
    index = index.reshape(1)
    slots = order_slots.reshape(1, modes)

    rows = call_forward(lat_count, index, slots, field_in)
    rows = lax.all_to_all(rows, "lat", 0, 0, tiled=True)
    legendre = call_legendre(lat_count, lat_dev, index, slots)
    weights = jnp.transpose(mix_weight, (0, 3, 2, 1))
    weights, legendre = lax.optimization_barrier((weights, legendre))
    weights = jnp.pad(weights, ((0, 0), (0, PAD - ord_dev), (0, 0), (0, 0)))
    weights = weights.reshape((2, PAIRS, 2) + weights.shape[2:]).swapaxes(0, 1)
    weights = lax.all_to_all(weights, "ch", 0, 0, tiled=True)
    coeffs = call_analysis(ord_dev, index, order_slots, rows, legendre)
    coeffs = lax.all_to_all(coeffs.reshape(-1, PAD, LANES), ("lat", "ch"), 0, 0, tiled=True)
    mixed = call_mix(coeffs.reshape(rows.shape), weights)
    mixed = lax.all_to_all(mixed.reshape(-1, PAD, LANES), ("lat", "ch"), 0, 0, tiled=True).reshape(rows.shape)
    synth = call_synthesis(ord_dev, lon, index, order_slots, mixed, legendre)
    synth = lax.all_to_all(synth, "lat", 0, 0, tiled=True)
    spectrum = call_spectrum(ord_dev, mixed)
    inverse_table = call_inverse_table(lat_count, lon, slots)
    field_out = call_backward(index, synth, inverse_table, field_in)
    return (field_out, spectrum)


def solution(mesh):
    placed = (P("lat", "ch", None), P(None, None, "ch", "lat"), P())
    return jax.shard_map(
        on_device,
        mesh=mesh,
        in_specs=placed,
        out_specs=(P("lat", "ch", None), P("lat", None, "ch", None)),
        check_vma=False,
    )
```

```python
import functools
import math

import jax
import jax.numpy as jnp
import numpy as np
from jax import lax
from jax.experimental import pallas as pl
from jax.experimental.pallas import tpu as pltpu
from jax.sharding import PartitionSpec as P

PAD = 16
PAIRS = 8
LANES = 128
NO_ORDER = 1000
PITCH = 17
RESCALE_BITS = 60
f32 = jnp.float32
bf16 = jnp.bfloat16


VMEM_MIB = 50
TABLE_MIB = 57


def cos_turns(turns):
    part = turns - jnp.floor(turns + 0.5)
    y = part * math.pi
    z = y * y
    s = 1.0 / 362880 - z * (1.0 / 39916800)
    s = -1.0 / 5040 + z * s
    s = 1.0 / 120 + z * s
    s = -1.0 / 6 + z * s
    s = y * (1.0 + z * s)
    return 1.0 - 2.0 * s * s


def minus_sin_turns(turns):
    return cos_turns(turns + 0.25)


def chunk_transpose(rows):
    lane = lax.broadcasted_iota(jnp.int32, rows[0].shape, 1)
    low = lane < 64
    even = (lane // 32) % 2 == 0
    mid = [None] * 4
    for i in range(2):
        a, b = rows[i], rows[i + 2]
        mid[i] = jnp.where(low, a, pltpu.roll(b, 64, 1))
        mid[i + 2] = jnp.where(low, pltpu.roll(a, 64, 1), b)
    out = []
    for i in (0, 2):
        a, b = mid[i], mid[i + 1]
        out.append(jnp.where(even, a, pltpu.roll(b, 32, 1)))
        out.append(jnp.where(even, pltpu.roll(a, 96, 1), b))
    return out


def digits_of(slots_ref):
    slots = slots_ref[...].astype(f32)
    high = jnp.floor(slots * (1.0 / PAD))
    return high.astype(bf16), (slots - PAD * high).astype(bf16)


def one_hot(hit):
    return jnp.where(hit, 1.0, 0.0).astype(bf16)


def slot_wanted(place, ord_dev, half):
    within = 2 * (place % PAIRS) + place // half
    return jnp.where(within < ord_dev, (place % half) // PAIRS * ord_dev + within, -1)


def order_lanes(slots_ref, ord_dev, lat_count):
    modes = slots_ref.shape[1]
    half = lat_count * PAIRS
    wanted = slot_wanted(lax.broadcasted_iota(jnp.int32, (1, 2 * half), 1), ord_dev, half)
    pick = one_hot(lax.broadcasted_iota(jnp.int32, (modes, 2 * half), 0) == wanted)
    digits = [jnp.broadcast_to(d.astype(f32), (8, modes)).astype(bf16) for d in digits_of(slots_ref)]
    high, low = [jnp.dot(d, pick, preferred_element_type=f32) for d in digits]
    return high[0:1] * PAD + low[0:1]


def order_rows(slots_ref, ord_dev, lat_count):
    modes = slots_ref.shape[1]
    half = lat_count * PAIRS
    wanted = slot_wanted(lax.broadcasted_iota(jnp.int32, (2 * half, 1), 0), ord_dev, half)
    pick = one_hot(lax.broadcasted_iota(jnp.int32, (2 * half, modes), 1) == wanted)
    contract = (((1,), (1,)), ((), ()))
    high, low = [
        lax.dot_general(
            pick,
            jnp.broadcast_to(d.astype(f32), (LANES, modes)).astype(bf16),
            contract,
            preferred_element_type=f32,
        )
        for d in digits_of(slots_ref)
    ]
    return high * PAD + low


def order_column(slots, wanted):
    place = lax.broadcasted_iota(jnp.int32, (wanted.shape[0], slots.shape[1]), 1)
    return jnp.sum(jnp.where(place == wanted, slots, 0.0), axis=1, keepdims=True)


def slot_of(j, lat_dev, index, lat_count):
    return jnp.where(index < lat_count // 2, j, lat_dev - 1 - j)


def forward_kernel(
    lat_dev, lat_count, ord_dev, index_ref, slots_ref, field_hbm, out_hbm, table, field_ref, rows, turned, out_ref, sem, sems
):
    fetch = pltpu.make_async_copy(field_hbm, field_ref, sem)
    fetch.start()
    lon = table.shape[0]
    half = table.shape[1] // 4
    order = order_lanes(slots_ref, ord_dev, lat_count)
    step_cos = cos_turns(order * (LANES / lon))
    step_sin = -minus_sin_turns(order * (LANES / lon))

    @pl.loop(0, LANES // PAD)
    def _(r):
        n = (lax.broadcasted_iota(jnp.int32, (PAD, order.shape[1]), 0) + r * PAD).astype(f32)
        turns = order * n * (1.0 / lon)
        re, im = cos_turns(turns), minus_sin_turns(turns)
        for k in range(lon // LANES):
            at = pl.ds(pl.multiple_of(k * LANES + r * PAD, PAD), PAD)
            for m2 in range(2):
                cut = slice(m2 * half, (m2 + 1) * half)
                table[at, 2 * m2 * half : (2 * m2 + 1) * half] = re[:, cut].astype(bf16)
                table[at, (2 * m2 + 1) * half : (2 * m2 + 2) * half] = im[:, cut].astype(bf16)
            re, im = re * step_cos + im * step_sin, im * step_cos - re * step_sin

    fetch.wait()
    ch_dev = field_ref.shape[1]
    field = field_ref[...].reshape(lat_dev * ch_dev, lon)
    for q in range(4):
        part = jnp.dot(field, table[:, q * half : (q + 1) * half], preferred_element_type=f32)
        rows[:, q] = part.reshape(lat_dev, ch_dev, half)
    index = index_ref[0]
    lat_total = lat_dev * lat_count
    for j in range(lat_dev):
        place = jnp.full((1, half), index * lat_dev + j, jnp.int32).astype(f32)
        quad = cos_turns((place + 0.5) * (0.5 / lat_total) - 0.25) * (math.pi / lat_total)
        block = rows[j].reshape(4 * ch_dev, half) * quad
        turned[pl.ds(slot_of(j, lat_dev, index, lat_count), half, stride=PITCH), :] = block.T
    turned[pl.ds(lat_dev, half, stride=PITCH), :] = jnp.zeros((half, LANES), f32)
    copies = []
    part = lat_count // sems.shape[0]
    for d in range(lat_count):
        for p in range(PAIRS):
            i = d * PAIRS + p
            out_ref[d, p] = turned[i * PITCH : i * PITCH + PAD, :].astype(bf16)
        if d % part == part - 1:
            cut = slice(d + 1 - part, d + 1)
            copies.append(pltpu.make_async_copy(out_ref.at[cut], out_hbm.at[cut], sems.at[d // part]))
            copies[-1].start()
    for copy in copies:
        copy.wait()


def inverse_table_kernel(ord_dev, lat_count, slots_ref, out_hbm, out_ref, orders, sem):
    lon = out_ref.shape[1]
    half = out_ref.shape[0] // 4
    steps = half // PAD
    orders[...] = order_rows(slots_ref, ord_dev, lat_count)

    @pl.loop(0, 2 * steps)
    def _(r):
        order = orders[pl.ds(pl.multiple_of(r * PAD, PAD), PAD), :]
        step_cos = cos_turns(order * (LANES / lon))
        step_sin = -minus_sin_turns(order * (LANES / lon))
        n = lax.broadcasted_iota(jnp.int32, (PAD, LANES), 1).astype(f32)
        turns = order * n * (1.0 / lon)
        re, im = cos_turns(turns), minus_sin_turns(turns)
        top = (r // steps) * (2 * half) + (r % steps) * PAD
        for k in range(lon // LANES):
            cut = slice(k * LANES, (k + 1) * LANES)
            out_ref[pl.ds(pl.multiple_of(top, PAD), PAD), cut] = re.astype(bf16)
            out_ref[pl.ds(pl.multiple_of(top + half, PAD), PAD), cut] = im.astype(bf16)
            re, im = re * step_cos + im * step_sin, im * step_cos - re * step_sin

    copy = pltpu.make_async_copy(out_ref, out_hbm, sem)
    copy.start()
    copy.wait()


def legendre_kernel(
    deg_dev, index_ref, scale_ref, slots_ref, geo_ref, prod_ref, out_hbm, cur, bef, resc, start, expo, root, buf, table, sems
):
    groups = cur.shape[0]
    pitch = 2 * PAD + 1
    log_step = RESCALE_BITS * math.log(2.0)
    shrink = 2.0 ** (-RESCALE_BITS)
    limit = 2.0**RESCALE_BITS
    row = lax.broadcasted_iota(jnp.int32, (PAD, 1), 0)
    order = order_column(slots_ref[...].astype(f32), jnp.where(row < deg_dev, index_ref[0] * deg_dev + row, -1))
    order = jnp.broadcast_to(jnp.where(row < deg_dev, order, 1.0 * NO_ORDER), (PAD, LANES))
    order_sq = order * order
    for state in (cur, bef, resc, root):
        state[...] = jnp.zeros_like(state)
    picked = jnp.zeros((PAD, 1), f32)
    for g in range(prod_ref.shape[1] // LANES):
        lane = lax.broadcasted_iota(jnp.int32, (PAD, LANES), 1) + g * LANES
        hit = order == lane.astype(f32)
        term = jnp.where(hit, prod_ref[:, g * LANES : (g + 1) * LANES], 0.0)
        picked = picked + jnp.sum(term, axis=1, keepdims=True)
    head = 0.5 * jnp.log(order + 0.5) + picked
    for g in range(groups):
        log_start = head + order * geo_ref[1:2, g * LANES : (g + 1) * LANES]
        start[g] = log_start
        expo[g] = jnp.exp(log_start)
        for twin in range(2):
            buf[g, pl.ds(PAD + twin * PAIRS + PAIRS - 1, PAD, stride=pitch), :] = jnp.zeros((PAD, LANES), f32)

    def block(index):
        now = [cur[g] for g in range(groups)]
        old = [bef[g] for g in range(groups)]
        factor = [expo[g] for g in range(groups)]
        cosine = [geo_ref[0:1, g * LANES : (g + 1) * LANES] for g in range(groups)]
        root_prev = root[...]
        for twin, i in [(t, k) for t in range(2) for k in range(deg_dev)]:
            degree = (2 * index + twin) * deg_dev + i
            deg = degree.astype(f32)
            gap = deg * deg - order_sq
            gap_one = jnp.maximum(gap, 1.0)
            inv = lax.rsqrt(gap_one)
            inv = inv * (1.5 - 0.5 * gap_one * inv * inv)
            alpha = inv * scale_ref[0, degree]
            beta = root_prev * scale_ref[1, degree]
            root_prev = jnp.maximum(gap, 0.0) * inv
            begin = jnp.where(order == deg, 1.0, 0.0)
            for g in range(groups):
                new = alpha * (cosine[g] * now[g] - beta * old[g]) + begin
                old[g], now[g] = now[g], new
                row = i % 2 * PAD + twin * PAIRS + i // 2
                buf[g, pl.ds(row, PAD, stride=pitch), :] = new * factor[g]
            if i in (deg_dev // 2, deg_dev - 1):
                for g in range(groups):
                    large = jnp.abs(now[g]) > limit
                    ratio = jnp.where(large, shrink, 1.0)
                    now[g] = now[g] * ratio
                    old[g] = old[g] * ratio
                    count = resc[g] + jnp.where(large, 1.0, 0.0)
                    resc[g] = count
                    factor[g] = jnp.exp(start[g] + count * log_step)
        root[...] = root_prev
        for g in range(groups):
            cur[g] = now[g]
            bef[g] = old[g]
            expo[g] = factor[g]
            for m in range(PAD):
                for side in range(2):
                    row = m * pitch + side * PAD
                    tile = buf[g, row : row + PAD, :].astype(bf16)
                    table[m, side, index, :, g * LANES : (g + 1) * LANES] = tile

    parts = sems.shape[0]
    count = table.shape[2] // parts
    copies = []
    for part in range(parts):
        pl.loop(part * count, (part + 1) * count)(block)
        cut = slice(part * count, (part + 1) * count)
        copies.append(pltpu.make_async_copy(table.at[:, :, cut], out_hbm.at[:, :, cut], sems.at[part]))
        copies[-1].start()
    for copy in copies:
        copy.wait()


def degree_parity(shape, dim, deg_dev):
    half = shape[dim] // 2
    i = lax.broadcasted_iota(jnp.int32, shape, dim)
    return ((i % half) // PAIRS * deg_dev + i // half) & 1


def order_of(slots_ref, index_ref, ord_dev, m):
    return slots_ref[index_ref[0] * ord_dev + jnp.minimum(m, ord_dev - 1)]


def fetch_pairs(table_hbm, table, sems):
    def copy(p):
        cut = pl.ds(2 * p, 2)
        return pltpu.make_async_copy(table_hbm.at[cut], table.at[cut], sems.at[p])

    for p in range(PAIRS):
        copy(p).start()
    return copy


def analysis_kernel(ord_dev, index_ref, slots_ref, rows_ref, table_hbm, out_ref, table, wide, sems):
    copy = fetch_pairs(table_hbm, table, sems)
    count = rows_ref.shape[0]
    half = count * PAIRS
    parity = degree_parity((table.shape[1], LANES), 0, ord_dev)

    @pl.loop(0, PAIRS)
    def _(p):
        north = jnp.concatenate([rows_ref[s, p] for s in range(count // 2)], axis=0)
        south = jnp.concatenate([rows_ref[count - 1 - s, p] for s in range(count // 2)], axis=0)
        both = jnp.concatenate([north, south], axis=1)
        copy(p).wait()
        for m2 in range(2):
            order = order_of(slots_ref, index_ref, ord_dev, 2 * p + m2)
            prod = jnp.dot(table[2 * p + m2], both, preferred_element_type=f32)
            mirror = prod[:, LANES:]
            coefs = prod[:, :LANES] + jnp.where(parity == (order & 1), mirror, -mirror)
            low, high = coefs[:half], coefs[half:]
            if m2 == 0:
                high = pltpu.roll(high, LANES // 2, 1)
            else:
                low = pltpu.roll(low, LANES // 2, 1)
            lane = lax.broadcasted_iota(jnp.int32, low.shape, 1)
            wide[pl.ds(2 * p + m2, half, stride=PITCH), :] = jnp.where(lane < LANES // 2, low, high)

    for i in range(half):
        out_ref[i // PAIRS, i % PAIRS] = wide[i * PITCH : i * PITCH + PAD, :].astype(bf16)


def weights_kernel(index_ref, weight_ref, *out_refs):
    ch_count = len(out_refs)
    last = weight_ref.shape[1] - 1
    for k, out_ref in enumerate(out_refs):
        there = lax.rem(index_ref[0] + k, ch_count)
        for w in range(2):
            for l2 in range(2):
                out_ref[w, l2] = weight_ref[w, jnp.minimum(2 * there + l2, last)]


def mix_kernel(index_ref, coef_ref, *refs):
    ch_count = len(refs) - 3
    out_ref, weight, sems = refs[ch_count:]
    copies = []
    for k in range(ch_count):
        source = lax.rem(index_ref[0] + ch_count - k, ch_count)
        copies.append(pltpu.make_async_copy(refs[k], weight.at[source], sems.at[k]))
        copies[-1].start()
    for copy in copies:
        copy.wait()
    bands = coef_ref.shape[0]
    ch_dev = LANES // 4
    channels = ch_count * ch_dev
    contract = (((1,), (1,)), ((), ()))
    step = MIX_BANDS
    count = step * PAD

    @pl.loop(0, bands // step)
    def _(chunk):
        here = pl.ds(chunk * step, step)
        groups = []
        for h in range(ch_count // 4):
            quads = [coef_ref[here, 4 * h + e].reshape(count, LANES).astype(f32) for e in range(4)]
            groups.append(chunk_transpose(quads))
        results = []
        for l2 in range(2):
            left = jnp.concatenate(
                [jnp.concatenate([g[2 * l2 + x] for g in groups], axis=1) for x in range(2)], axis=0
            ).astype(bf16)
            prod = [
                lax.dot_general(
                    left,
                    weight[:, w, l2].reshape(channels, channels),
                    contract,
                    preferred_element_type=f32,
                )
                for w in range(2)
            ]
            results.append(prod[0][:count] - prod[1][count:])
            results.append(prod[1][:count] + prod[0][count:])
        for h in range(ch_count // 4):
            quads = chunk_transpose([r[:, h * LANES : (h + 1) * LANES] for r in results])
            for e in range(4):
                out_ref[here, 4 * h + e] = quads[e].astype(bf16).reshape(step, PAD, LANES)


def widen(mixed_ref, wide):
    for i in range(mixed_ref.shape[0] * PAIRS):
        wide[i * PITCH : i * PITCH + PAD, :] = mixed_ref[i // PAIRS, i % PAIRS].astype(f32)


def side_of(wide, count, m):
    turned = wide[pl.ds(m, count * PAIRS, stride=PITCH), :].T
    return jnp.concatenate([turned[: LANES // 2], turned[LANES // 2 :]], axis=1)


def synthesis_kernel(ord_dev, lon, index_ref, slots_ref, mixed_ref, table_hbm, out_ref, table, wide, sems):
    copy = fetch_pairs(table_hbm, table, sems)
    widen(mixed_ref, wide)
    count = out_ref.shape[0]
    half = LANES // 2
    parity = degree_parity((half, table.shape[1]), 1, ord_dev)

    @pl.loop(0, PAIRS)
    def _(p):
        copy(p).wait()
        north, south = [], []
        for m2 in range(2):
            order = order_of(slots_ref, index_ref, ord_dev, 2 * p + m2)
            weight = jnp.where(order == 0, 1.0 / lon, 2.0 / lon)
            part = side_of(wide, count, 2 * p + m2)
            same = parity == (order & 1)
            split = jnp.concatenate([jnp.where(same, part, 0.0), jnp.where(same, 0.0, part)], axis=0)
            prod = jnp.dot(split.astype(bf16), table[2 * p + m2], preferred_element_type=f32)
            north.append((prod[:half] + prod[half:]) * weight)
            south.append((prod[:half] - prod[half:]) * weight)
        up = jnp.concatenate(north, axis=0).T.astype(bf16)
        down = jnp.concatenate(south, axis=0).T.astype(bf16)
        for s in range(count // 2):
            out_ref[s, p] = up[s * PAD : (s + 1) * PAD]
            out_ref[count - 1 - s, p] = down[s * PAD : (s + 1) * PAD]


def spectrum_kernel(ord_dev, mixed_ref, pick_ref, out_ref, wide):
    count = mixed_ref.shape[0]
    widen(mixed_ref, wide)

    @pl.loop(0, ord_dev)
    def _(m):
        side = side_of(wide, count, m).astype(bf16)
        spec = jnp.dot(side, pick_ref[...], preferred_element_type=f32).astype(bf16)
        out_ref[m] = spec.reshape(out_ref.shape[1:])


def backward_kernel(
    lat_dev, lat_count, index_ref, rows_ref, table_hbm, field_hbm, out_ref, wide, left, table_ref, field_ref, sems
):
    copies = [
        pltpu.make_async_copy(table_hbm, table_ref, sems.at[0]),
        pltpu.make_async_copy(field_hbm, field_ref, sems.at[1]),
    ]
    for copy in copies:
        copy.start()
    half = rows_ref.shape[0] * rows_ref.shape[1]
    ch_dev = LANES // 4
    for i in range(half):
        wide[i * PITCH : i * PITCH + PAD, :] = rows_ref[i // PAIRS, i % PAIRS].astype(f32)
    for j in range(lat_dev):
        slot = slot_of(j, lat_dev, index_ref[0], lat_count)
        block = wide[pl.ds(slot, half, stride=PITCH), :].T.astype(bf16)
        for q in range(4):
            left[j * ch_dev : (j + 1) * ch_dev, q * half : (q + 1) * half] = block[
                q * ch_dev : (q + 1) * ch_dev
            ]
    lon = out_ref.shape[2]
    for copy in copies:
        copy.wait()
    for b in range(4):
        cut = slice(b * lon // 4, (b + 1) * lon // 4)
        wave = jnp.dot(left[...], table_ref[:, cut], preferred_element_type=f32)
        cubic = wave * wave * wave
        grown = 0.5 * wave * (1.0 + jnp.tanh(math.sqrt(2.0 / math.pi) * (wave + 0.044715 * cubic)))
        field = field_ref[:, :, cut].astype(f32)
        out_ref[:, :, cut] = (field + grown.reshape(field.shape)).astype(bf16)


def params(mib=VMEM_MIB):
    return pltpu.CompilerParams(vmem_limit_bytes=int(mib * 2**20))


def cost(flops, moved):
    return pl.CostEstimate(flops=int(flops), bytes_accessed=int(moved), transcendentals=0)


MIX_BANDS = 8
vmem = pl.BlockSpec(memory_space=pltpu.VMEM)
smem = pl.BlockSpec(memory_space=pltpu.SMEM)
hbm = pl.BlockSpec(memory_space=pltpu.HBM)


def buffer_of(lat_count):
    return jax.ShapeDtypeStruct((lat_count, PAIRS, PAD, LANES), bf16)


def call_forward(lat_count, index, slots, field_in):
    lat_dev, ch_dev, lon = field_in.shape
    half = lat_count * PAIRS
    return pl.pallas_call(
        functools.partial(forward_kernel, lat_dev, lat_count, slots.shape[1] // lat_count),
        out_shape=buffer_of(lat_count),
        in_specs=[smem, vmem, hbm],
        out_specs=hbm,
        scratch_shapes=[
            pltpu.VMEM((lon, 4 * half), bf16),
            pltpu.VMEM(field_in.shape, bf16),
            pltpu.VMEM((lat_dev, 4, ch_dev, half), f32),
            pltpu.VMEM((half * PITCH, LANES), f32),
            pltpu.VMEM((lat_count, PAIRS, PAD, LANES), bf16),
            pltpu.SemaphoreType.DMA,
            pltpu.SemaphoreType.DMA((4,)),
        ],
        compiler_params=params(TABLE_MIB),
        name="forward",
    )(index, slots, field_in)


def call_legendre(lat_count, lat_dev, index, slots):
    lat_total = lat_count * lat_dev
    modes = slots.shape[1]
    ord_dev = modes // lat_count
    full = lat_count * PAD
    near = full // 2
    angle = math.pi * (np.arange(lat_total) + 0.5) / lat_total
    geo = np.zeros((2, lat_count, PAD), np.float32)
    geo[0, :, :lat_dev] = np.cos(angle).reshape(lat_count, lat_dev)
    geo[1, :, :lat_dev] = np.log(np.sin(angle)).reshape(lat_count, lat_dev)
    geo = geo.reshape(2, full)[:, :near]
    k = np.arange(1, modes)
    prod = np.zeros((1, full), np.float32)
    prod[0, 1:modes] = np.cumsum(0.5 * np.log((2.0 * k - 1.0) / (2.0 * k)))
    deg = np.arange(modes, dtype=np.float64)
    scale = np.sqrt(np.maximum(4.0 * deg * deg - 1.0, 1.0))
    scales = np.ones((2, modes), np.float32)
    scales[0] = scale
    scales[1, 1:] = 1.0 / scale[:-1]
    groups = near // LANES
    parts = 4
    state = pltpu.VMEM((groups, PAD, LANES), f32)
    table = pl.pallas_call(
        functools.partial(legendre_kernel, ord_dev),
        out_shape=jax.ShapeDtypeStruct((PAD, 2, lat_count // 2, PAD, near), bf16),
        in_specs=[smem, smem, vmem, vmem, vmem],
        out_specs=hbm,
        scratch_shapes=[state] * 5
        + [
            pltpu.VMEM((PAD, LANES), f32),
            pltpu.VMEM((groups, PAD * (2 * PAD + 1), LANES), f32),
            pltpu.VMEM((PAD, 2, lat_count // 2, PAD, near), bf16),
            pltpu.SemaphoreType.DMA((parts,)),
        ],
        compiler_params=params(TABLE_MIB),
        cost_estimate=cost(8e9, 2e7),
        name="legendre",
    )(index, jnp.asarray(scales), slots, jnp.asarray(geo), jnp.asarray(prod))
    return table.reshape(PAD, full, near)


def call_inverse_table(lat_count, lon, slots):
    half = lat_count * PAIRS
    return pl.pallas_call(
        functools.partial(inverse_table_kernel, slots.shape[1] // lat_count, lat_count),
        out_shape=jax.ShapeDtypeStruct((4 * half, lon), bf16),
        in_specs=[vmem],
        out_specs=hbm,
        scratch_shapes=[
            pltpu.VMEM((4 * half, lon), bf16),
            pltpu.VMEM((2 * half, LANES), f32),
            pltpu.SemaphoreType.DMA,
        ],
        compiler_params=params(TABLE_MIB),
        cost_estimate=cost(2e9, 4e6),
        name="inverse_table",
    )(slots)


def call_analysis(ord_dev, index, orders, rows, table):
    lat_count = rows.shape[0]
    return pl.pallas_call(
        functools.partial(analysis_kernel, ord_dev),
        out_shape=jax.ShapeDtypeStruct(rows.shape, bf16),
        in_specs=[smem, smem, vmem, hbm],
        out_specs=vmem,
        scratch_shapes=[
            pltpu.VMEM(table.shape, bf16),
            pltpu.VMEM((lat_count * PAIRS * PITCH, LANES), f32),
            pltpu.SemaphoreType.DMA((PAIRS,)),
        ],
        compiler_params=params(),
        name="analysis",
    )(index, orders, rows, table)


def exchange_weights(index, weights):
    ch_count = lax.axis_size("ch")
    piece = jax.ShapeDtypeStruct((2, 2) + weights.shape[2:], bf16)
    pieces = pl.pallas_call(
        weights_kernel,
        out_shape=(piece,) * ch_count,
        in_specs=[smem, vmem],
        out_specs=(vmem,) * ch_count,
        compiler_params=params(),
        name="weights",
    )(index, weights)
    moved = [pieces[0]]
    for k in range(1, ch_count):
        ring = [(e, (e + k) % ch_count) for e in range(ch_count)]
        moved.append(lax.ppermute(pieces[k], "ch", ring))
    return moved


def call_mix(index, coeffs, weights):
    ch_count = len(weights)
    return pl.pallas_call(
        mix_kernel,
        out_shape=jax.ShapeDtypeStruct(coeffs.shape, bf16),
        in_specs=[smem, vmem] + [hbm] * ch_count,
        out_specs=vmem,
        scratch_shapes=[
            pltpu.VMEM((ch_count,) + weights[0].shape, bf16),
            pltpu.SemaphoreType.DMA((ch_count,)),
        ],
        compiler_params=params(),
        name="mix",
    )(index, coeffs, *weights)


def call_synthesis(ord_dev, lon, index, orders, mixed, table):
    lat_count = mixed.shape[0]
    return pl.pallas_call(
        functools.partial(synthesis_kernel, ord_dev, lon),
        out_shape=buffer_of(mixed.shape[0]),
        in_specs=[smem, smem, vmem, hbm],
        out_specs=vmem,
        scratch_shapes=[
            pltpu.VMEM(table.shape, bf16),
            pltpu.VMEM((lat_count * PAIRS * PITCH, LANES), f32),
            pltpu.SemaphoreType.DMA((PAIRS,)),
        ],
        compiler_params=params(),
        name="synthesis",
    )(index, orders, mixed, table)


def call_spectrum(ord_dev, mixed):
    lat_count = mixed.shape[0]
    modes = ord_dev * lat_count
    pick = np.zeros((lat_count, PAD, modes), np.float32)
    pick[:, :ord_dev] = np.eye(modes, dtype=np.float32).reshape(lat_count, ord_dev, modes)
    pick = pick.reshape(lat_count * PAIRS, 2, modes).transpose(1, 0, 2)
    pick = jnp.asarray(pick.reshape(lat_count * PAD, modes), bf16)
    return pl.pallas_call(
        functools.partial(spectrum_kernel, ord_dev),
        out_shape=jax.ShapeDtypeStruct((ord_dev, 2, LANES // 4, modes), bf16),
        in_specs=[vmem, vmem],
        out_specs=vmem,
        scratch_shapes=[pltpu.VMEM((lat_count * PAIRS * PITCH, LANES), f32)],
        compiler_params=params(),
        cost_estimate=cost(3e9, 4e6),
        name="spectrum",
    )(mixed, pick)


def call_backward(index, rows, table, field_in):
    lat_dev, ch_dev, _ = field_in.shape
    lat_count = rows.shape[0]
    half = lat_count * PAIRS
    return pl.pallas_call(
        functools.partial(backward_kernel, lat_dev, lat_count),
        out_shape=jax.ShapeDtypeStruct(field_in.shape, bf16),
        in_specs=[smem, vmem, hbm, hbm],
        out_specs=vmem,
        scratch_shapes=[
            pltpu.VMEM((half * PITCH, LANES), f32),
            pltpu.VMEM((lat_dev * ch_dev, 4 * half), bf16),
            pltpu.VMEM(table.shape, bf16),
            pltpu.VMEM(field_in.shape, bf16),
            pltpu.SemaphoreType.DMA((2,)),
        ],
        compiler_params=params(),
        name="backward",
    )(index, rows, table, field_in)


def on_device(field_in, mix_weight, order_slots):
    lat_dev, _, lon = field_in.shape
    lat_count = lax.axis_size("lat")
    modes = order_slots.shape[0]
    ord_dev = modes // lat_count
    index = lax.axis_index("lat")
    index = index.reshape(1)
    slots = order_slots.reshape(1, modes)

    rows = call_forward(lat_count, index, slots, field_in)
    rows = lax.all_to_all(rows, "lat", 0, 0, tiled=True)
    legendre = call_legendre(lat_count, lat_dev, index, slots)
    weights = jnp.transpose(mix_weight, (0, 3, 2, 1))
    weights, legendre = lax.optimization_barrier((weights, legendre))
    ch_index = lax.axis_index("ch").reshape(1)
    weights = exchange_weights(ch_index, weights)
    coeffs = call_analysis(ord_dev, index, order_slots, rows, legendre)
    coeffs, weights = lax.optimization_barrier((coeffs, weights))
    coeffs = lax.all_to_all(coeffs.reshape(-1, PAD, LANES), ("lat", "ch"), 0, 0, tiled=True)
    mixed = call_mix(ch_index, coeffs.reshape(rows.shape), weights)
    mixed = lax.all_to_all(mixed.reshape(-1, PAD, LANES), ("lat", "ch"), 0, 0, tiled=True).reshape(rows.shape)
    synth = call_synthesis(ord_dev, lon, index, order_slots, mixed, legendre)
    synth = lax.all_to_all(synth, "lat", 0, 0, tiled=True)
    spectrum = call_spectrum(ord_dev, mixed)
    inverse_table = call_inverse_table(lat_count, lon, slots)
    field_out = call_backward(index, synth, inverse_table, field_in)
    return (field_out, spectrum)


def solution(mesh):
    placed = (P("lat", "ch", None), P(None, None, "ch", "lat"), P())
    return jax.shard_map(
        on_device,
        mesh=mesh,
        in_specs=placed,
        out_specs=(P("lat", "ch", None), P("lat", None, "ch", None)),
        check_vma=False,
    )
```

```python
import functools
import math

import jax
import jax.numpy as jnp
import numpy as np
from jax import lax
from jax.experimental import pallas as pl
from jax.experimental.pallas import tpu as pltpu
from jax.sharding import PartitionSpec as P

PAD = 16
PAIRS = 8
LANES = 128
NO_ORDER = 1000
PITCH = 17
RESCALE_BITS = 60
f32 = jnp.float32
bf16 = jnp.bfloat16


VMEM_MIB = 50
TABLE_MIB = 57


def cos_turns(turns):
    part = turns - jnp.floor(turns + 0.5)
    y = part * math.pi
    z = y * y
    s = 1.0 / 362880 - z * (1.0 / 39916800)
    s = -1.0 / 5040 + z * s
    s = 1.0 / 120 + z * s
    s = -1.0 / 6 + z * s
    s = y * (1.0 + z * s)
    return 1.0 - 2.0 * s * s


def minus_sin_turns(turns):
    return cos_turns(turns + 0.25)


def chunk_transpose(rows):
    lane = lax.broadcasted_iota(jnp.int32, rows[0].shape, 1)
    low = lane < 64
    even = (lane // 32) % 2 == 0
    mid = [None] * 4
    for i in range(2):
        a, b = rows[i], rows[i + 2]
        mid[i] = jnp.where(low, a, pltpu.roll(b, 64, 1))
        mid[i + 2] = jnp.where(low, pltpu.roll(a, 64, 1), b)
    out = []
    for i in (0, 2):
        a, b = mid[i], mid[i + 1]
        out.append(jnp.where(even, a, pltpu.roll(b, 32, 1)))
        out.append(jnp.where(even, pltpu.roll(a, 96, 1), b))
    return out


def digits_of(slots_ref):
    slots = slots_ref[...].astype(f32)
    high = jnp.floor(slots * (1.0 / PAD))
    return high.astype(bf16), (slots - PAD * high).astype(bf16)


def one_hot(hit):
    return jnp.where(hit, 1.0, 0.0).astype(bf16)


def slot_wanted(place, ord_dev, half):
    within = 2 * (place % PAIRS) + place // half
    return jnp.where(within < ord_dev, (place % half) // PAIRS * ord_dev + within, -1)


def order_lanes(slots_ref, ord_dev, lat_count):
    modes = slots_ref.shape[1]
    half = lat_count * PAIRS
    wanted = slot_wanted(lax.broadcasted_iota(jnp.int32, (1, 2 * half), 1), ord_dev, half)
    pick = one_hot(lax.broadcasted_iota(jnp.int32, (modes, 2 * half), 0) == wanted)
    digits = [jnp.broadcast_to(d.astype(f32), (8, modes)).astype(bf16) for d in digits_of(slots_ref)]
    high, low = [jnp.dot(d, pick, preferred_element_type=f32) for d in digits]
    return high[0:1] * PAD + low[0:1]


def order_rows(slots_ref, ord_dev, lat_count):
    modes = slots_ref.shape[1]
    half = lat_count * PAIRS
    wanted = slot_wanted(lax.broadcasted_iota(jnp.int32, (2 * half, 1), 0), ord_dev, half)
    pick = one_hot(lax.broadcasted_iota(jnp.int32, (2 * half, modes), 1) == wanted)
    contract = (((1,), (1,)), ((), ()))
    high, low = [
        lax.dot_general(
            pick,
            jnp.broadcast_to(d.astype(f32), (LANES, modes)).astype(bf16),
            contract,
            preferred_element_type=f32,
        )
        for d in digits_of(slots_ref)
    ]
    return high * PAD + low


def order_column(slots, wanted):
    place = lax.broadcasted_iota(jnp.int32, (wanted.shape[0], slots.shape[1]), 1)
    return jnp.sum(jnp.where(place == wanted, slots, 0.0), axis=1, keepdims=True)


def slot_of(j, lat_dev, index, lat_count):
    return jnp.where(index < lat_count // 2, j, lat_dev - 1 - j)


def forward_kernel(
    lat_dev, lat_count, ord_dev, index_ref, slots_ref, field_hbm, out_hbm, table, field_ref, rows, turned, out_ref, sem, sems
):
    fetch = pltpu.make_async_copy(field_hbm, field_ref, sem)
    fetch.start()
    lon = table.shape[0]
    half = table.shape[1] // 4
    order = order_lanes(slots_ref, ord_dev, lat_count)
    step_cos = cos_turns(order * (LANES / lon))
    step_sin = -minus_sin_turns(order * (LANES / lon))

    @pl.loop(0, LANES // PAD)
    def _(r):
        n = (lax.broadcasted_iota(jnp.int32, (PAD, order.shape[1]), 0) + r * PAD).astype(f32)
        turns = order * n * (1.0 / lon)
        re, im = cos_turns(turns), minus_sin_turns(turns)
        for k in range(lon // LANES):
            at = pl.ds(pl.multiple_of(k * LANES + r * PAD, PAD), PAD)
            for m2 in range(2):
                cut = slice(m2 * half, (m2 + 1) * half)
                table[at, 2 * m2 * half : (2 * m2 + 1) * half] = re[:, cut].astype(bf16)
                table[at, (2 * m2 + 1) * half : (2 * m2 + 2) * half] = im[:, cut].astype(bf16)
            re, im = re * step_cos + im * step_sin, im * step_cos - re * step_sin

    fetch.wait()
    ch_dev = field_ref.shape[1]
    field = field_ref[...].reshape(lat_dev * ch_dev, lon)
    for q in range(4):
        part = jnp.dot(field, table[:, q * half : (q + 1) * half], preferred_element_type=f32)
        rows[:, q] = part.reshape(lat_dev, ch_dev, half)
    index = index_ref[0]
    lat_total = lat_dev * lat_count
    for j in range(lat_dev):
        place = jnp.full((1, half), index * lat_dev + j, jnp.int32).astype(f32)
        quad = cos_turns((place + 0.5) * (0.5 / lat_total) - 0.25) * (math.pi / lat_total)
        block = rows[j].reshape(4 * ch_dev, half) * quad
        turned[pl.ds(slot_of(j, lat_dev, index, lat_count), half, stride=PITCH), :] = block.T
    turned[pl.ds(lat_dev, half, stride=PITCH), :] = jnp.zeros((half, LANES), f32)
    copies = []
    part = lat_count // sems.shape[0]
    for d in range(lat_count):
        for p in range(PAIRS):
            i = d * PAIRS + p
            out_ref[d, p] = turned[i * PITCH : i * PITCH + PAD, :].astype(bf16)
        if d % part == part - 1:
            cut = slice(d + 1 - part, d + 1)
            copies.append(pltpu.make_async_copy(out_ref.at[cut], out_hbm.at[cut], sems.at[d // part]))
            copies[-1].start()
    for copy in copies:
        copy.wait()


def inverse_table_kernel(ord_dev, lat_count, slots_ref, out_hbm, out_ref, orders, sem):
    lon = out_ref.shape[1]
    half = out_ref.shape[0] // 4
    steps = half // PAD
    orders[...] = order_rows(slots_ref, ord_dev, lat_count)

    @pl.loop(0, 2 * steps)
    def _(r):
        order = orders[pl.ds(pl.multiple_of(r * PAD, PAD), PAD), :]
        step_cos = cos_turns(order * (LANES / lon))
        step_sin = -minus_sin_turns(order * (LANES / lon))
        n = lax.broadcasted_iota(jnp.int32, (PAD, LANES), 1).astype(f32)
        turns = order * n * (1.0 / lon)
        re, im = cos_turns(turns), minus_sin_turns(turns)
        top = (r // steps) * (2 * half) + (r % steps) * PAD
        for k in range(lon // LANES):
            cut = slice(k * LANES, (k + 1) * LANES)
            out_ref[pl.ds(pl.multiple_of(top, PAD), PAD), cut] = re.astype(bf16)
            out_ref[pl.ds(pl.multiple_of(top + half, PAD), PAD), cut] = im.astype(bf16)
            re, im = re * step_cos + im * step_sin, im * step_cos - re * step_sin

    copy = pltpu.make_async_copy(out_ref, out_hbm, sem)
    copy.start()
    copy.wait()


def legendre_kernel(
    deg_dev, index_ref, scale_ref, slots_ref, geo_ref, prod_ref, out_hbm, cur, bef, resc, start, expo, root, buf, table, sems
):
    groups = cur.shape[0]
    pitch = 2 * PAD + 1
    log_step = RESCALE_BITS * math.log(2.0)
    shrink = 2.0 ** (-RESCALE_BITS)
    limit = 2.0**RESCALE_BITS
    row = lax.broadcasted_iota(jnp.int32, (PAD, 1), 0)
    order = order_column(slots_ref[...].astype(f32), jnp.where(row < deg_dev, index_ref[0] * deg_dev + row, -1))
    order = jnp.broadcast_to(jnp.where(row < deg_dev, order, 1.0 * NO_ORDER), (PAD, LANES))
    order_sq = order * order
    for state in (cur, bef, resc, root):
        state[...] = jnp.zeros_like(state)
    picked = jnp.zeros((PAD, 1), f32)
    for g in range(prod_ref.shape[1] // LANES):
        lane = lax.broadcasted_iota(jnp.int32, (PAD, LANES), 1) + g * LANES
        hit = order == lane.astype(f32)
        term = jnp.where(hit, prod_ref[:, g * LANES : (g + 1) * LANES], 0.0)
        picked = picked + jnp.sum(term, axis=1, keepdims=True)
    head = 0.5 * jnp.log(order + 0.5) + picked
    for g in range(groups):
        log_start = head + order * geo_ref[1:2, g * LANES : (g + 1) * LANES]
        start[g] = log_start
        expo[g] = jnp.exp(log_start)
        for twin in range(2):
            buf[g, pl.ds(PAD + twin * PAIRS + PAIRS - 1, PAD, stride=pitch), :] = jnp.zeros((PAD, LANES), f32)

    def block(index):
        now = [cur[g] for g in range(groups)]
        old = [bef[g] for g in range(groups)]
        factor = [expo[g] for g in range(groups)]
        cosine = [geo_ref[0:1, g * LANES : (g + 1) * LANES] for g in range(groups)]
        root_prev = root[...]
        for twin, i in [(t, k) for t in range(2) for k in range(deg_dev)]:
            degree = (2 * index + twin) * deg_dev + i
            deg = degree.astype(f32)
            gap = deg * deg - order_sq
            gap_one = jnp.maximum(gap, 1.0)
            inv = lax.rsqrt(gap_one)
            inv = inv * (1.5 - 0.5 * gap_one * inv * inv)
            alpha = inv * scale_ref[0, degree]
            beta = root_prev * scale_ref[1, degree]
            root_prev = jnp.maximum(gap, 0.0) * inv
            begin = jnp.where(order == deg, 1.0, 0.0)
            for g in range(groups):
                new = alpha * (cosine[g] * now[g] - beta * old[g]) + begin
                old[g], now[g] = now[g], new
                row = i % 2 * PAD + twin * PAIRS + i // 2
                buf[g, pl.ds(row, PAD, stride=pitch), :] = new * factor[g]
            if i in (deg_dev // 2, deg_dev - 1):
                for g in range(groups):
                    large = jnp.abs(now[g]) > limit
                    ratio = jnp.where(large, shrink, 1.0)
                    now[g] = now[g] * ratio
                    old[g] = old[g] * ratio
                    count = resc[g] + jnp.where(large, 1.0, 0.0)
                    resc[g] = count
                    factor[g] = jnp.exp(start[g] + count * log_step)
        root[...] = root_prev
        for g in range(groups):
            cur[g] = now[g]
            bef[g] = old[g]
            expo[g] = factor[g]
            for m in range(PAD):
                for side in range(2):
                    row = m * pitch + side * PAD
                    tile = buf[g, row : row + PAD, :].astype(bf16)
                    table[m, side, index, :, g * LANES : (g + 1) * LANES] = tile

    parts = sems.shape[0]
    count = table.shape[2] // parts
    copies = []
    for part in range(parts):
        pl.loop(part * count, (part + 1) * count)(block)
        cut = slice(part * count, (part + 1) * count)
        copies.append(pltpu.make_async_copy(table.at[:, :, cut], out_hbm.at[:, :, cut], sems.at[part]))
        copies[-1].start()
    for copy in copies:
        copy.wait()


def degree_parity(shape, dim, deg_dev):
    half = shape[dim] // 2
    i = lax.broadcasted_iota(jnp.int32, shape, dim)
    return ((i % half) // PAIRS * deg_dev + i // half) & 1


def order_of(slots_ref, index_ref, ord_dev, m):
    return slots_ref[index_ref[0] * ord_dev + jnp.minimum(m, ord_dev - 1)]


def fetch_pairs(table_hbm, table, sems):
    def copy(p):
        cut = pl.ds(2 * p, 2)
        return pltpu.make_async_copy(table_hbm.at[cut], table.at[cut], sems.at[p])

    for p in range(PAIRS):
        copy(p).start()
    return copy


def analysis_kernel(ord_dev, index_ref, slots_ref, rows_ref, table_hbm, out_ref, table, wide, sems):
    copy = fetch_pairs(table_hbm, table, sems)
    count = rows_ref.shape[0]
    half = count * PAIRS
    parity = degree_parity((table.shape[1], LANES), 0, ord_dev)

    @pl.loop(0, PAIRS)
    def _(p):
        north = jnp.concatenate([rows_ref[s, p] for s in range(count // 2)], axis=0)
        south = jnp.concatenate([rows_ref[count - 1 - s, p] for s in range(count // 2)], axis=0)
        both = jnp.concatenate([north, south], axis=1)
        copy(p).wait()
        for m2 in range(2):
            order = order_of(slots_ref, index_ref, ord_dev, 2 * p + m2)
            prod = jnp.dot(table[2 * p + m2], both, preferred_element_type=f32)
            mirror = prod[:, LANES:]
            coefs = prod[:, :LANES] + jnp.where(parity == (order & 1), mirror, -mirror)
            low, high = coefs[:half], coefs[half:]
            if m2 == 0:
                high = pltpu.roll(high, LANES // 2, 1)
            else:
                low = pltpu.roll(low, LANES // 2, 1)
            lane = lax.broadcasted_iota(jnp.int32, low.shape, 1)
            wide[pl.ds(2 * p + m2, half, stride=PITCH), :] = jnp.where(lane < LANES // 2, low, high)

    for i in range(half):
        out_ref[i // PAIRS, i % PAIRS] = wide[i * PITCH : i * PITCH + PAD, :].astype(bf16)


def weights_kernel(index_ref, weight_ref, *out_refs):
    ch_count = len(out_refs)
    last = weight_ref.shape[1] - 1
    for k, out_ref in enumerate(out_refs):
        there = lax.rem(index_ref[0] + k, ch_count)
        for w in range(2):
            for l2 in range(2):
                out_ref[w, l2] = weight_ref[w, jnp.minimum(2 * there + l2, last)]


def mix_kernel(index_ref, coef_ref, *refs):
    ch_count = len(refs) - 3
    out_ref, weight, sems = refs[ch_count:]
    copies = []
    for k in range(ch_count):
        source = lax.rem(index_ref[0] + ch_count - k, ch_count)
        copies.append(pltpu.make_async_copy(refs[k], weight.at[source], sems.at[k]))
        copies[-1].start()
    for copy in copies:
        copy.wait()
    bands = coef_ref.shape[0]
    ch_dev = LANES // 4
    channels = ch_count * ch_dev
    contract = (((1,), (1,)), ((), ()))
    step = MIX_BANDS
    count = step * PAD

    @pl.loop(0, bands // step)
    def _(chunk):
        here = pl.ds(chunk * step, step)
        groups = []
        for h in range(ch_count // 4):
            quads = [coef_ref[here, 4 * h + e].reshape(count, LANES).astype(f32) for e in range(4)]
            groups.append(chunk_transpose(quads))
        results = []
        for l2 in range(2):
            left = jnp.concatenate(
                [jnp.concatenate([g[2 * l2 + x] for g in groups], axis=1) for x in range(2)], axis=0
            ).astype(bf16)
            prod = [
                lax.dot_general(
                    left,
                    weight[:, w, l2].reshape(channels, channels),
                    contract,
                    preferred_element_type=f32,
                )
                for w in range(2)
            ]
            results.append(prod[0][:count] - prod[1][count:])
            results.append(prod[1][:count] + prod[0][count:])
        for h in range(ch_count // 4):
            quads = chunk_transpose([r[:, h * LANES : (h + 1) * LANES] for r in results])
            for e in range(4):
                out_ref[here, 4 * h + e] = quads[e].astype(bf16).reshape(step, PAD, LANES)


def widen(mixed_ref, wide):
    for i in range(mixed_ref.shape[0] * PAIRS):
        wide[i * PITCH : i * PITCH + PAD, :] = mixed_ref[i // PAIRS, i % PAIRS].astype(f32)


def side_of(wide, count, m):
    turned = wide[pl.ds(m, count * PAIRS, stride=PITCH), :].astype(bf16).T
    return jnp.concatenate([turned[: LANES // 2], turned[LANES // 2 :]], axis=1)


def synthesis_kernel(ord_dev, lon, index_ref, slots_ref, mixed_ref, table_hbm, out_ref, table, wide, sems):
    copy = fetch_pairs(table_hbm, table, sems)
    widen(mixed_ref, wide)
    count = out_ref.shape[0]
    half = LANES // 2
    parity = degree_parity((half, table.shape[1]), 1, ord_dev)

    @pl.loop(0, PAIRS)
    def _(p):
        copy(p).wait()
        north, south = [], []
        for m2 in range(2):
            order = order_of(slots_ref, index_ref, ord_dev, 2 * p + m2)
            weight = jnp.where(order == 0, 1.0 / lon, 2.0 / lon)
            part = side_of(wide, count, 2 * p + m2).astype(f32)
            same = parity == (order & 1)
            split = jnp.concatenate([jnp.where(same, part, 0.0), jnp.where(same, 0.0, part)], axis=0)
            prod = jnp.dot(split.astype(bf16), table[2 * p + m2], preferred_element_type=f32)
            north.append((prod[:half] + prod[half:]) * weight)
            south.append((prod[:half] - prod[half:]) * weight)
        up = jnp.concatenate(north, axis=0).astype(bf16).T
        down = jnp.concatenate(south, axis=0).astype(bf16).T
        for s in range(count // 2):
            out_ref[s, p] = up[s * PAD : (s + 1) * PAD]
            out_ref[count - 1 - s, p] = down[s * PAD : (s + 1) * PAD]


def spectrum_kernel(ord_dev, mixed_ref, pick_ref, out_ref, wide):
    count = mixed_ref.shape[0]
    widen(mixed_ref, wide)

    @pl.loop(0, ord_dev)
    def _(m):
        side = side_of(wide, count, m)
        spec = jnp.dot(side, pick_ref[...], preferred_element_type=f32).astype(bf16)
        out_ref[m] = spec.reshape(out_ref.shape[1:])


def backward_kernel(
    lat_dev, lat_count, index_ref, rows_ref, table_hbm, field_hbm, out_ref, wide, left, table_ref, field_ref, sems
):
    copies = [
        pltpu.make_async_copy(table_hbm, table_ref, sems.at[0]),
        pltpu.make_async_copy(field_hbm, field_ref, sems.at[1]),
    ]
    for copy in copies:
        copy.start()
    half = rows_ref.shape[0] * rows_ref.shape[1]
    ch_dev = LANES // 4
    for i in range(half):
        wide[i * PITCH : i * PITCH + PAD, :] = rows_ref[i // PAIRS, i % PAIRS].astype(f32)
    for j in range(lat_dev):
        slot = slot_of(j, lat_dev, index_ref[0], lat_count)
        block = wide[pl.ds(slot, half, stride=PITCH), :].astype(bf16).T
        for q in range(4):
            left[j * ch_dev : (j + 1) * ch_dev, q * half : (q + 1) * half] = block[
                q * ch_dev : (q + 1) * ch_dev
            ]
    lon = out_ref.shape[2]
    for copy in copies:
        copy.wait()
    for b in range(4):
        cut = slice(b * lon // 4, (b + 1) * lon // 4)
        wave = jnp.dot(left[...], table_ref[:, cut], preferred_element_type=f32)
        cubic = wave * wave * wave
        grown = 0.5 * wave * (1.0 + jnp.tanh(math.sqrt(2.0 / math.pi) * (wave + 0.044715 * cubic)))
        field = field_ref[:, :, cut].astype(f32)
        out_ref[:, :, cut] = (field + grown.reshape(field.shape)).astype(bf16)


def params(mib=VMEM_MIB):
    return pltpu.CompilerParams(vmem_limit_bytes=int(mib * 2**20))


def cost(flops, moved):
    return pl.CostEstimate(flops=int(flops), bytes_accessed=int(moved), transcendentals=0)


MIX_BANDS = 8
vmem = pl.BlockSpec(memory_space=pltpu.VMEM)
smem = pl.BlockSpec(memory_space=pltpu.SMEM)
hbm = pl.BlockSpec(memory_space=pltpu.HBM)


def buffer_of(lat_count):
    return jax.ShapeDtypeStruct((lat_count, PAIRS, PAD, LANES), bf16)


def call_forward(lat_count, index, slots, field_in):
    lat_dev, ch_dev, lon = field_in.shape
    half = lat_count * PAIRS
    return pl.pallas_call(
        functools.partial(forward_kernel, lat_dev, lat_count, slots.shape[1] // lat_count),
        out_shape=buffer_of(lat_count),
        in_specs=[smem, vmem, hbm],
        out_specs=hbm,
        scratch_shapes=[
            pltpu.VMEM((lon, 4 * half), bf16),
            pltpu.VMEM(field_in.shape, bf16),
            pltpu.VMEM((lat_dev, 4, ch_dev, half), f32),
            pltpu.VMEM((half * PITCH, LANES), f32),
            pltpu.VMEM((lat_count, PAIRS, PAD, LANES), bf16),
            pltpu.SemaphoreType.DMA,
            pltpu.SemaphoreType.DMA((4,)),
        ],
        compiler_params=params(TABLE_MIB),
        name="forward",
    )(index, slots, field_in)


def call_legendre(lat_count, lat_dev, index, slots):
    lat_total = lat_count * lat_dev
    modes = slots.shape[1]
    ord_dev = modes // lat_count
    full = lat_count * PAD
    near = full // 2
    angle = math.pi * (np.arange(lat_total) + 0.5) / lat_total
    geo = np.zeros((2, lat_count, PAD), np.float32)
    geo[0, :, :lat_dev] = np.cos(angle).reshape(lat_count, lat_dev)
    geo[1, :, :lat_dev] = np.log(np.sin(angle)).reshape(lat_count, lat_dev)
    geo = geo.reshape(2, full)[:, :near]
    k = np.arange(1, modes)
    prod = np.zeros((1, full), np.float32)
    prod[0, 1:modes] = np.cumsum(0.5 * np.log((2.0 * k - 1.0) / (2.0 * k)))
    deg = np.arange(modes, dtype=np.float64)
    scale = np.sqrt(np.maximum(4.0 * deg * deg - 1.0, 1.0))
    scales = np.ones((2, modes), np.float32)
    scales[0] = scale
    scales[1, 1:] = 1.0 / scale[:-1]
    groups = near // LANES
    parts = 4
    state = pltpu.VMEM((groups, PAD, LANES), f32)
    table = pl.pallas_call(
        functools.partial(legendre_kernel, ord_dev),
        out_shape=jax.ShapeDtypeStruct((PAD, 2, lat_count // 2, PAD, near), bf16),
        in_specs=[smem, smem, vmem, vmem, vmem],
        out_specs=hbm,
        scratch_shapes=[state] * 5
        + [
            pltpu.VMEM((PAD, LANES), f32),
            pltpu.VMEM((groups, PAD * (2 * PAD + 1), LANES), f32),
            pltpu.VMEM((PAD, 2, lat_count // 2, PAD, near), bf16),
            pltpu.SemaphoreType.DMA((parts,)),
        ],
        compiler_params=params(TABLE_MIB),
        cost_estimate=cost(8e9, 2e7),
        name="legendre",
    )(index, jnp.asarray(scales), slots, jnp.asarray(geo), jnp.asarray(prod))
    return table.reshape(PAD, full, near)


def call_inverse_table(lat_count, lon, slots):
    half = lat_count * PAIRS
    return pl.pallas_call(
        functools.partial(inverse_table_kernel, slots.shape[1] // lat_count, lat_count),
        out_shape=jax.ShapeDtypeStruct((4 * half, lon), bf16),
        in_specs=[vmem],
        out_specs=hbm,
        scratch_shapes=[
            pltpu.VMEM((4 * half, lon), bf16),
            pltpu.VMEM((2 * half, LANES), f32),
            pltpu.SemaphoreType.DMA,
        ],
        compiler_params=params(TABLE_MIB),
        cost_estimate=cost(2e9, 4e6),
        name="inverse_table",
    )(slots)


def call_analysis(ord_dev, index, orders, rows, table):
    lat_count = rows.shape[0]
    return pl.pallas_call(
        functools.partial(analysis_kernel, ord_dev),
        out_shape=jax.ShapeDtypeStruct(rows.shape, bf16),
        in_specs=[smem, smem, vmem, hbm],
        out_specs=vmem,
        scratch_shapes=[
            pltpu.VMEM(table.shape, bf16),
            pltpu.VMEM((lat_count * PAIRS * PITCH, LANES), f32),
            pltpu.SemaphoreType.DMA((PAIRS,)),
        ],
        compiler_params=params(),
        name="analysis",
    )(index, orders, rows, table)


def weight_pieces(index, weights, ch_count):
    piece = jax.ShapeDtypeStruct((2, 2) + weights.shape[2:], bf16)
    return pl.pallas_call(
        weights_kernel,
        out_shape=(piece,) * ch_count,
        in_specs=[smem, vmem],
        out_specs=(vmem,) * ch_count,
        compiler_params=params(),
        name="weights",
    )(index, weights)


def move_along(pieces, steps):
    count = len(pieces)
    pieces = list(pieces)
    for k in steps:
        pieces[k] = lax.ppermute(pieces[k], "ch", [(e, (e + k) % count) for e in range(count)])
    return tuple(pieces)


def call_mix(index, coeffs, weights):
    ch_count = len(weights)
    return pl.pallas_call(
        mix_kernel,
        out_shape=jax.ShapeDtypeStruct(coeffs.shape, bf16),
        in_specs=[smem, vmem] + [hbm] * ch_count,
        out_specs=vmem,
        scratch_shapes=[
            pltpu.VMEM((ch_count,) + weights[0].shape, bf16),
            pltpu.SemaphoreType.DMA((ch_count,)),
        ],
        compiler_params=params(),
        name="mix",
    )(index, coeffs, *weights)


def call_synthesis(ord_dev, lon, index, orders, mixed, table):
    lat_count = mixed.shape[0]
    return pl.pallas_call(
        functools.partial(synthesis_kernel, ord_dev, lon),
        out_shape=buffer_of(mixed.shape[0]),
        in_specs=[smem, smem, vmem, hbm],
        out_specs=vmem,
        scratch_shapes=[
            pltpu.VMEM(table.shape, bf16),
            pltpu.VMEM((lat_count * PAIRS * PITCH, LANES), f32),
            pltpu.SemaphoreType.DMA((PAIRS,)),
        ],
        compiler_params=params(),
        name="synthesis",
    )(index, orders, mixed, table)


def call_spectrum(ord_dev, mixed):
    lat_count = mixed.shape[0]
    modes = ord_dev * lat_count
    pick = np.zeros((lat_count, PAD, modes), np.float32)
    pick[:, :ord_dev] = np.eye(modes, dtype=np.float32).reshape(lat_count, ord_dev, modes)
    pick = pick.reshape(lat_count * PAIRS, 2, modes).transpose(1, 0, 2)
    pick = jnp.asarray(pick.reshape(lat_count * PAD, modes), bf16)
    return pl.pallas_call(
        functools.partial(spectrum_kernel, ord_dev),
        out_shape=jax.ShapeDtypeStruct((ord_dev, 2, LANES // 4, modes), bf16),
        in_specs=[vmem, vmem],
        out_specs=vmem,
        scratch_shapes=[pltpu.VMEM((lat_count * PAIRS * PITCH, LANES), f32)],
        compiler_params=params(),
        cost_estimate=cost(3e9, 4e6),
        name="spectrum",
    )(mixed, pick)


def call_backward(index, rows, table, field_in):
    lat_dev, ch_dev, _ = field_in.shape
    lat_count = rows.shape[0]
    half = lat_count * PAIRS
    return pl.pallas_call(
        functools.partial(backward_kernel, lat_dev, lat_count),
        out_shape=jax.ShapeDtypeStruct(field_in.shape, bf16),
        in_specs=[smem, vmem, hbm, hbm],
        out_specs=vmem,
        scratch_shapes=[
            pltpu.VMEM((half * PITCH, LANES), f32),
            pltpu.VMEM((lat_dev * ch_dev, 4 * half), bf16),
            pltpu.VMEM(table.shape, bf16),
            pltpu.VMEM(field_in.shape, bf16),
            pltpu.SemaphoreType.DMA((2,)),
        ],
        compiler_params=params(),
        name="backward",
    )(index, rows, table, field_in)


def on_device(field_in, mix_weight, order_slots):
    lat_dev, _, lon = field_in.shape
    lat_count = lax.axis_size("lat")
    modes = order_slots.shape[0]
    ord_dev = modes // lat_count
    index = lax.axis_index("lat")
    index = index.reshape(1)
    slots = order_slots.reshape(1, modes)

    rows = call_forward(lat_count, index, slots, field_in)
    rows = lax.all_to_all(rows, "lat", 0, 0, tiled=True)
    legendre = call_legendre(lat_count, lat_dev, index, slots)
    weights = jnp.transpose(mix_weight, (0, 3, 2, 1))
    weights, legendre = lax.optimization_barrier((weights, legendre))
    ch_index = lax.axis_index("ch").reshape(1)
    ch_count = lax.axis_size("ch")
    far = sorted(range(1, ch_count), key=lambda k: -min(k, ch_count - k))[: ch_count // 2]
    near = [k for k in range(1, ch_count) if k not in far]
    weights = move_along(weight_pieces(ch_index, weights, ch_count), far)
    coeffs = call_analysis(ord_dev, index, order_slots, rows, legendre)
    coeffs, weights = lax.optimization_barrier((coeffs, weights))
    weights = move_along(weights, near)
    coeffs = lax.all_to_all(coeffs.reshape(-1, PAD, LANES), ("lat", "ch"), 0, 0, tiled=True)
    mixed = call_mix(ch_index, coeffs.reshape(rows.shape), weights)
    mixed = lax.all_to_all(mixed.reshape(-1, PAD, LANES), ("lat", "ch"), 0, 0, tiled=True).reshape(rows.shape)
    synth = call_synthesis(ord_dev, lon, index, order_slots, mixed, legendre)
    synth = lax.all_to_all(synth, "lat", 0, 0, tiled=True)
    spectrum = call_spectrum(ord_dev, mixed)
    inverse_table = call_inverse_table(lat_count, lon, slots)
    field_out = call_backward(index, synth, inverse_table, field_in)
    return (field_out, spectrum)


def solution(mesh):
    placed = (P("lat", "ch", None), P(None, None, "ch", "lat"), P())
    return jax.shard_map(
        on_device,
        mesh=mesh,
        in_specs=placed,
        out_specs=(P("lat", "ch", None), P("lat", None, "ch", None)),
        check_vma=False,
    )
```

```python
import functools
import math

import jax
import jax.numpy as jnp
import numpy as np
from jax import lax
from jax.experimental import pallas as pl
from jax.experimental.pallas import tpu as pltpu
from jax.sharding import PartitionSpec as P

PAD = 16
PAIRS = 8
LANES = 128
NO_ORDER = 1000
PITCH = 17
RESCALE_BITS = 60
f32 = jnp.float32
bf16 = jnp.bfloat16


VMEM_MIB = 50
TABLE_MIB = 57


def cos_turns(turns):
    part = turns - jnp.floor(turns + 0.5)
    y = part * math.pi
    z = y * y
    s = 1.0 / 362880 - z * (1.0 / 39916800)
    s = -1.0 / 5040 + z * s
    s = 1.0 / 120 + z * s
    s = -1.0 / 6 + z * s
    s = y * (1.0 + z * s)
    return 1.0 - 2.0 * s * s


def minus_sin_turns(turns):
    return cos_turns(turns + 0.25)


def chunk_transpose(rows):
    lane = lax.broadcasted_iota(jnp.int32, rows[0].shape, 1)
    low = lane < 64
    even = (lane // 32) % 2 == 0
    mid = [None] * 4
    for i in range(2):
        a, b = rows[i], rows[i + 2]
        mid[i] = jnp.where(low, a, pltpu.roll(b, 64, 1))
        mid[i + 2] = jnp.where(low, pltpu.roll(a, 64, 1), b)
    out = []
    for i in (0, 2):
        a, b = mid[i], mid[i + 1]
        out.append(jnp.where(even, a, pltpu.roll(b, 32, 1)))
        out.append(jnp.where(even, pltpu.roll(a, 96, 1), b))
    return out


def digits_of(slots_ref):
    slots = slots_ref[...].astype(f32)
    high = jnp.floor(slots * (1.0 / PAD))
    return high.astype(bf16), (slots - PAD * high).astype(bf16)


def one_hot(hit):
    return jnp.where(hit, 1.0, 0.0).astype(bf16)


def slot_wanted(place, ord_dev, half):
    within = 2 * (place % PAIRS) + place // half
    return jnp.where(within < ord_dev, (place % half) // PAIRS * ord_dev + within, -1)


def order_lanes(slots_ref, ord_dev, lat_count):
    modes = slots_ref.shape[1]
    half = lat_count * PAIRS
    wanted = slot_wanted(lax.broadcasted_iota(jnp.int32, (1, 2 * half), 1), ord_dev, half)
    pick = one_hot(lax.broadcasted_iota(jnp.int32, (modes, 2 * half), 0) == wanted)
    digits = [jnp.broadcast_to(d.astype(f32), (8, modes)).astype(bf16) for d in digits_of(slots_ref)]
    high, low = [jnp.dot(d, pick, preferred_element_type=f32) for d in digits]
    return high[0:1] * PAD + low[0:1]


def order_rows(slots_ref, ord_dev, lat_count):
    modes = slots_ref.shape[1]
    half = lat_count * PAIRS
    wanted = slot_wanted(lax.broadcasted_iota(jnp.int32, (2 * half, 1), 0), ord_dev, half)
    pick = one_hot(lax.broadcasted_iota(jnp.int32, (2 * half, modes), 1) == wanted)
    contract = (((1,), (1,)), ((), ()))
    high, low = [
        lax.dot_general(
            pick,
            jnp.broadcast_to(d.astype(f32), (LANES, modes)).astype(bf16),
            contract,
            preferred_element_type=f32,
        )
        for d in digits_of(slots_ref)
    ]
    return high * PAD + low


def order_column(slots, wanted):
    place = lax.broadcasted_iota(jnp.int32, (wanted.shape[0], slots.shape[1]), 1)
    return jnp.sum(jnp.where(place == wanted, slots, 0.0), axis=1, keepdims=True)


def slot_of(j, lat_dev, index, lat_count):
    return jnp.where(index < lat_count // 2, j, lat_dev - 1 - j)


def narrow(wide, out_ref, out_hbm, sems):
    count = out_ref.shape[0]
    part = count // sems.shape[0]
    copies = []
    for d in range(count):
        for p in range(PAIRS):
            i = d * PAIRS + p
            out_ref[d, p] = wide[i * PITCH : i * PITCH + PAD, :].astype(bf16)
        if d % part == part - 1:
            cut = slice(d + 1 - part, d + 1)
            copies.append(pltpu.make_async_copy(out_ref.at[cut], out_hbm.at[cut], sems.at[d // part]))
            copies[-1].start()
    for copy in copies:
        copy.wait()


def forward_kernel(
    lat_dev, lat_count, ord_dev, index_ref, slots_ref, field_hbm, out_hbm, table, field_ref, rows, turned, out_ref, sem, sems
):
    fetch = pltpu.make_async_copy(field_hbm, field_ref, sem)
    fetch.start()
    lon = table.shape[0]
    half = table.shape[1] // 4
    order = order_lanes(slots_ref, ord_dev, lat_count)
    step_cos = cos_turns(order * (LANES / lon))
    step_sin = -minus_sin_turns(order * (LANES / lon))

    @pl.loop(0, LANES // PAD)
    def _(r):
        n = (lax.broadcasted_iota(jnp.int32, (PAD, order.shape[1]), 0) + r * PAD).astype(f32)
        turns = order * n * (1.0 / lon)
        re, im = cos_turns(turns), minus_sin_turns(turns)
        for k in range(lon // LANES):
            at = pl.ds(pl.multiple_of(k * LANES + r * PAD, PAD), PAD)
            for m2 in range(2):
                cut = slice(m2 * half, (m2 + 1) * half)
                table[at, 2 * m2 * half : (2 * m2 + 1) * half] = re[:, cut].astype(bf16)
                table[at, (2 * m2 + 1) * half : (2 * m2 + 2) * half] = im[:, cut].astype(bf16)
            re, im = re * step_cos + im * step_sin, im * step_cos - re * step_sin

    fetch.wait()
    ch_dev = field_ref.shape[1]
    field = field_ref[...].reshape(lat_dev * ch_dev, lon)
    for q in range(4):
        part = jnp.dot(field, table[:, q * half : (q + 1) * half], preferred_element_type=f32)
        rows[:, q] = part.reshape(lat_dev, ch_dev, half)
    index = index_ref[0]
    lat_total = lat_dev * lat_count
    for j in range(lat_dev):
        place = jnp.full((1, half), index * lat_dev + j, jnp.int32).astype(f32)
        quad = cos_turns((place + 0.5) * (0.5 / lat_total) - 0.25) * (math.pi / lat_total)
        block = rows[j].reshape(4 * ch_dev, half) * quad
        turned[pl.ds(slot_of(j, lat_dev, index, lat_count), half, stride=PITCH), :] = block.astype(bf16).T.astype(f32)
    turned[pl.ds(lat_dev, half, stride=PITCH), :] = jnp.zeros((half, LANES), f32)
    narrow(turned, out_ref, out_hbm, sems)


def inverse_table_kernel(ord_dev, lat_count, slots_ref, out_hbm, out_ref, orders, sem):
    lon = out_ref.shape[1]
    half = out_ref.shape[0] // 4
    steps = half // PAD
    orders[...] = order_rows(slots_ref, ord_dev, lat_count)

    @pl.loop(0, 2 * steps)
    def _(r):
        order = orders[pl.ds(pl.multiple_of(r * PAD, PAD), PAD), :]
        step_cos = cos_turns(order * (LANES / lon))
        step_sin = -minus_sin_turns(order * (LANES / lon))
        n = lax.broadcasted_iota(jnp.int32, (PAD, LANES), 1).astype(f32)
        turns = order * n * (1.0 / lon)
        re, im = cos_turns(turns), minus_sin_turns(turns)
        top = (r // steps) * (2 * half) + (r % steps) * PAD
        for k in range(lon // LANES):
            cut = slice(k * LANES, (k + 1) * LANES)
            out_ref[pl.ds(pl.multiple_of(top, PAD), PAD), cut] = re.astype(bf16)
            out_ref[pl.ds(pl.multiple_of(top + half, PAD), PAD), cut] = im.astype(bf16)
            re, im = re * step_cos + im * step_sin, im * step_cos - re * step_sin

    copy = pltpu.make_async_copy(out_ref, out_hbm, sem)
    copy.start()
    copy.wait()


def legendre_kernel(
    deg_dev, index_ref, slots_ref, geo_ref, prod_ref, out_hbm, cur, bef, resc, start, expo, buf, table, sems
):
    groups = cur.shape[0]
    pitch = 2 * PAD + 1
    log_step = RESCALE_BITS * math.log(2.0)
    shrink = 2.0 ** (-RESCALE_BITS)
    limit = 2.0**RESCALE_BITS
    row = lax.broadcasted_iota(jnp.int32, (PAD, 1), 0)
    order = order_column(slots_ref[...].astype(f32), jnp.where(row < deg_dev, index_ref[0] * deg_dev + row, -1))
    order = jnp.broadcast_to(jnp.where(row < deg_dev, order, 1.0 * NO_ORDER), (PAD, LANES))
    order_sq = order * order
    for state in (cur, bef, resc):
        state[...] = jnp.zeros_like(state)
    picked = jnp.zeros((PAD, 1), f32)
    for g in range(prod_ref.shape[1] // LANES):
        lane = lax.broadcasted_iota(jnp.int32, (PAD, LANES), 1) + g * LANES
        hit = order == lane.astype(f32)
        term = jnp.where(hit, prod_ref[:, g * LANES : (g + 1) * LANES], 0.0)
        picked = picked + jnp.sum(term, axis=1, keepdims=True)
    head = 0.5 * jnp.log(order + 0.5) + picked
    for g in range(groups):
        log_start = head + order * geo_ref[1:2, g * LANES : (g + 1) * LANES]
        start[g] = log_start
        expo[g] = jnp.exp(log_start)
        for twin in range(2):
            buf[g, pl.ds(PAD + twin * PAIRS + PAIRS - 1, PAD, stride=pitch), :] = jnp.zeros((PAD, LANES), f32)

    def block(index):
        now = [cur[g] for g in range(groups)]
        old = [bef[g] for g in range(groups)]
        factor = [expo[g] for g in range(groups)]
        cosine = [geo_ref[0:1, g * LANES : (g + 1) * LANES] for g in range(groups)]
        lane = lax.broadcasted_iota(jnp.int32, (PAD, LANES), 1) + 2 * index * deg_dev
        degs = lane.astype(f32)
        prev = degs - 1.0
        alphas = jnp.sqrt(
            jnp.maximum(4.0 * degs * degs - 1.0, 1.0) / jnp.maximum(degs * degs - order_sq, 1.0)
        )
        betas = jnp.sqrt(
            jnp.maximum(prev * prev - order_sq, 0.0) / jnp.maximum(4.0 * prev * prev - 1.0, 1.0)
        )
        for twin, i in [(t, k) for t in range(2) for k in range(deg_dev)]:
            at = twin * deg_dev + i
            alpha = jnp.broadcast_to(alphas[:, at : at + 1], (PAD, LANES))
            beta = jnp.broadcast_to(betas[:, at : at + 1], (PAD, LANES))
            both = alpha * beta
            begin = jnp.where(order == (2 * index * deg_dev + at).astype(f32), 1.0, 0.0)
            for g in range(groups):
                new = (alpha * cosine[g]) * now[g] + (begin - both * old[g])
                old[g], now[g] = now[g], new
                row = i % 2 * PAD + twin * PAIRS + i // 2
                buf[g, pl.ds(row, PAD, stride=pitch), :] = new * factor[g]
            if i in (deg_dev // 2, deg_dev - 1):
                for g in range(groups):
                    large = jnp.abs(now[g]) > limit
                    ratio = jnp.where(large, shrink, 1.0)
                    now[g] = now[g] * ratio
                    old[g] = old[g] * ratio
                    count = resc[g] + jnp.where(large, 1.0, 0.0)
                    resc[g] = count
                    factor[g] = jnp.exp(start[g] + count * log_step)
        for g in range(groups):
            cur[g] = now[g]
            bef[g] = old[g]
            expo[g] = factor[g]
            for m in range(PAD):
                for side in range(2):
                    row = m * pitch + side * PAD
                    tile = buf[g, row : row + PAD, :].astype(bf16)
                    table[m, side, index, :, g * LANES : (g + 1) * LANES] = tile

    parts = sems.shape[0]
    count = table.shape[2] // parts
    copies = []
    for part in range(parts):
        pl.loop(part * count, (part + 1) * count)(block)
        cut = slice(part * count, (part + 1) * count)
        copies.append(pltpu.make_async_copy(table.at[:, :, cut], out_hbm.at[:, :, cut], sems.at[part]))
        copies[-1].start()
    for copy in copies:
        copy.wait()


def degree_parity(shape, dim, deg_dev):
    half = shape[dim] // 2
    i = lax.broadcasted_iota(jnp.int32, shape, dim)
    return ((i % half) // PAIRS * deg_dev + i // half) & 1


def order_of(slots_ref, index_ref, ord_dev, m):
    return slots_ref[index_ref[0] * ord_dev + jnp.minimum(m, ord_dev - 1)]


def fetch_pairs(table_hbm, table, sems):
    def copy(p):
        cut = pl.ds(2 * p, 2)
        return pltpu.make_async_copy(table_hbm.at[cut], table.at[cut], sems.at[p])

    for p in range(PAIRS):
        copy(p).start()
    return copy


def analysis_kernel(
    ord_dev, index_ref, slots_ref, rows_ref, table_hbm, out_hbm, table, wide, sems, out_ref, leave
):
    copy = fetch_pairs(table_hbm, table, sems)
    count = rows_ref.shape[0]
    half = count * PAIRS
    parity = degree_parity((table.shape[1], LANES), 0, ord_dev)

    @pl.loop(0, PAIRS)
    def _(p):
        north = jnp.concatenate([rows_ref[s, p] for s in range(count // 2)], axis=0)
        south = jnp.concatenate([rows_ref[count - 1 - s, p] for s in range(count // 2)], axis=0)
        both = jnp.concatenate([north, south], axis=1)
        copy(p).wait()
        for m2 in range(2):
            order = order_of(slots_ref, index_ref, ord_dev, 2 * p + m2)
            prod = jnp.dot(table[2 * p + m2], both, preferred_element_type=f32)
            mirror = prod[:, LANES:]
            coefs = prod[:, :LANES] + jnp.where(parity == (order & 1), mirror, -mirror)
            low, high = coefs[:half], coefs[half:]
            if m2 == 0:
                high = pltpu.roll(high, LANES // 2, 1)
            else:
                low = pltpu.roll(low, LANES // 2, 1)
            lane = lax.broadcasted_iota(jnp.int32, low.shape, 1)
            wide[pl.ds(2 * p + m2, half, stride=PITCH), :] = jnp.where(lane < LANES // 2, low, high)

    narrow(wide, out_ref, out_hbm, leave)


def weights_kernel(index_ref, weight_ref, *out_refs):
    ch_count = len(out_refs)
    last = weight_ref.shape[1] - 1
    for k, out_ref in enumerate(out_refs):
        there = lax.rem(index_ref[0] + k, ch_count)
        for w in range(2):
            for l2 in range(2):
                out_ref[w, l2] = weight_ref[w, jnp.minimum(2 * there + l2, last)]


def mix_kernel(index_ref, coef_ref, *refs):
    ch_count = len(refs) - 3
    out_ref, weight, sems = refs[ch_count:]
    copies = []
    for k in range(ch_count):
        source = lax.rem(index_ref[0] + ch_count - k, ch_count)
        copies.append(pltpu.make_async_copy(refs[k], weight.at[source], sems.at[k]))
        copies[-1].start()
    for copy in copies:
        copy.wait()
    bands = coef_ref.shape[0]
    ch_dev = LANES // 4
    channels = ch_count * ch_dev
    contract = (((1,), (1,)), ((), ()))
    step = MIX_BANDS
    count = step * PAD

    @pl.loop(0, bands // step)
    def _(chunk):
        here = pl.ds(chunk * step, step)
        groups = []
        for h in range(ch_count // 4):
            quads = [coef_ref[here, 4 * h + e].reshape(count, LANES).astype(f32) for e in range(4)]
            groups.append(chunk_transpose(quads))
        results = []
        for l2 in range(2):
            left = jnp.concatenate(
                [jnp.concatenate([g[2 * l2 + x] for g in groups], axis=1) for x in range(2)], axis=0
            ).astype(bf16)
            prod = [
                lax.dot_general(
                    left,
                    weight[:, w, l2].reshape(channels, channels),
                    contract,
                    preferred_element_type=f32,
                )
                for w in range(2)
            ]
            results.append(prod[0][:count] - prod[1][count:])
            results.append(prod[1][:count] + prod[0][count:])
        for h in range(ch_count // 4):
            quads = chunk_transpose([r[:, h * LANES : (h + 1) * LANES] for r in results])
            for e in range(4):
                out_ref[here, 4 * h + e] = quads[e].astype(bf16).reshape(step, PAD, LANES)


def widen(mixed_ref, wide):
    for i in range(mixed_ref.shape[0] * PAIRS):
        wide[i * PITCH : i * PITCH + PAD, :] = mixed_ref[i // PAIRS, i % PAIRS].astype(f32)


def side_of(wide, count, m):
    turned = wide[pl.ds(m, count * PAIRS, stride=PITCH), :].astype(bf16).T
    return jnp.concatenate([turned[: LANES // 2], turned[LANES // 2 :]], axis=1)


def synthesis_kernel(ord_dev, lon, index_ref, slots_ref, mixed_ref, table_hbm, out_hbm, table, wide, sems, out_ref, leave):
    copy = fetch_pairs(table_hbm, table, sems)
    widen(mixed_ref, wide)
    count = out_ref.shape[0]
    half = LANES // 2
    parity = degree_parity((half, table.shape[1]), 1, ord_dev)

    def sent(p):
        return pltpu.make_async_copy(out_ref.at[:, p], out_hbm.at[:, p], leave.at[p])

    @pl.loop(0, PAIRS)
    def _(p):
        copy(p).wait()
        north, south = [], []
        for m2 in range(2):
            order = order_of(slots_ref, index_ref, ord_dev, 2 * p + m2)
            weight = jnp.where(order == 0, 1.0 / lon, 2.0 / lon)
            part = side_of(wide, count, 2 * p + m2).astype(f32)
            same = parity == (order & 1)
            split = jnp.concatenate([jnp.where(same, part, 0.0), jnp.where(same, 0.0, part)], axis=0)
            prod = jnp.dot(split.astype(bf16), table[2 * p + m2], preferred_element_type=f32)
            north.append((prod[:half] + prod[half:]) * weight)
            south.append((prod[:half] - prod[half:]) * weight)
        up = jnp.concatenate(north, axis=0).astype(bf16).T
        down = jnp.concatenate(south, axis=0).astype(bf16).T
        for s in range(count // 2):
            out_ref[s, p] = up[s * PAD : (s + 1) * PAD]
            out_ref[count - 1 - s, p] = down[s * PAD : (s + 1) * PAD]
        sent(p).start()

    for p in range(PAIRS):
        sent(p).wait()


def spectrum_kernel(ord_dev, mixed_ref, pick_ref, out_ref, wide):
    count = mixed_ref.shape[0]
    widen(mixed_ref, wide)

    @pl.loop(0, ord_dev)
    def _(m):
        side = side_of(wide, count, m)
        spec = jnp.dot(side, pick_ref[...], preferred_element_type=f32).astype(bf16)
        out_ref[m] = spec.reshape(out_ref.shape[1:])


def backward_kernel(
    lat_dev, lat_count, index_ref, rows_ref, table_hbm, field_hbm, out_ref, wide, left, table_ref, field_ref, sems
):
    copies = [
        pltpu.make_async_copy(table_hbm, table_ref, sems.at[0]),
        pltpu.make_async_copy(field_hbm, field_ref, sems.at[1]),
    ]
    for copy in copies:
        copy.start()
    half = rows_ref.shape[0] * rows_ref.shape[1]
    ch_dev = LANES // 4
    for i in range(half):
        wide[i * PITCH : i * PITCH + PAD, :] = rows_ref[i // PAIRS, i % PAIRS].astype(f32)
    for j in range(lat_dev):
        slot = slot_of(j, lat_dev, index_ref[0], lat_count)
        block = wide[pl.ds(slot, half, stride=PITCH), :].astype(bf16).T
        for q in range(4):
            left[j * ch_dev : (j + 1) * ch_dev, q * half : (q + 1) * half] = block[
                q * ch_dev : (q + 1) * ch_dev
            ]
    lon = out_ref.shape[2]
    for copy in copies:
        copy.wait()
    for b in range(4):
        cut = slice(b * lon // 4, (b + 1) * lon // 4)
        wave = jnp.dot(left[...], table_ref[:, cut], preferred_element_type=f32)
        cubic = wave * wave * wave
        grown = 0.5 * wave * (1.0 + jnp.tanh(math.sqrt(2.0 / math.pi) * (wave + 0.044715 * cubic)))
        field = field_ref[:, :, cut].astype(f32)
        out_ref[:, :, cut] = (field + grown.reshape(field.shape)).astype(bf16)


def params(mib=VMEM_MIB):
    return pltpu.CompilerParams(vmem_limit_bytes=int(mib * 2**20))


def cost(flops, moved):
    return pl.CostEstimate(flops=int(flops), bytes_accessed=int(moved), transcendentals=0)


MIX_BANDS = 8
vmem = pl.BlockSpec(memory_space=pltpu.VMEM)
smem = pl.BlockSpec(memory_space=pltpu.SMEM)
hbm = pl.BlockSpec(memory_space=pltpu.HBM)


def buffer_of(lat_count):
    return jax.ShapeDtypeStruct((lat_count, PAIRS, PAD, LANES), bf16)


def call_forward(lat_count, index, slots, field_in):
    lat_dev, ch_dev, lon = field_in.shape
    half = lat_count * PAIRS
    return pl.pallas_call(
        functools.partial(forward_kernel, lat_dev, lat_count, slots.shape[1] // lat_count),
        out_shape=buffer_of(lat_count),
        in_specs=[smem, vmem, hbm],
        out_specs=hbm,
        scratch_shapes=[
            pltpu.VMEM((lon, 4 * half), bf16),
            pltpu.VMEM(field_in.shape, bf16),
            pltpu.VMEM((lat_dev, 4, ch_dev, half), f32),
            pltpu.VMEM((half * PITCH, LANES), f32),
            pltpu.VMEM((lat_count, PAIRS, PAD, LANES), bf16),
            pltpu.SemaphoreType.DMA,
            pltpu.SemaphoreType.DMA((4,)),
        ],
        compiler_params=params(TABLE_MIB),
        name="forward",
    )(index, slots, field_in)


def call_legendre(lat_count, lat_dev, index, slots):
    lat_total = lat_count * lat_dev
    modes = slots.shape[1]
    ord_dev = modes // lat_count
    full = lat_count * PAD
    near = full // 2
    angle = math.pi * (np.arange(lat_total) + 0.5) / lat_total
    geo = np.zeros((2, lat_count, PAD), np.float32)
    geo[0, :, :lat_dev] = np.cos(angle).reshape(lat_count, lat_dev)
    geo[1, :, :lat_dev] = np.log(np.sin(angle)).reshape(lat_count, lat_dev)
    geo = geo.reshape(2, full)[:, :near]
    k = np.arange(1, modes)
    prod = np.zeros((1, full), np.float32)
    prod[0, 1:modes] = np.cumsum(0.5 * np.log((2.0 * k - 1.0) / (2.0 * k)))
    groups = near // LANES
    parts = 4
    state = pltpu.VMEM((groups, PAD, LANES), f32)
    table = pl.pallas_call(
        functools.partial(legendre_kernel, ord_dev),
        out_shape=jax.ShapeDtypeStruct((PAD, 2, lat_count // 2, PAD, near), bf16),
        in_specs=[smem, vmem, vmem, vmem],
        out_specs=hbm,
        scratch_shapes=[state] * 5
        + [
            pltpu.VMEM((groups, PAD * (2 * PAD + 1), LANES), f32),
            pltpu.VMEM((PAD, 2, lat_count // 2, PAD, near), bf16),
            pltpu.SemaphoreType.DMA((parts,)),
        ],
        compiler_params=params(TABLE_MIB),
        cost_estimate=cost(8e9, 2e7),
        name="legendre",
    )(index, slots, jnp.asarray(geo), jnp.asarray(prod))
    return table.reshape(PAD, full, near)


def call_inverse_table(lat_count, lon, slots):
    half = lat_count * PAIRS
    return pl.pallas_call(
        functools.partial(inverse_table_kernel, slots.shape[1] // lat_count, lat_count),
        out_shape=jax.ShapeDtypeStruct((4 * half, lon), bf16),
        in_specs=[vmem],
        out_specs=hbm,
        scratch_shapes=[
            pltpu.VMEM((4 * half, lon), bf16),
            pltpu.VMEM((2 * half, LANES), f32),
            pltpu.SemaphoreType.DMA,
        ],
        compiler_params=params(TABLE_MIB),
        cost_estimate=cost(2e9, 4e6),
        name="inverse_table",
    )(slots)


def call_analysis(ord_dev, index, orders, rows, table):
    lat_count = rows.shape[0]
    return pl.pallas_call(
        functools.partial(analysis_kernel, ord_dev),
        out_shape=jax.ShapeDtypeStruct(rows.shape, bf16),
        in_specs=[smem, smem, vmem, hbm],
        out_specs=hbm,
        scratch_shapes=[
            pltpu.VMEM(table.shape, bf16),
            pltpu.VMEM((lat_count * PAIRS * PITCH, LANES), f32),
            pltpu.SemaphoreType.DMA((PAIRS,)),
            pltpu.VMEM((lat_count, PAIRS, PAD, LANES), bf16),
            pltpu.SemaphoreType.DMA((4,)),
        ],
        compiler_params=params(),
        name="analysis",
    )(index, orders, rows, table)


def weight_pieces(index, weights, ch_count):
    piece = jax.ShapeDtypeStruct((2, 2) + weights.shape[2:], bf16)
    return pl.pallas_call(
        weights_kernel,
        out_shape=(piece,) * ch_count,
        in_specs=[smem, vmem],
        out_specs=(vmem,) * ch_count,
        compiler_params=params(),
        name="weights",
    )(index, weights)


def move_along(pieces, steps):
    count = len(pieces)
    pieces = list(pieces)
    for k in steps:
        pieces[k] = lax.ppermute(pieces[k], "ch", [(e, (e + k) % count) for e in range(count)])
    return tuple(pieces)


def call_mix(index, coeffs, weights):
    ch_count = len(weights)
    return pl.pallas_call(
        mix_kernel,
        out_shape=jax.ShapeDtypeStruct(coeffs.shape, bf16),
        in_specs=[smem, vmem] + [hbm] * ch_count,
        out_specs=vmem,
        scratch_shapes=[
            pltpu.VMEM((ch_count,) + weights[0].shape, bf16),
            pltpu.SemaphoreType.DMA((ch_count,)),
        ],
        compiler_params=params(),
        name="mix",
    )(index, coeffs, *weights)


def call_synthesis(ord_dev, lon, index, orders, mixed, table):
    lat_count = mixed.shape[0]
    return pl.pallas_call(
        functools.partial(synthesis_kernel, ord_dev, lon),
        out_shape=buffer_of(mixed.shape[0]),
        in_specs=[smem, smem, vmem, hbm],
        out_specs=hbm,
        scratch_shapes=[
            pltpu.VMEM(table.shape, bf16),
            pltpu.VMEM((lat_count * PAIRS * PITCH, LANES), f32),
            pltpu.SemaphoreType.DMA((PAIRS,)),
            pltpu.VMEM((lat_count, PAIRS, PAD, LANES), bf16),
            pltpu.SemaphoreType.DMA((PAIRS,)),
        ],
        compiler_params=params(),
        name="synthesis",
    )(index, orders, mixed, table)


def call_spectrum(ord_dev, mixed):
    lat_count = mixed.shape[0]
    modes = ord_dev * lat_count
    pick = np.zeros((lat_count, PAD, modes), np.float32)
    pick[:, :ord_dev] = np.eye(modes, dtype=np.float32).reshape(lat_count, ord_dev, modes)
    pick = pick.reshape(lat_count * PAIRS, 2, modes).transpose(1, 0, 2)
    pick = jnp.asarray(pick.reshape(lat_count * PAD, modes), bf16)
    return pl.pallas_call(
        functools.partial(spectrum_kernel, ord_dev),
        out_shape=jax.ShapeDtypeStruct((ord_dev, 2, LANES // 4, modes), bf16),
        in_specs=[vmem, vmem],
        out_specs=vmem,
        scratch_shapes=[pltpu.VMEM((lat_count * PAIRS * PITCH, LANES), f32)],
        compiler_params=params(),
        cost_estimate=cost(3e9, 4e6),
        name="spectrum",
    )(mixed, pick)


def call_backward(index, rows, table, field_in):
    lat_dev, ch_dev, _ = field_in.shape
    lat_count = rows.shape[0]
    half = lat_count * PAIRS
    return pl.pallas_call(
        functools.partial(backward_kernel, lat_dev, lat_count),
        out_shape=jax.ShapeDtypeStruct(field_in.shape, bf16),
        in_specs=[smem, vmem, hbm, hbm],
        out_specs=vmem,
        scratch_shapes=[
            pltpu.VMEM((half * PITCH, LANES), f32),
            pltpu.VMEM((lat_dev * ch_dev, 4 * half), bf16),
            pltpu.VMEM(table.shape, bf16),
            pltpu.VMEM(field_in.shape, bf16),
            pltpu.SemaphoreType.DMA((2,)),
        ],
        compiler_params=params(),
        name="backward",
    )(index, rows, table, field_in)


def on_device(field_in, mix_weight, order_slots):
    lat_dev, _, lon = field_in.shape
    lat_count = lax.axis_size("lat")
    modes = order_slots.shape[0]
    ord_dev = modes // lat_count
    index = lax.axis_index("lat")
    index = index.reshape(1)
    slots = order_slots.reshape(1, modes)

    rows = call_forward(lat_count, index, slots, field_in)
    rows = lax.all_to_all(rows, "lat", 0, 0, tiled=True)
    legendre = call_legendre(lat_count, lat_dev, index, slots)
    weights = jnp.transpose(mix_weight, (0, 3, 2, 1))
    weights, legendre = lax.optimization_barrier((weights, legendre))
    ch_index = lax.axis_index("ch").reshape(1)
    ch_count = lax.axis_size("ch")
    far = sorted(range(1, ch_count), key=lambda k: -min(k, ch_count - k))[: ch_count // 2]
    near = [k for k in range(1, ch_count) if k not in far]
    weights = move_along(weight_pieces(ch_index, weights, ch_count), far)
    coeffs = call_analysis(ord_dev, index, order_slots, rows, legendre)
    coeffs, weights = lax.optimization_barrier((coeffs, weights))
    weights = move_along(weights, near)
    coeffs = lax.all_to_all(coeffs.reshape(-1, PAD, LANES), ("lat", "ch"), 0, 0, tiled=True)
    mixed = call_mix(ch_index, coeffs.reshape(rows.shape), weights)
    mixed = lax.all_to_all(mixed.reshape(-1, PAD, LANES), ("lat", "ch"), 0, 0, tiled=True).reshape(rows.shape)
    synth = call_synthesis(ord_dev, lon, index, order_slots, mixed, legendre)
    synth = lax.all_to_all(synth, "lat", 0, 0, tiled=True)
    spectrum = call_spectrum(ord_dev, mixed)
    inverse_table = call_inverse_table(lat_count, lon, slots)
    field_out = call_backward(index, synth, inverse_table, field_in)
    return (field_out, spectrum)


def solution(mesh):
    placed = (P("lat", "ch", None), P(None, None, "ch", "lat"), P())
    return jax.shard_map(
        on_device,
        mesh=mesh,
        in_specs=placed,
        out_specs=(P("lat", "ch", None), P("lat", None, "ch", None)),
        check_vma=False,
    )
```

```python
import functools
import math

import jax
import jax.numpy as jnp
import numpy as np
from jax import lax
from jax.experimental import pallas as pl
from jax.experimental.pallas import tpu as pltpu
from jax.sharding import PartitionSpec as P

PAD = 16
PAIRS = 8
LANES = 128
NO_ORDER = 1000
PITCH = 17
RESCALE_BITS = 60
f32 = jnp.float32
bf16 = jnp.bfloat16


VMEM_MIB = 50
TABLE_MIB = 57


def cos_turns(turns):
    part = turns - jnp.floor(turns + 0.5)
    y = part * math.pi
    z = y * y
    s = 1.0 / 362880 - z * (1.0 / 39916800)
    s = -1.0 / 5040 + z * s
    s = 1.0 / 120 + z * s
    s = -1.0 / 6 + z * s
    s = y * (1.0 + z * s)
    return 1.0 - 2.0 * s * s


def minus_sin_turns(turns):
    return cos_turns(turns + 0.25)


def chunk_transpose(rows):
    lane = lax.broadcasted_iota(jnp.int32, rows[0].shape, 1)
    low = lane < 64
    even = (lane // 32) % 2 == 0
    mid = [None] * 4
    for i in range(2):
        a, b = rows[i], rows[i + 2]
        mid[i] = jnp.where(low, a, pltpu.roll(b, 64, 1))
        mid[i + 2] = jnp.where(low, pltpu.roll(a, 64, 1), b)
    out = []
    for i in (0, 2):
        a, b = mid[i], mid[i + 1]
        out.append(jnp.where(even, a, pltpu.roll(b, 32, 1)))
        out.append(jnp.where(even, pltpu.roll(a, 96, 1), b))
    return out


def digits_of(slots_ref):
    slots = slots_ref[...].astype(f32)
    high = jnp.floor(slots * (1.0 / PAD))
    return high.astype(bf16), (slots - PAD * high).astype(bf16)


def one_hot(hit):
    return jnp.where(hit, 1.0, 0.0).astype(bf16)


def slot_wanted(place, ord_dev, half):
    within = 2 * (place % PAIRS) + place // half
    return jnp.where(within < ord_dev, (place % half) // PAIRS * ord_dev + within, -1)


def order_lanes(slots_ref, ord_dev, lat_count):
    modes = slots_ref.shape[1]
    half = lat_count * PAIRS
    wanted = slot_wanted(lax.broadcasted_iota(jnp.int32, (1, 2 * half), 1), ord_dev, half)
    pick = one_hot(lax.broadcasted_iota(jnp.int32, (modes, 2 * half), 0) == wanted)
    digits = [jnp.broadcast_to(d.astype(f32), (8, modes)).astype(bf16) for d in digits_of(slots_ref)]
    high, low = [jnp.dot(d, pick, preferred_element_type=f32) for d in digits]
    return high[0:1] * PAD + low[0:1]


def order_rows(slots_ref, ord_dev, lat_count):
    modes = slots_ref.shape[1]
    half = lat_count * PAIRS
    wanted = slot_wanted(lax.broadcasted_iota(jnp.int32, (2 * half, 1), 0), ord_dev, half)
    pick = one_hot(lax.broadcasted_iota(jnp.int32, (2 * half, modes), 1) == wanted)
    contract = (((1,), (1,)), ((), ()))
    high, low = [
        lax.dot_general(
            pick,
            jnp.broadcast_to(d.astype(f32), (LANES, modes)).astype(bf16),
            contract,
            preferred_element_type=f32,
        )
        for d in digits_of(slots_ref)
    ]
    return high * PAD + low


def order_column(slots, wanted):
    place = lax.broadcasted_iota(jnp.int32, (wanted.shape[0], slots.shape[1]), 1)
    return jnp.sum(jnp.where(place == wanted, slots, 0.0), axis=1, keepdims=True)


def slot_of(j, lat_dev, index, lat_count):
    return jnp.where(index < lat_count // 2, j, lat_dev - 1 - j)


def narrow(wide, out_ref, out_hbm, sems):
    count = out_ref.shape[0]
    part = count // sems.shape[0]
    copies = []
    for d in range(count):
        for p in range(PAIRS):
            i = d * PAIRS + p
            out_ref[d, p] = wide[i * PITCH : i * PITCH + PAD, :].astype(bf16)
        if d % part == part - 1:
            cut = slice(d + 1 - part, d + 1)
            copies.append(pltpu.make_async_copy(out_ref.at[cut], out_hbm.at[cut], sems.at[d // part]))
            copies[-1].start()
    for copy in copies:
        copy.wait()


def forward_kernel(
    lat_dev, lat_count, ord_dev, index_ref, slots_ref, field_hbm, out_hbm, table, field_ref, rows, turned, out_ref, sem, sems
):
    fetch = pltpu.make_async_copy(field_hbm, field_ref, sem)
    fetch.start()
    lon = table.shape[0]
    half = table.shape[1] // 4
    order = order_lanes(slots_ref, ord_dev, lat_count)
    step_cos = cos_turns(order * (LANES / lon))
    step_sin = -minus_sin_turns(order * (LANES / lon))

    @pl.loop(0, LANES // PAD)
    def _(r):
        n = (lax.broadcasted_iota(jnp.int32, (PAD, order.shape[1]), 0) + r * PAD).astype(f32)
        turns = order * n * (1.0 / lon)
        re, im = cos_turns(turns), minus_sin_turns(turns)
        for k in range(lon // LANES):
            at = pl.ds(pl.multiple_of(k * LANES + r * PAD, PAD), PAD)
            for m2 in range(2):
                cut = slice(m2 * half, (m2 + 1) * half)
                table[at, 2 * m2 * half : (2 * m2 + 1) * half] = re[:, cut].astype(bf16)
                table[at, (2 * m2 + 1) * half : (2 * m2 + 2) * half] = im[:, cut].astype(bf16)
            re, im = re * step_cos + im * step_sin, im * step_cos - re * step_sin

    fetch.wait()
    ch_dev = field_ref.shape[1]
    field = field_ref[...].reshape(lat_dev * ch_dev, lon)
    for q in range(4):
        part = jnp.dot(field, table[:, q * half : (q + 1) * half], preferred_element_type=f32)
        rows[:, q] = part.reshape(lat_dev, ch_dev, half)
    index = index_ref[0]
    lat_total = lat_dev * lat_count
    for j in range(lat_dev):
        place = jnp.full((1, half), index * lat_dev + j, jnp.int32).astype(f32)
        quad = cos_turns((place + 0.5) * (0.5 / lat_total) - 0.25) * (math.pi / lat_total)
        block = rows[j].reshape(4 * ch_dev, half) * quad
        turned[pl.ds(slot_of(j, lat_dev, index, lat_count), half, stride=PITCH), :] = block.astype(bf16).T.astype(f32)
    turned[pl.ds(lat_dev, half, stride=PITCH), :] = jnp.zeros((half, LANES), f32)
    narrow(turned, out_ref, out_hbm, sems)


def inverse_table_kernel(ord_dev, lat_count, slots_ref, out_hbm, out_ref, orders, sem):
    lon = out_ref.shape[1]
    half = out_ref.shape[0] // 4
    steps = half // PAD
    orders[...] = order_rows(slots_ref, ord_dev, lat_count)

    @pl.loop(0, 2 * steps)
    def _(r):
        order = orders[pl.ds(pl.multiple_of(r * PAD, PAD), PAD), :]
        step_cos = cos_turns(order * (LANES / lon))
        step_sin = -minus_sin_turns(order * (LANES / lon))
        n = lax.broadcasted_iota(jnp.int32, (PAD, LANES), 1).astype(f32)
        turns = order * n * (1.0 / lon)
        re, im = cos_turns(turns), minus_sin_turns(turns)
        top = (r // steps) * (2 * half) + (r % steps) * PAD
        for k in range(lon // LANES):
            cut = slice(k * LANES, (k + 1) * LANES)
            out_ref[pl.ds(pl.multiple_of(top, PAD), PAD), cut] = re.astype(bf16)
            out_ref[pl.ds(pl.multiple_of(top + half, PAD), PAD), cut] = im.astype(bf16)
            re, im = re * step_cos + im * step_sin, im * step_cos - re * step_sin

    copy = pltpu.make_async_copy(out_ref, out_hbm, sem)
    copy.start()
    copy.wait()


def legendre_kernel(
    deg_dev, index_ref, slots_ref, geo_ref, prod_ref, out_hbm, cur, bef, resc, start, expo, buf, table, sems
):
    groups = cur.shape[0]
    pitch = 2 * PAD + 1
    log_step = RESCALE_BITS * math.log(2.0)
    shrink = 2.0 ** (-RESCALE_BITS)
    limit = 2.0**RESCALE_BITS
    row = lax.broadcasted_iota(jnp.int32, (PAD, 1), 0)
    order = order_column(slots_ref[...].astype(f32), jnp.where(row < deg_dev, index_ref[0] * deg_dev + row, -1))
    order = jnp.broadcast_to(jnp.where(row < deg_dev, order, 1.0 * NO_ORDER), (PAD, LANES))
    order_sq = order * order
    for state in (cur, bef, resc):
        state[...] = jnp.zeros_like(state)
    picked = jnp.zeros((PAD, 1), f32)
    for g in range(prod_ref.shape[1] // LANES):
        lane = lax.broadcasted_iota(jnp.int32, (PAD, LANES), 1) + g * LANES
        hit = order == lane.astype(f32)
        term = jnp.where(hit, prod_ref[:, g * LANES : (g + 1) * LANES], 0.0)
        picked = picked + jnp.sum(term, axis=1, keepdims=True)
    head = 0.5 * jnp.log(order + 0.5) + picked
    for g in range(groups):
        log_start = head + order * geo_ref[1:2, g * LANES : (g + 1) * LANES]
        start[g] = log_start
        expo[g] = jnp.exp(log_start)
        for twin in range(2):
            buf[g, pl.ds(PAD + twin * PAIRS + PAIRS - 1, PAD, stride=pitch), :] = jnp.zeros((PAD, LANES), f32)

    def block(index):
        now = [cur[g] for g in range(groups)]
        old = [bef[g] for g in range(groups)]
        factor = [expo[g] for g in range(groups)]
        cosine = [geo_ref[0:1, g * LANES : (g + 1) * LANES] for g in range(groups)]
        lane = lax.broadcasted_iota(jnp.int32, (PAD, LANES), 1) + 2 * index * deg_dev
        degs = lane.astype(f32)
        prev = degs - 1.0
        alphas = jnp.sqrt(
            jnp.maximum(4.0 * degs * degs - 1.0, 1.0) / jnp.maximum(degs * degs - order_sq, 1.0)
        )
        betas = jnp.sqrt(
            jnp.maximum(prev * prev - order_sq, 0.0) / jnp.maximum(4.0 * prev * prev - 1.0, 1.0)
        )
        for twin, i in [(t, k) for t in range(2) for k in range(deg_dev)]:
            at = twin * deg_dev + i
            alpha = jnp.broadcast_to(alphas[:, at : at + 1], (PAD, LANES))
            beta = jnp.broadcast_to(betas[:, at : at + 1], (PAD, LANES))
            both = alpha * beta
            begin = jnp.where(order == (2 * index * deg_dev + at).astype(f32), 1.0, 0.0)
            for g in range(groups):
                new = (alpha * cosine[g]) * now[g] + (begin - both * old[g])
                old[g], now[g] = now[g], new
                row = i % 2 * PAD + twin * PAIRS + i // 2
                buf[g, pl.ds(row, PAD, stride=pitch), :] = new * factor[g]
            if i in (deg_dev // 2, deg_dev - 1):
                for g in range(groups):
                    large = jnp.abs(now[g]) > limit
                    ratio = jnp.where(large, shrink, 1.0)
                    now[g] = now[g] * ratio
                    old[g] = old[g] * ratio
                    count = resc[g] + jnp.where(large, 1.0, 0.0)
                    resc[g] = count
                    factor[g] = jnp.exp(start[g] + count * log_step)
        for g in range(groups):
            cur[g] = now[g]
            bef[g] = old[g]
            expo[g] = factor[g]
            for m in range(PAD):
                for side in range(2):
                    row = m * pitch + side * PAD
                    tile = buf[g, row : row + PAD, :].astype(bf16)
                    table[m, side, index, :, g * LANES : (g + 1) * LANES] = tile

    parts = sems.shape[0]
    count = table.shape[2] // parts
    copies = []
    for part in range(parts):
        pl.loop(part * count, (part + 1) * count)(block)
        cut = slice(part * count, (part + 1) * count)
        copies.append(pltpu.make_async_copy(table.at[:, :, cut], out_hbm.at[:, :, cut], sems.at[part]))
        copies[-1].start()
    for copy in copies:
        copy.wait()


def degree_parity(shape, dim, deg_dev):
    half = shape[dim] // 2
    i = lax.broadcasted_iota(jnp.int32, shape, dim)
    return ((i % half) // PAIRS * deg_dev + i // half) & 1


def order_of(slots_ref, index_ref, ord_dev, m):
    return slots_ref[index_ref[0] * ord_dev + jnp.minimum(m, ord_dev - 1)]


def fetch_pairs(table_hbm, table, sems):
    def copy(p):
        cut = pl.ds(2 * p, 2)
        return pltpu.make_async_copy(table_hbm.at[cut], table.at[cut], sems.at[p])

    for p in range(PAIRS):
        copy(p).start()
    return copy


def analysis_kernel(
    ord_dev, index_ref, slots_ref, rows_ref, table_hbm, out_hbm, table, wide, sems, out_ref, leave
):
    copy = fetch_pairs(table_hbm, table, sems)
    count = rows_ref.shape[0]
    half = count * PAIRS
    parity = degree_parity((table.shape[1], LANES), 0, ord_dev)

    @pl.loop(0, PAIRS)
    def _(p):
        north = jnp.concatenate([rows_ref[s, p] for s in range(count // 2)], axis=0)
        south = jnp.concatenate([rows_ref[count - 1 - s, p] for s in range(count // 2)], axis=0)
        both = jnp.concatenate([north, south], axis=1)
        copy(p).wait()
        for m2 in range(2):
            order = order_of(slots_ref, index_ref, ord_dev, 2 * p + m2)
            prod = jnp.dot(table[2 * p + m2], both, preferred_element_type=f32)
            mirror = prod[:, LANES:]
            coefs = prod[:, :LANES] + jnp.where(parity == (order & 1), mirror, -mirror)
            low, high = coefs[:half], coefs[half:]
            if m2 == 0:
                high = pltpu.roll(high, LANES // 2, 1)
            else:
                low = pltpu.roll(low, LANES // 2, 1)
            lane = lax.broadcasted_iota(jnp.int32, low.shape, 1)
            wide[pl.ds(2 * p + m2, half, stride=PITCH), :] = jnp.where(lane < LANES // 2, low, high)

    narrow(wide, out_ref, out_hbm, leave)


def weights_kernel(index_ref, weight_ref, *out_refs):
    ch_count = len(out_refs)
    last = weight_ref.shape[1] - 1
    for k, out_ref in enumerate(out_refs):
        there = lax.rem(index_ref[0] + k, ch_count)
        for w in range(2):
            for l2 in range(2):
                out_ref[w, l2] = weight_ref[w, jnp.minimum(2 * there + l2, last)]


def mix_kernel(index_ref, coef_ref, *refs):
    ch_count = len(refs) - 3
    out_ref, weight, sems = refs[ch_count:]
    copies = []
    for k in range(ch_count):
        source = lax.rem(index_ref[0] + ch_count - k, ch_count)
        copies.append(pltpu.make_async_copy(refs[k], weight.at[source], sems.at[k]))
        copies[-1].start()
    for copy in copies:
        copy.wait()
    bands = coef_ref.shape[0]
    ch_dev = LANES // 4
    channels = ch_count * ch_dev
    contract = (((1,), (1,)), ((), ()))
    step = MIX_BANDS
    count = step * PAD

    @pl.loop(0, bands // step)
    def _(chunk):
        here = pl.ds(chunk * step, step)
        groups = []
        for h in range(ch_count // 4):
            quads = [coef_ref[here, 4 * h + e].reshape(count, LANES).astype(f32) for e in range(4)]
            groups.append(chunk_transpose(quads))
        results = []
        for l2 in range(2):
            left = jnp.concatenate(
                [jnp.concatenate([g[2 * l2 + x] for g in groups], axis=1) for x in range(2)], axis=0
            ).astype(bf16)
            prod = [
                lax.dot_general(
                    left,
                    weight[:, w, l2].reshape(channels, channels),
                    contract,
                    preferred_element_type=f32,
                )
                for w in range(2)
            ]
            results.append(prod[0][:count] - prod[1][count:])
            results.append(prod[1][:count] + prod[0][count:])
        for h in range(ch_count // 4):
            quads = chunk_transpose([r[:, h * LANES : (h + 1) * LANES] for r in results])
            for e in range(4):
                out_ref[here, 4 * h + e] = quads[e].astype(bf16).reshape(step, PAD, LANES)


def widen(mixed_ref, wide):
    for i in range(mixed_ref.shape[0] * PAIRS):
        wide[i * PITCH : i * PITCH + PAD, :] = mixed_ref[i // PAIRS, i % PAIRS].astype(f32)


def side_of(wide, count, m):
    turned = wide[pl.ds(m, count * PAIRS, stride=PITCH), :].astype(bf16).T
    return jnp.concatenate([turned[: LANES // 2], turned[LANES // 2 :]], axis=1)


def synthesis_kernel(ord_dev, lon, index_ref, slots_ref, mixed_ref, table_hbm, out_hbm, table, wide, sems, out_ref, leave):
    copy = fetch_pairs(table_hbm, table, sems)
    widen(mixed_ref, wide)
    count = out_ref.shape[0]
    half = LANES // 2
    parity = degree_parity((half, table.shape[1]), 1, ord_dev)

    def sent(p):
        return pltpu.make_async_copy(out_ref.at[:, p], out_hbm.at[:, p], leave.at[p])

    @pl.loop(0, PAIRS)
    def _(p):
        copy(p).wait()
        north, south = [], []
        for m2 in range(2):
            order = order_of(slots_ref, index_ref, ord_dev, 2 * p + m2)
            weight = jnp.where(order == 0, 1.0 / lon, 2.0 / lon)
            part = side_of(wide, count, 2 * p + m2).astype(f32)
            same = parity == (order & 1)
            split = jnp.concatenate([jnp.where(same, part, 0.0), jnp.where(same, 0.0, part)], axis=0)
            prod = jnp.dot(split.astype(bf16), table[2 * p + m2], preferred_element_type=f32)
            north.append((prod[:half] + prod[half:]) * weight)
            south.append((prod[:half] - prod[half:]) * weight)
        up = jnp.concatenate(north, axis=0).astype(bf16).T
        down = jnp.concatenate(south, axis=0).astype(bf16).T
        for s in range(count // 2):
            out_ref[s, p] = up[s * PAD : (s + 1) * PAD]
            out_ref[count - 1 - s, p] = down[s * PAD : (s + 1) * PAD]
        sent(p).start()

    for p in range(PAIRS):
        sent(p).wait()


def spectrum_kernel(ord_dev, mixed_ref, pick_ref, out_ref, wide):
    count = mixed_ref.shape[0]
    widen(mixed_ref, wide)

    @pl.loop(0, ord_dev)
    def _(m):
        side = side_of(wide, count, m)
        spec = jnp.dot(side, pick_ref[...], preferred_element_type=f32).astype(bf16)
        out_ref[m] = spec.reshape(out_ref.shape[1:])


def backward_kernel(
    lat_dev, lat_count, index_ref, rows_ref, table_hbm, field_hbm, out_ref, wide, left, table_ref, field_ref, sems
):
    copies = [
        pltpu.make_async_copy(table_hbm, table_ref, sems.at[0]),
        pltpu.make_async_copy(field_hbm, field_ref, sems.at[1]),
    ]
    for copy in copies:
        copy.start()
    half = rows_ref.shape[0] * rows_ref.shape[1]
    ch_dev = LANES // 4
    for i in range(half):
        wide[i * PITCH : i * PITCH + PAD, :] = rows_ref[i // PAIRS, i % PAIRS].astype(f32)
    for j in range(lat_dev):
        slot = slot_of(j, lat_dev, index_ref[0], lat_count)
        block = wide[pl.ds(slot, half, stride=PITCH), :].astype(bf16).T
        for q in range(4):
            left[j * ch_dev : (j + 1) * ch_dev, q * half : (q + 1) * half] = block[
                q * ch_dev : (q + 1) * ch_dev
            ]
    lon = out_ref.shape[2]
    for copy in copies:
        copy.wait()
    for b in range(4):
        cut = slice(b * lon // 4, (b + 1) * lon // 4)
        wave = jnp.dot(left[...], table_ref[:, cut], preferred_element_type=f32)
        cubic = wave * wave * wave
        grown = 0.5 * wave * (1.0 + jnp.tanh(math.sqrt(2.0 / math.pi) * (wave + 0.044715 * cubic)))
        field = field_ref[:, :, cut].astype(f32)
        out_ref[:, :, cut] = (field + grown.reshape(field.shape)).astype(bf16)


def params(mib=VMEM_MIB):
    return pltpu.CompilerParams(vmem_limit_bytes=int(mib * 2**20))


def cost(flops, moved):
    return pl.CostEstimate(flops=int(flops), bytes_accessed=int(moved), transcendentals=0)


MIX_BANDS = 16
vmem = pl.BlockSpec(memory_space=pltpu.VMEM)
smem = pl.BlockSpec(memory_space=pltpu.SMEM)
hbm = pl.BlockSpec(memory_space=pltpu.HBM)


def buffer_of(lat_count):
    return jax.ShapeDtypeStruct((lat_count, PAIRS, PAD, LANES), bf16)


def call_forward(lat_count, index, slots, field_in):
    lat_dev, ch_dev, lon = field_in.shape
    half = lat_count * PAIRS
    return pl.pallas_call(
        functools.partial(forward_kernel, lat_dev, lat_count, slots.shape[1] // lat_count),
        out_shape=buffer_of(lat_count),
        in_specs=[smem, vmem, hbm],
        out_specs=hbm,
        scratch_shapes=[
            pltpu.VMEM((lon, 4 * half), bf16),
            pltpu.VMEM(field_in.shape, bf16),
            pltpu.VMEM((lat_dev, 4, ch_dev, half), f32),
            pltpu.VMEM((half * PITCH, LANES), f32),
            pltpu.VMEM((lat_count, PAIRS, PAD, LANES), bf16),
            pltpu.SemaphoreType.DMA,
            pltpu.SemaphoreType.DMA((4,)),
        ],
        compiler_params=params(TABLE_MIB),
        name="forward",
    )(index, slots, field_in)


def call_legendre(lat_count, lat_dev, index, slots):
    lat_total = lat_count * lat_dev
    modes = slots.shape[1]
    ord_dev = modes // lat_count
    full = lat_count * PAD
    near = full // 2
    angle = math.pi * (np.arange(lat_total) + 0.5) / lat_total
    geo = np.zeros((2, lat_count, PAD), np.float32)
    geo[0, :, :lat_dev] = np.cos(angle).reshape(lat_count, lat_dev)
    geo[1, :, :lat_dev] = np.log(np.sin(angle)).reshape(lat_count, lat_dev)
    geo = geo.reshape(2, full)[:, :near]
    k = np.arange(1, modes)
    prod = np.zeros((1, full), np.float32)
    prod[0, 1:modes] = np.cumsum(0.5 * np.log((2.0 * k - 1.0) / (2.0 * k)))
    groups = near // LANES
    parts = 4
    state = pltpu.VMEM((groups, PAD, LANES), f32)
    table = pl.pallas_call(
        functools.partial(legendre_kernel, ord_dev),
        out_shape=jax.ShapeDtypeStruct((PAD, 2, lat_count // 2, PAD, near), bf16),
        in_specs=[smem, vmem, vmem, vmem],
        out_specs=hbm,
        scratch_shapes=[state] * 5
        + [
            pltpu.VMEM((groups, PAD * (2 * PAD + 1), LANES), f32),
            pltpu.VMEM((PAD, 2, lat_count // 2, PAD, near), bf16),
            pltpu.SemaphoreType.DMA((parts,)),
        ],
        compiler_params=params(TABLE_MIB),
        cost_estimate=cost(8e9, 2e7),
        name="legendre",
    )(index, slots, jnp.asarray(geo), jnp.asarray(prod))
    return table.reshape(PAD, full, near)


def call_inverse_table(lat_count, lon, slots):
    half = lat_count * PAIRS
    return pl.pallas_call(
        functools.partial(inverse_table_kernel, slots.shape[1] // lat_count, lat_count),
        out_shape=jax.ShapeDtypeStruct((4 * half, lon), bf16),
        in_specs=[vmem],
        out_specs=hbm,
        scratch_shapes=[
            pltpu.VMEM((4 * half, lon), bf16),
            pltpu.VMEM((2 * half, LANES), f32),
            pltpu.SemaphoreType.DMA,
        ],
        compiler_params=params(TABLE_MIB),
        cost_estimate=cost(2e9, 4e6),
        name="inverse_table",
    )(slots)


def call_analysis(ord_dev, index, orders, rows, table):
    lat_count = rows.shape[0]
    return pl.pallas_call(
        functools.partial(analysis_kernel, ord_dev),
        out_shape=jax.ShapeDtypeStruct(rows.shape, bf16),
        in_specs=[smem, smem, vmem, hbm],
        out_specs=hbm,
        scratch_shapes=[
            pltpu.VMEM(table.shape, bf16),
            pltpu.VMEM((lat_count * PAIRS * PITCH, LANES), f32),
            pltpu.SemaphoreType.DMA((PAIRS,)),
            pltpu.VMEM((lat_count, PAIRS, PAD, LANES), bf16),
            pltpu.SemaphoreType.DMA((4,)),
        ],
        compiler_params=params(),
        name="analysis",
    )(index, orders, rows, table)


def weight_pieces(index, weights, ch_count):
    piece = jax.ShapeDtypeStruct((2, 2) + weights.shape[2:], bf16)
    return pl.pallas_call(
        weights_kernel,
        out_shape=(piece,) * ch_count,
        in_specs=[smem, vmem],
        out_specs=(vmem,) * ch_count,
        compiler_params=params(),
        name="weights",
    )(index, weights)


def move_along(pieces, steps):
    count = len(pieces)
    pieces = list(pieces)
    for k in steps:
        pieces[k] = lax.ppermute(pieces[k], "ch", [(e, (e + k) % count) for e in range(count)])
    return tuple(pieces)


def call_mix(index, coeffs, weights):
    ch_count = len(weights)
    return pl.pallas_call(
        mix_kernel,
        out_shape=jax.ShapeDtypeStruct(coeffs.shape, bf16),
        in_specs=[smem, vmem] + [hbm] * ch_count,
        out_specs=vmem,
        scratch_shapes=[
            pltpu.VMEM((ch_count,) + weights[0].shape, bf16),
            pltpu.SemaphoreType.DMA((ch_count,)),
        ],
        compiler_params=params(),
        name="mix",
    )(index, coeffs, *weights)


def call_synthesis(ord_dev, lon, index, orders, mixed, table):
    lat_count = mixed.shape[0]
    return pl.pallas_call(
        functools.partial(synthesis_kernel, ord_dev, lon),
        out_shape=buffer_of(mixed.shape[0]),
        in_specs=[smem, smem, vmem, hbm],
        out_specs=hbm,
        scratch_shapes=[
            pltpu.VMEM(table.shape, bf16),
            pltpu.VMEM((lat_count * PAIRS * PITCH, LANES), f32),
            pltpu.SemaphoreType.DMA((PAIRS,)),
            pltpu.VMEM((lat_count, PAIRS, PAD, LANES), bf16),
            pltpu.SemaphoreType.DMA((PAIRS,)),
        ],
        compiler_params=params(),
        name="synthesis",
    )(index, orders, mixed, table)


def call_spectrum(ord_dev, mixed):
    lat_count = mixed.shape[0]
    modes = ord_dev * lat_count
    pick = np.zeros((lat_count, PAD, modes), np.float32)
    pick[:, :ord_dev] = np.eye(modes, dtype=np.float32).reshape(lat_count, ord_dev, modes)
    pick = pick.reshape(lat_count * PAIRS, 2, modes).transpose(1, 0, 2)
    pick = jnp.asarray(pick.reshape(lat_count * PAD, modes), bf16)
    return pl.pallas_call(
        functools.partial(spectrum_kernel, ord_dev),
        out_shape=jax.ShapeDtypeStruct((ord_dev, 2, LANES // 4, modes), bf16),
        in_specs=[vmem, vmem],
        out_specs=vmem,
        scratch_shapes=[pltpu.VMEM((lat_count * PAIRS * PITCH, LANES), f32)],
        compiler_params=params(),
        cost_estimate=cost(3e9, 4e6),
        name="spectrum",
    )(mixed, pick)


def call_backward(index, rows, table, field_in):
    lat_dev, ch_dev, _ = field_in.shape
    lat_count = rows.shape[0]
    half = lat_count * PAIRS
    return pl.pallas_call(
        functools.partial(backward_kernel, lat_dev, lat_count),
        out_shape=jax.ShapeDtypeStruct(field_in.shape, bf16),
        in_specs=[smem, vmem, hbm, hbm],
        out_specs=vmem,
        scratch_shapes=[
            pltpu.VMEM((half * PITCH, LANES), f32),
            pltpu.VMEM((lat_dev * ch_dev, 4 * half), bf16),
            pltpu.VMEM(table.shape, bf16),
            pltpu.VMEM(field_in.shape, bf16),
            pltpu.SemaphoreType.DMA((2,)),
        ],
        compiler_params=params(),
        name="backward",
    )(index, rows, table, field_in)


def on_device(field_in, mix_weight, order_slots):
    lat_dev, _, lon = field_in.shape
    lat_count = lax.axis_size("lat")
    modes = order_slots.shape[0]
    ord_dev = modes // lat_count
    index = lax.axis_index("lat")
    index = index.reshape(1)
    slots = order_slots.reshape(1, modes)

    rows = call_forward(lat_count, index, slots, field_in)
    rows = lax.all_to_all(rows, "lat", 0, 0, tiled=True)
    legendre = call_legendre(lat_count, lat_dev, index, slots)
    weights = jnp.transpose(mix_weight, (0, 3, 2, 1))
    weights, legendre = lax.optimization_barrier((weights, legendre))
    ch_index = lax.axis_index("ch").reshape(1)
    ch_count = lax.axis_size("ch")
    far = sorted(range(1, ch_count), key=lambda k: -min(k, ch_count - k))[: ch_count // 2 - 1]
    near = [k for k in range(1, ch_count) if k not in far]
    weights = move_along(weight_pieces(ch_index, weights, ch_count), far)
    coeffs = call_analysis(ord_dev, index, order_slots, rows, legendre)
    coeffs, weights = lax.optimization_barrier((coeffs, weights))
    weights = move_along(weights, near)
    coeffs = lax.all_to_all(coeffs.reshape(-1, PAD, LANES), ("lat", "ch"), 0, 0, tiled=True)
    mixed = call_mix(ch_index, coeffs.reshape(rows.shape), weights)
    mixed = lax.all_to_all(mixed.reshape(-1, PAD, LANES), ("lat", "ch"), 0, 0, tiled=True).reshape(rows.shape)
    synth = call_synthesis(ord_dev, lon, index, order_slots, mixed, legendre)
    synth = lax.all_to_all(synth, "lat", 0, 0, tiled=True)
    spectrum = call_spectrum(ord_dev, mixed)
    inverse_table = call_inverse_table(lat_count, lon, slots)
    field_out = call_backward(index, synth, inverse_table, field_in)
    return (field_out, spectrum)


def solution(mesh):
    placed = (P("lat", "ch", None), P(None, None, "ch", "lat"), P())
    return jax.shard_map(
        on_device,
        mesh=mesh,
        in_specs=placed,
        out_specs=(P("lat", "ch", None), P("lat", None, "ch", None)),
        check_vma=False,
    )
```

```python
import functools
import math

import jax
import jax.numpy as jnp
import numpy as np
from jax import lax
from jax.experimental import pallas as pl
from jax.experimental.pallas import tpu as pltpu
from jax.sharding import PartitionSpec as P

PAD = 16
PAIRS = 8
LANES = 128
NO_ORDER = 1000
PITCH = 17
RESCALE_BITS = 60
f32 = jnp.float32
bf16 = jnp.bfloat16


VMEM_MIB = 50
TABLE_MIB = 57


def cos_turns(turns):
    part = turns - jnp.floor(turns + 0.5)
    y = part * math.pi
    z = y * y
    s = 1.0 / 362880 - z * (1.0 / 39916800)
    s = -1.0 / 5040 + z * s
    s = 1.0 / 120 + z * s
    s = -1.0 / 6 + z * s
    s = y * (1.0 + z * s)
    return 1.0 - 2.0 * s * s


def minus_sin_turns(turns):
    return cos_turns(turns + 0.25)


def chunk_transpose(rows):
    lane = lax.broadcasted_iota(jnp.int32, rows[0].shape, 1)
    low = lane < 64
    even = (lane // 32) % 2 == 0
    mid = [None] * 4
    for i in range(2):
        a, b = rows[i], rows[i + 2]
        mid[i] = jnp.where(low, a, pltpu.roll(b, 64, 1))
        mid[i + 2] = jnp.where(low, pltpu.roll(a, 64, 1), b)
    out = []
    for i in (0, 2):
        a, b = mid[i], mid[i + 1]
        out.append(jnp.where(even, a, pltpu.roll(b, 32, 1)))
        out.append(jnp.where(even, pltpu.roll(a, 96, 1), b))
    return out


def digits_of(slots_ref):
    slots = slots_ref[...].astype(f32)
    high = jnp.floor(slots * (1.0 / PAD))
    return high.astype(bf16), (slots - PAD * high).astype(bf16)


def one_hot(hit):
    return jnp.where(hit, 1.0, 0.0).astype(bf16)


def slot_wanted(place, ord_dev, half):
    within = 2 * (place % PAIRS) + place // half
    return jnp.where(within < ord_dev, (place % half) // PAIRS * ord_dev + within, -1)


def order_lanes(slots_ref, ord_dev, lat_count):
    modes = slots_ref.shape[1]
    half = lat_count * PAIRS
    wanted = slot_wanted(lax.broadcasted_iota(jnp.int32, (1, 2 * half), 1), ord_dev, half)
    pick = one_hot(lax.broadcasted_iota(jnp.int32, (modes, 2 * half), 0) == wanted)
    digits = [jnp.broadcast_to(d.astype(f32), (8, modes)).astype(bf16) for d in digits_of(slots_ref)]
    high, low = [jnp.dot(d, pick, preferred_element_type=f32) for d in digits]
    return high[0:1] * PAD + low[0:1]


def order_rows(slots_ref, ord_dev, lat_count):
    modes = slots_ref.shape[1]
    half = lat_count * PAIRS
    wanted = slot_wanted(lax.broadcasted_iota(jnp.int32, (2 * half, 1), 0), ord_dev, half)
    pick = one_hot(lax.broadcasted_iota(jnp.int32, (2 * half, modes), 1) == wanted)
    contract = (((1,), (1,)), ((), ()))
    high, low = [
        lax.dot_general(
            pick,
            jnp.broadcast_to(d.astype(f32), (LANES, modes)).astype(bf16),
            contract,
            preferred_element_type=f32,
        )
        for d in digits_of(slots_ref)
    ]
    return high * PAD + low


def order_column(slots, wanted):
    place = lax.broadcasted_iota(jnp.int32, (wanted.shape[0], slots.shape[1]), 1)
    return jnp.sum(jnp.where(place == wanted, slots, 0.0), axis=1, keepdims=True)


def slot_of(j, lat_dev, index, lat_count):
    return jnp.where(index < lat_count // 2, j, lat_dev - 1 - j)


def narrow(wide, out_ref, out_hbm, sems):
    count = out_ref.shape[0]
    part = count // sems.shape[0]
    copies = []
    for d in range(count):
        for p in range(PAIRS):
            i = d * PAIRS + p
            out_ref[d, p] = wide[i * PITCH : i * PITCH + PAD, :].astype(bf16)
        if d % part == part - 1:
            cut = slice(d + 1 - part, d + 1)
            copies.append(pltpu.make_async_copy(out_ref.at[cut], out_hbm.at[cut], sems.at[d // part]))
            copies[-1].start()
    for copy in copies:
        copy.wait()


def forward_kernel(
    lat_dev, lat_count, ord_dev, index_ref, slots_ref, field_hbm, out_hbm, table, field_ref, rows, turned, out_ref, sem, sems
):
    fetch = pltpu.make_async_copy(field_hbm, field_ref, sem)
    fetch.start()
    lon = table.shape[0]
    half = table.shape[1] // 4
    order = order_lanes(slots_ref, ord_dev, lat_count)
    step_cos = cos_turns(order * (LANES / lon))
    step_sin = -minus_sin_turns(order * (LANES / lon))

    @pl.loop(0, LANES // PAD)
    def _(r):
        n = (lax.broadcasted_iota(jnp.int32, (PAD, order.shape[1]), 0) + r * PAD).astype(f32)
        turns = order * n * (1.0 / lon)
        re, im = cos_turns(turns), minus_sin_turns(turns)
        for k in range(lon // LANES):
            at = pl.ds(pl.multiple_of(k * LANES + r * PAD, PAD), PAD)
            for m2 in range(2):
                cut = slice(m2 * half, (m2 + 1) * half)
                table[at, 2 * m2 * half : (2 * m2 + 1) * half] = re[:, cut].astype(bf16)
                table[at, (2 * m2 + 1) * half : (2 * m2 + 2) * half] = im[:, cut].astype(bf16)
            re, im = re * step_cos + im * step_sin, im * step_cos - re * step_sin

    fetch.wait()
    ch_dev = field_ref.shape[1]
    field = field_ref[...].reshape(lat_dev * ch_dev, lon)
    for q in range(4):
        part = jnp.dot(field, table[:, q * half : (q + 1) * half], preferred_element_type=f32)
        rows[:, q] = part.reshape(lat_dev, ch_dev, half)
    index = index_ref[0]
    lat_total = lat_dev * lat_count
    for j in range(lat_dev):
        place = jnp.full((1, half), index * lat_dev + j, jnp.int32).astype(f32)
        quad = cos_turns((place + 0.5) * (0.5 / lat_total) - 0.25) * (math.pi / lat_total)
        block = rows[j].reshape(4 * ch_dev, half) * quad
        turned[pl.ds(slot_of(j, lat_dev, index, lat_count), half, stride=PITCH), :] = block.astype(bf16).T.astype(f32)
    turned[pl.ds(lat_dev, half, stride=PITCH), :] = jnp.zeros((half, LANES), f32)
    narrow(turned, out_ref, out_hbm, sems)


def inverse_table_kernel(ord_dev, lat_count, slots_ref, out_hbm, out_ref, orders, sem):
    lon = out_ref.shape[1]
    half = out_ref.shape[0] // 4
    steps = half // PAD
    orders[...] = order_rows(slots_ref, ord_dev, lat_count)

    @pl.loop(0, 2 * steps)
    def _(r):
        order = orders[pl.ds(pl.multiple_of(r * PAD, PAD), PAD), :]
        step_cos = cos_turns(order * (LANES / lon))
        step_sin = -minus_sin_turns(order * (LANES / lon))
        n = lax.broadcasted_iota(jnp.int32, (PAD, LANES), 1).astype(f32)
        turns = order * n * (1.0 / lon)
        re, im = cos_turns(turns), minus_sin_turns(turns)
        top = (r // steps) * (2 * half) + (r % steps) * PAD
        for k in range(lon // LANES):
            cut = slice(k * LANES, (k + 1) * LANES)
            out_ref[pl.ds(pl.multiple_of(top, PAD), PAD), cut] = re.astype(bf16)
            out_ref[pl.ds(pl.multiple_of(top + half, PAD), PAD), cut] = im.astype(bf16)
            re, im = re * step_cos + im * step_sin, im * step_cos - re * step_sin

    copy = pltpu.make_async_copy(out_ref, out_hbm, sem)
    copy.start()
    copy.wait()


def legendre_kernel(
    deg_dev, index_ref, slots_ref, geo_ref, prod_ref, out_hbm, cur, bef, resc, start, expo, buf, table, sems
):
    groups = cur.shape[0]
    pitch = 2 * PAD + 1
    log_step = RESCALE_BITS * math.log(2.0)
    shrink = 2.0 ** (-RESCALE_BITS)
    limit = 2.0**RESCALE_BITS
    row = lax.broadcasted_iota(jnp.int32, (PAD, 1), 0)
    order = order_column(slots_ref[...].astype(f32), jnp.where(row < deg_dev, index_ref[0] * deg_dev + row, -1))
    order = jnp.broadcast_to(jnp.where(row < deg_dev, order, 1.0 * NO_ORDER), (PAD, LANES))
    order_sq = order * order
    for state in (cur, bef, resc):
        state[...] = jnp.zeros_like(state)
    picked = jnp.zeros((PAD, 1), f32)
    for g in range(prod_ref.shape[1] // LANES):
        lane = lax.broadcasted_iota(jnp.int32, (PAD, LANES), 1) + g * LANES
        hit = order == lane.astype(f32)
        term = jnp.where(hit, prod_ref[:, g * LANES : (g + 1) * LANES], 0.0)
        picked = picked + jnp.sum(term, axis=1, keepdims=True)
    head = 0.5 * jnp.log(order + 0.5) + picked
    for g in range(groups):
        log_start = head + order * geo_ref[1:2, g * LANES : (g + 1) * LANES]
        start[g] = log_start
        expo[g] = jnp.exp(log_start)
        for twin in range(2):
            buf[g, pl.ds(PAD + twin * PAIRS + PAIRS - 1, PAD, stride=pitch), :] = jnp.zeros((PAD, LANES), f32)

    def block(index):
        now = [cur[g] for g in range(groups)]
        old = [bef[g] for g in range(groups)]
        factor = [expo[g] for g in range(groups)]
        cosine = [geo_ref[0:1, g * LANES : (g + 1) * LANES] for g in range(groups)]
        lane = lax.broadcasted_iota(jnp.int32, (PAD, LANES), 1) + 2 * index * deg_dev
        degs = lane.astype(f32)
        prev = degs - 1.0
        alphas = jnp.sqrt(
            jnp.maximum(4.0 * degs * degs - 1.0, 1.0) / jnp.maximum(degs * degs - order_sq, 1.0)
        )
        betas = jnp.sqrt(
            jnp.maximum(prev * prev - order_sq, 0.0) / jnp.maximum(4.0 * prev * prev - 1.0, 1.0)
        )
        for twin, i in [(t, k) for t in range(2) for k in range(deg_dev)]:
            at = twin * deg_dev + i
            alpha = jnp.broadcast_to(alphas[:, at : at + 1], (PAD, LANES))
            beta = jnp.broadcast_to(betas[:, at : at + 1], (PAD, LANES))
            both = alpha * beta
            begin = jnp.where(order == (2 * index * deg_dev + at).astype(f32), 1.0, 0.0)
            for g in range(groups):
                new = (alpha * cosine[g]) * now[g] + (begin - both * old[g])
                old[g], now[g] = now[g], new
                row = i % 2 * PAD + twin * PAIRS + i // 2
                buf[g, pl.ds(row, PAD, stride=pitch), :] = new * factor[g]
            if i in (deg_dev // 2, deg_dev - 1):
                for g in range(groups):
                    large = jnp.abs(now[g]) > limit
                    ratio = jnp.where(large, shrink, 1.0)
                    now[g] = now[g] * ratio
                    old[g] = old[g] * ratio
                    count = resc[g] + jnp.where(large, 1.0, 0.0)
                    resc[g] = count
                    factor[g] = jnp.exp(start[g] + count * log_step)
        for g in range(groups):
            cur[g] = now[g]
            bef[g] = old[g]
            expo[g] = factor[g]
            for m in range(PAD):
                for side in range(2):
                    row = m * pitch + side * PAD
                    tile = buf[g, row : row + PAD, :].astype(bf16)
                    table[m, side, index, :, g * LANES : (g + 1) * LANES] = tile

    parts = sems.shape[0]
    count = table.shape[2] // parts
    copies = []
    for part in range(parts):
        pl.loop(part * count, (part + 1) * count)(block)
        cut = slice(part * count, (part + 1) * count)
        copies.append(pltpu.make_async_copy(table.at[:, :, cut], out_hbm.at[:, :, cut], sems.at[part]))
        copies[-1].start()
    for copy in copies:
        copy.wait()


def degree_parity(shape, dim, deg_dev):
    half = shape[dim] // 2
    i = lax.broadcasted_iota(jnp.int32, shape, dim)
    return ((i % half) // PAIRS * deg_dev + i // half) & 1


def order_of(slots_ref, index_ref, ord_dev, m):
    return slots_ref[index_ref[0] * ord_dev + jnp.minimum(m, ord_dev - 1)]


def fetch_pairs(table_hbm, table, sems):
    def copy(p):
        cut = pl.ds(2 * p, 2)
        return pltpu.make_async_copy(table_hbm.at[cut], table.at[cut], sems.at[p])

    for p in range(PAIRS):
        copy(p).start()
    return copy


def analysis_kernel(
    ord_dev, index_ref, slots_ref, rows_ref, table_hbm, out_hbm, table, wide, sems, out_ref, leave
):
    copy = fetch_pairs(table_hbm, table, sems)
    count = rows_ref.shape[0]
    half = count * PAIRS
    parity = degree_parity((table.shape[1], LANES), 0, ord_dev)

    @pl.loop(0, PAIRS)
    def _(p):
        north = jnp.concatenate([rows_ref[s, p] for s in range(count // 2)], axis=0)
        south = jnp.concatenate([rows_ref[count - 1 - s, p] for s in range(count // 2)], axis=0)
        both = jnp.concatenate([north, south], axis=1)
        copy(p).wait()
        for m2 in range(2):
            order = order_of(slots_ref, index_ref, ord_dev, 2 * p + m2)
            prod = jnp.dot(table[2 * p + m2], both, preferred_element_type=f32)
            mirror = prod[:, LANES:]
            coefs = prod[:, :LANES] + jnp.where(parity == (order & 1), mirror, -mirror)
            low, high = coefs[:half], coefs[half:]
            if m2 == 0:
                high = pltpu.roll(high, LANES // 2, 1)
            else:
                low = pltpu.roll(low, LANES // 2, 1)
            lane = lax.broadcasted_iota(jnp.int32, low.shape, 1)
            wide[pl.ds(2 * p + m2, half, stride=PITCH), :] = jnp.where(lane < LANES // 2, low, high)

    narrow(wide, out_ref, out_hbm, leave)


def weights_kernel(index_ref, weight_ref, *out_refs):
    ch_count = len(out_refs)
    last = weight_ref.shape[1] - 1
    for k, out_ref in enumerate(out_refs):
        there = lax.rem(index_ref[0] + k, ch_count)
        for w in range(2):
            for l2 in range(2):
                out_ref[w, l2] = weight_ref[w, jnp.minimum(2 * there + l2, last)]


def mix_kernel(index_ref, coef_ref, *refs):
    ch_count = len(refs) - 3
    out_ref, weight, sems = refs[ch_count:]
    copies = []
    for k in range(ch_count):
        source = lax.rem(index_ref[0] + ch_count - k, ch_count)
        copies.append(pltpu.make_async_copy(refs[k], weight.at[source], sems.at[k]))
        copies[-1].start()
    for copy in copies:
        copy.wait()
    bands = coef_ref.shape[0]
    ch_dev = LANES // 4
    channels = ch_count * ch_dev
    contract = (((1,), (1,)), ((), ()))
    step = MIX_BANDS
    count = step * PAD

    @pl.loop(0, bands // step)
    def _(chunk):
        here = pl.ds(chunk * step, step)
        groups = []
        for h in range(ch_count // 4):
            quads = [coef_ref[here, 4 * h + e].reshape(count, LANES).astype(f32) for e in range(4)]
            groups.append(chunk_transpose(quads))
        results = []
        for l2 in range(2):
            left = jnp.concatenate(
                [jnp.concatenate([g[2 * l2 + x] for g in groups], axis=1) for x in range(2)], axis=0
            ).astype(bf16)
            prod = [
                lax.dot_general(
                    left,
                    weight[:, w, l2].reshape(channels, channels),
                    contract,
                    preferred_element_type=f32,
                )
                for w in range(2)
            ]
            results.append(prod[0][:count] - prod[1][count:])
            results.append(prod[1][:count] + prod[0][count:])
        for h in range(ch_count // 4):
            quads = chunk_transpose([r[:, h * LANES : (h + 1) * LANES] for r in results])
            for e in range(4):
                out_ref[here, 4 * h + e] = quads[e].astype(bf16).reshape(step, PAD, LANES)


def widen(mixed_ref, wide):
    for i in range(mixed_ref.shape[0] * PAIRS):
        wide[i * PITCH : i * PITCH + PAD, :] = mixed_ref[i // PAIRS, i % PAIRS].astype(f32)


def side_of(wide, count, m):
    turned = wide[pl.ds(m, count * PAIRS, stride=PITCH), :].astype(bf16).T
    return jnp.concatenate([turned[: LANES // 2], turned[LANES // 2 :]], axis=1)


def synthesis_kernel(ord_dev, lon, index_ref, slots_ref, mixed_ref, table_hbm, out_hbm, table, wide, sems, out_ref, leave):
    copy = fetch_pairs(table_hbm, table, sems)
    widen(mixed_ref, wide)
    count = out_ref.shape[0]
    half = LANES // 2
    parity = degree_parity((half, table.shape[1]), 1, ord_dev)

    def sent(p):
        return pltpu.make_async_copy(out_ref.at[:, p], out_hbm.at[:, p], leave.at[p])

    @pl.loop(0, PAIRS)
    def _(p):
        copy(p).wait()
        north, south = [], []
        for m2 in range(2):
            order = order_of(slots_ref, index_ref, ord_dev, 2 * p + m2)
            weight = jnp.where(order == 0, 1.0 / lon, 2.0 / lon)
            part = side_of(wide, count, 2 * p + m2).astype(f32)
            same = parity == (order & 1)
            split = jnp.concatenate([jnp.where(same, part, 0.0), jnp.where(same, 0.0, part)], axis=0)
            prod = jnp.dot(split.astype(bf16), table[2 * p + m2], preferred_element_type=f32)
            north.append((prod[:half] + prod[half:]) * weight)
            south.append((prod[:half] - prod[half:]) * weight)
        up = jnp.concatenate(north, axis=0).astype(bf16).T
        down = jnp.concatenate(south, axis=0).astype(bf16).T
        for s in range(count // 2):
            out_ref[s, p] = up[s * PAD : (s + 1) * PAD]
            out_ref[count - 1 - s, p] = down[s * PAD : (s + 1) * PAD]
        sent(p).start()

    for p in range(PAIRS):
        sent(p).wait()


def spectrum_kernel(ord_dev, mixed_ref, pick_ref, out_ref, wide):
    count = mixed_ref.shape[0]
    widen(mixed_ref, wide)

    @pl.loop(0, ord_dev)
    def _(m):
        side = side_of(wide, count, m)
        spec = jnp.dot(side, pick_ref[...], preferred_element_type=f32).astype(bf16)
        out_ref[m] = spec.reshape(out_ref.shape[1:])


def backward_kernel(
    lat_dev, lat_count, index_ref, rows_ref, table_hbm, field_hbm, out_ref, wide, left, table_ref, field_ref, sems
):
    copies = [
        pltpu.make_async_copy(table_hbm, table_ref, sems.at[0]),
        pltpu.make_async_copy(field_hbm, field_ref, sems.at[1]),
    ]
    for copy in copies:
        copy.start()
    half = rows_ref.shape[0] * rows_ref.shape[1]
    ch_dev = LANES // 4
    for i in range(half):
        wide[i * PITCH : i * PITCH + PAD, :] = rows_ref[i // PAIRS, i % PAIRS].astype(f32)
    for j in range(lat_dev):
        slot = slot_of(j, lat_dev, index_ref[0], lat_count)
        block = wide[pl.ds(slot, half, stride=PITCH), :].astype(bf16).T
        for q in range(4):
            left[j * ch_dev : (j + 1) * ch_dev, q * half : (q + 1) * half] = block[
                q * ch_dev : (q + 1) * ch_dev
            ]
    lon = out_ref.shape[2]
    for copy in copies:
        copy.wait()
    for b in range(4):
        cut = slice(b * lon // 4, (b + 1) * lon // 4)
        wave = jnp.dot(left[...], table_ref[:, cut], preferred_element_type=f32)
        cubic = wave * wave * wave
        grown = 0.5 * wave * (1.0 + jnp.tanh(math.sqrt(2.0 / math.pi) * (wave + 0.044715 * cubic)))
        field = field_ref[:, :, cut].astype(f32)
        out_ref[:, :, cut] = (field + grown.reshape(field.shape)).astype(bf16)


def params(mib=VMEM_MIB):
    return pltpu.CompilerParams(vmem_limit_bytes=int(mib * 2**20))


def cost(flops, moved):
    return pl.CostEstimate(flops=int(flops), bytes_accessed=int(moved), transcendentals=0)


MIX_BANDS = 32
vmem = pl.BlockSpec(memory_space=pltpu.VMEM)
smem = pl.BlockSpec(memory_space=pltpu.SMEM)
hbm = pl.BlockSpec(memory_space=pltpu.HBM)


def buffer_of(lat_count):
    return jax.ShapeDtypeStruct((lat_count, PAIRS, PAD, LANES), bf16)


def call_forward(lat_count, index, slots, field_in):
    lat_dev, ch_dev, lon = field_in.shape
    half = lat_count * PAIRS
    return pl.pallas_call(
        functools.partial(forward_kernel, lat_dev, lat_count, slots.shape[1] // lat_count),
        out_shape=buffer_of(lat_count),
        in_specs=[smem, vmem, hbm],
        out_specs=hbm,
        scratch_shapes=[
            pltpu.VMEM((lon, 4 * half), bf16),
            pltpu.VMEM(field_in.shape, bf16),
            pltpu.VMEM((lat_dev, 4, ch_dev, half), f32),
            pltpu.VMEM((half * PITCH, LANES), f32),
            pltpu.VMEM((lat_count, PAIRS, PAD, LANES), bf16),
            pltpu.SemaphoreType.DMA,
            pltpu.SemaphoreType.DMA((4,)),
        ],
        compiler_params=params(TABLE_MIB),
        name="forward",
    )(index, slots, field_in)


def call_legendre(lat_count, lat_dev, index, slots):
    lat_total = lat_count * lat_dev
    modes = slots.shape[1]
    ord_dev = modes // lat_count
    full = lat_count * PAD
    near = full // 2
    angle = math.pi * (np.arange(lat_total) + 0.5) / lat_total
    geo = np.zeros((2, lat_count, PAD), np.float32)
    geo[0, :, :lat_dev] = np.cos(angle).reshape(lat_count, lat_dev)
    geo[1, :, :lat_dev] = np.log(np.sin(angle)).reshape(lat_count, lat_dev)
    geo = geo.reshape(2, full)[:, :near]
    k = np.arange(1, modes)
    prod = np.zeros((1, full), np.float32)
    prod[0, 1:modes] = np.cumsum(0.5 * np.log((2.0 * k - 1.0) / (2.0 * k)))
    groups = near // LANES
    parts = 4
    state = pltpu.VMEM((groups, PAD, LANES), f32)
    table = pl.pallas_call(
        functools.partial(legendre_kernel, ord_dev),
        out_shape=jax.ShapeDtypeStruct((PAD, 2, lat_count // 2, PAD, near), bf16),
        in_specs=[smem, vmem, vmem, vmem],
        out_specs=hbm,
        scratch_shapes=[state] * 5
        + [
            pltpu.VMEM((groups, PAD * (2 * PAD + 1), LANES), f32),
            pltpu.VMEM((PAD, 2, lat_count // 2, PAD, near), bf16),
            pltpu.SemaphoreType.DMA((parts,)),
        ],
        compiler_params=params(TABLE_MIB),
        cost_estimate=cost(8e9, 2e7),
        name="legendre",
    )(index, slots, jnp.asarray(geo), jnp.asarray(prod))
    return table.reshape(PAD, full, near)


def call_inverse_table(lat_count, lon, slots):
    half = lat_count * PAIRS
    return pl.pallas_call(
        functools.partial(inverse_table_kernel, slots.shape[1] // lat_count, lat_count),
        out_shape=jax.ShapeDtypeStruct((4 * half, lon), bf16),
        in_specs=[vmem],
        out_specs=hbm,
        scratch_shapes=[
            pltpu.VMEM((4 * half, lon), bf16),
            pltpu.VMEM((2 * half, LANES), f32),
            pltpu.SemaphoreType.DMA,
        ],
        compiler_params=params(TABLE_MIB),
        cost_estimate=cost(2e9, 4e6),
        name="inverse_table",
    )(slots)


def call_analysis(ord_dev, index, orders, rows, table):
    lat_count = rows.shape[0]
    return pl.pallas_call(
        functools.partial(analysis_kernel, ord_dev),
        out_shape=jax.ShapeDtypeStruct(rows.shape, bf16),
        in_specs=[smem, smem, vmem, hbm],
        out_specs=hbm,
        scratch_shapes=[
            pltpu.VMEM(table.shape, bf16),
            pltpu.VMEM((lat_count * PAIRS * PITCH, LANES), f32),
            pltpu.SemaphoreType.DMA((PAIRS,)),
            pltpu.VMEM((lat_count, PAIRS, PAD, LANES), bf16),
            pltpu.SemaphoreType.DMA((4,)),
        ],
        compiler_params=params(),
        name="analysis",
    )(index, orders, rows, table)


def weight_pieces(index, weights, ch_count):
    piece = jax.ShapeDtypeStruct((2, 2) + weights.shape[2:], bf16)
    return pl.pallas_call(
        weights_kernel,
        out_shape=(piece,) * ch_count,
        in_specs=[smem, vmem],
        out_specs=(vmem,) * ch_count,
        compiler_params=params(),
        name="weights",
    )(index, weights)


def move_along(pieces, steps):
    count = len(pieces)
    pieces = list(pieces)
    for k in steps:
        pieces[k] = lax.ppermute(pieces[k], "ch", [(e, (e + k) % count) for e in range(count)])
    return tuple(pieces)


def call_mix(index, coeffs, weights):
    ch_count = len(weights)
    return pl.pallas_call(
        mix_kernel,
        out_shape=jax.ShapeDtypeStruct(coeffs.shape, bf16),
        in_specs=[smem, vmem] + [hbm] * ch_count,
        out_specs=vmem,
        scratch_shapes=[
            pltpu.VMEM((ch_count,) + weights[0].shape, bf16),
            pltpu.SemaphoreType.DMA((ch_count,)),
        ],
        compiler_params=params(),
        name="mix",
    )(index, coeffs, *weights)


def call_synthesis(ord_dev, lon, index, orders, mixed, table):
    lat_count = mixed.shape[0]
    return pl.pallas_call(
        functools.partial(synthesis_kernel, ord_dev, lon),
        out_shape=buffer_of(mixed.shape[0]),
        in_specs=[smem, smem, vmem, hbm],
        out_specs=hbm,
        scratch_shapes=[
            pltpu.VMEM(table.shape, bf16),
            pltpu.VMEM((lat_count * PAIRS * PITCH, LANES), f32),
            pltpu.SemaphoreType.DMA((PAIRS,)),
            pltpu.VMEM((lat_count, PAIRS, PAD, LANES), bf16),
            pltpu.SemaphoreType.DMA((PAIRS,)),
        ],
        compiler_params=params(),
        name="synthesis",
    )(index, orders, mixed, table)


def call_spectrum(ord_dev, mixed):
    lat_count = mixed.shape[0]
    modes = ord_dev * lat_count
    pick = np.zeros((lat_count, PAD, modes), np.float32)
    pick[:, :ord_dev] = np.eye(modes, dtype=np.float32).reshape(lat_count, ord_dev, modes)
    pick = pick.reshape(lat_count * PAIRS, 2, modes).transpose(1, 0, 2)
    pick = jnp.asarray(pick.reshape(lat_count * PAD, modes), bf16)
    return pl.pallas_call(
        functools.partial(spectrum_kernel, ord_dev),
        out_shape=jax.ShapeDtypeStruct((ord_dev, 2, LANES // 4, modes), bf16),
        in_specs=[vmem, vmem],
        out_specs=vmem,
        scratch_shapes=[pltpu.VMEM((lat_count * PAIRS * PITCH, LANES), f32)],
        compiler_params=params(),
        cost_estimate=cost(3e9, 4e6),
        name="spectrum",
    )(mixed, pick)


def call_backward(index, rows, table, field_in):
    lat_dev, ch_dev, _ = field_in.shape
    lat_count = rows.shape[0]
    half = lat_count * PAIRS
    return pl.pallas_call(
        functools.partial(backward_kernel, lat_dev, lat_count),
        out_shape=jax.ShapeDtypeStruct(field_in.shape, bf16),
        in_specs=[smem, vmem, hbm, hbm],
        out_specs=vmem,
        scratch_shapes=[
            pltpu.VMEM((half * PITCH, LANES), f32),
            pltpu.VMEM((lat_dev * ch_dev, 4 * half), bf16),
            pltpu.VMEM(table.shape, bf16),
            pltpu.VMEM(field_in.shape, bf16),
            pltpu.SemaphoreType.DMA((2,)),
        ],
        compiler_params=params(),
        name="backward",
    )(index, rows, table, field_in)


def on_device(field_in, mix_weight, order_slots):
    lat_dev, _, lon = field_in.shape
    lat_count = lax.axis_size("lat")
    modes = order_slots.shape[0]
    ord_dev = modes // lat_count
    index = lax.axis_index("lat")
    index = index.reshape(1)
    slots = order_slots.reshape(1, modes)

    rows = call_forward(lat_count, index, slots, field_in)
    rows = lax.all_to_all(rows, "lat", 0, 0, tiled=True)
    legendre = call_legendre(lat_count, lat_dev, index, slots)
    weights = jnp.transpose(mix_weight, (0, 3, 2, 1))
    weights, legendre = lax.optimization_barrier((weights, legendre))
    ch_index = lax.axis_index("ch").reshape(1)
    ch_count = lax.axis_size("ch")
    far = sorted(range(1, ch_count), key=lambda k: -min(k, ch_count - k))[: ch_count // 2 - 1]
    near = [k for k in range(1, ch_count) if k not in far]
    weights = move_along(weight_pieces(ch_index, weights, ch_count), far)
    coeffs = call_analysis(ord_dev, index, order_slots, rows, legendre)
    coeffs, weights = lax.optimization_barrier((coeffs, weights))
    weights = move_along(weights, near)
    coeffs = lax.all_to_all(coeffs.reshape(-1, PAD, LANES), ("lat", "ch"), 0, 0, tiled=True)
    mixed = call_mix(ch_index, coeffs.reshape(rows.shape), weights)
    mixed = lax.all_to_all(mixed.reshape(-1, PAD, LANES), ("lat", "ch"), 0, 0, tiled=True).reshape(rows.shape)
    synth = call_synthesis(ord_dev, lon, index, order_slots, mixed, legendre)
    synth = lax.all_to_all(synth, "lat", 0, 0, tiled=True)
    spectrum = call_spectrum(ord_dev, mixed)
    inverse_table = call_inverse_table(lat_count, lon, slots)
    field_out = call_backward(index, synth, inverse_table, field_in)
    return (field_out, spectrum)


def solution(mesh):
    placed = (P("lat", "ch", None), P(None, None, "ch", "lat"), P())
    return jax.shard_map(
        on_device,
        mesh=mesh,
        in_specs=placed,
        out_specs=(P("lat", "ch", None), P("lat", None, "ch", None)),
        check_vma=False,
    )
```
